256 devices in a mesh: sec: 16 (over y, z_lo, core), row: 16 (over z_hi, x).
Axes of the slice: x: 4, y: 4, z: 8 (z_hi: 4, z_lo: 2; z = z_hi * 2 + z_lo), core: 2. Of those that a mesh axis runs over, the one named last changes fastest.
Arguments:
- env_in: bfloat16 [32, 16, 2, 256, 512], P('row', 'sec'), may hold values from -6 to 6
- ket_mps: bfloat16 [4, 16, 2, 512, 512], P(None, 'sec'), may hold values from -0.25 to 0.25
- bra_mps: bfloat16 [4, 16, 2, 256, 256], P(None, 'sec'), may hold values from -0.375 to 0.375
- ket_sizes: int32 [16, 2], replicated, may hold values from 64 to 512, as said below
- bra_sizes: int32 [16, 2], replicated, may hold values from 64 to 256, as said below
- entries: int32 [32, 8, 3], P('row'), may hold values from 0 to 31, as said below
- coeffs: float32 [32, 8], P('row'), may hold values from -3 to 3
Outputs:
- env_out: bfloat16 [32, 16, 2, 256, 512], P('row', 'sec')
The draws below stay inside these ranges and needn't reach their ends.
Inputs may be any that keep to these rules, and one draw needn't show every extreme that they name: `ket_sizes`: each ket sector size is at least 64 and at most 512; one sector has exactly 512. `bra_sizes`: each bra sector size is at least 64 and at most 256; one sector has exactly 256. `entries`: every entry (wo, sp, s) of input channel wi conserves charge: c(wo) = c(wi) + n(sp) - n(s); sp and s lie in 0 to 3.
All inputs are finite; a program needn't handle non-finite values.
Results may differ from the reference program's by a relative error of at most 0.014.
Values may be sent and summed in bfloat16 or wider, within the bound.
No kernel may reach another device: no remote copies, remote signals or barrier semaphores. Data moves between devices by JAX's collectives and lax.ppermute only.
A program may use at most 128 MiB of HBM per device.

```python
import jax
import jax.numpy as jnp
from jax import lax

MW = 32
KB = 512
BB = 256
PHYS = 4
EPW = 8
QB = 2
QA = 16
CH = 2
N_ROW = 16


def draw_sizes(key, low, high):
    values = jax.random.randint(key, (QA, QB), low, high + 1)
    where_top = jax.random.randint(jax.random.fold_in(key, 7), (), 0, QA * QB)
    flat = values.reshape(-1)
    flat = jnp.where(jnp.arange(QA * QB) == where_top, high, flat)
    return flat.reshape(QA, QB).astype(jnp.int32)


def draw_ket_sizes(key, part):
    return draw_sizes(jax.random.fold_in(key, 11), KB // 8, KB)


def draw_bra_sizes(key, part):
    return draw_sizes(jax.random.fold_in(key, 13), BB // 4, BB)


def draw_entries(key, part):
    first, second, third = jax.random.split(jax.random.fold_in(key, 17), 3)
    phys_bra = jax.random.randint(first, (MW, EPW), 0, 4)
    phys_try = jax.random.randint(second, (MW, EPW), 0, 4)
    channel = jnp.arange(MW)[:, None]
    klass = channel % 9
    in_a = klass % 3 - 1
    in_b = klass // 3 - 1
    need_a = in_a + phys_bra % 2 - phys_try % 2
    need_b = in_b + phys_bra // 2 - phys_try // 2
    usable = (jnp.abs(need_a) <= 1) & (jnp.abs(need_b) <= 1)
    phys_ket = jnp.where(usable, phys_try, phys_bra)
    need_a = jnp.where(usable, need_a, in_a)
    need_b = jnp.where(usable, need_b, in_b)
    target = need_a + 1 + 3 * (need_b + 1)
    members = (MW - target + 8) // 9
    slots = jnp.arange(EPW)[None, :]
    offset = jax.random.randint(third, (MW, 1), 0, 1 << 20)
    pick = (offset + slots) % members
    out_w = target + 9 * pick
    return jnp.stack([out_w, phys_bra, phys_ket], axis=-1).astype(jnp.int32)


def levels(stream_key, dims, shards, least, high):
    level, own = 1.0, jax.random.fold_in(stream_key, 6)
    for axis_at, parts in shards:
        draws = jnp.exp(jax.random.uniform(jax.random.fold_in(own, axis_at), (parts,), jnp.float32, least / len(shards), high / len(shards)))
        level = level * jnp.repeat(draws, dims[axis_at] // parts).reshape([-1 if axis == axis_at else 1 for axis in range(len(dims))])
    return level


def bell_draw(rng, dims, width, limit, cuts=(), held_as=jnp.bfloat16):
    gain = levels(rng, dims, cuts, -0.22, 0.18) if cuts else 1.0
    values = jax.random.normal(rng, dims, jnp.float32) * width * gain
    return jnp.minimum(jnp.maximum(values, -limit), limit).astype(held_as)


def setup_inputs(seed: int = 0) -> dict:
    keys = jax.random.split(jax.random.key(seed), 8)
    return {
        "env_in": bell_draw(keys[0], (MW, QA, QB, BB, KB), 1.0, 6.0, ((0, 16), (1, 16))),
        "ket_mps": bell_draw(keys[1], (PHYS, QA, QB, KB, KB), KB ** -0.5, 0.25, ((1, 16),)),
        "bra_mps": bell_draw(keys[2], (PHYS, QA, QB, BB, BB), BB ** -0.5, 0.375, ((1, 16),)),
        "ket_sizes": draw_ket_sizes(jax.random.fold_in(keys[7], 71), 0),
        "bra_sizes": draw_bra_sizes(jax.random.fold_in(keys[7], 71), 0),
        "entries": draw_entries(jax.random.fold_in(keys[7], 71), 0),
        "coeffs": bell_draw(keys[6], (MW, EPW), 1.0, 3.0, ((0, 16),), jnp.float32),
    }


def channel_charge(channel):
    klass = channel % 9
    return klass % 3 - 1, klass // 3 - 1


def keep_block(block, rows, cols):
    keep_rows = lax.broadcasted_iota(jnp.int32, block.shape, block.ndim - 2) < rows[..., None, None]
    keep_cols = lax.broadcasted_iota(jnp.int32, block.shape, block.ndim - 1) < cols[..., None, None]
    return jnp.where(keep_rows & keep_cols, block, jnp.zeros_like(block))


def reference(env_in, ket_mps, bra_mps, ket_sizes, bra_sizes, entries, coeffs):
    ket_ext = jnp.pad(ket_sizes, 2)
    bra_ext = jnp.pad(bra_sizes, 2)
    env_pad = jnp.pad(env_in, ((0, 0), (1, 0), (1, 0), (0, 0), (0, 0)))
    ket_pad = jnp.pad(ket_mps, ((0, 0), (1, 0), (1, 0), (0, 0), (0, 0)))
    bra_pad = jnp.pad(bra_mps, ((0, 0), (1, 1), (1, 1), (0, 0), (0, 0)))
    zero = jnp.zeros((), jnp.int32)

    def sizes_at(ext, shift_a, shift_b):
        return lax.dynamic_slice(ext, ((shift_a + 2).astype(jnp.int32), (shift_b + 2).astype(jnp.int32)), (QA, QB))

    def entry_term(item):
        chan = item // EPW
        slot = item % EPW
        out_w = entries[chan, slot, 0]
        phys_bra = entries[chan, slot, 1]
        phys_ket = entries[chan, slot, 2]
        value = coeffs[chan, slot]
        up_a = phys_ket % 2
        up_b = phys_ket // 2
        in_a, in_b = channel_charge(chan)
        out_a, out_b = channel_charge(out_w)
        env_blk = lax.dynamic_slice(env_pad, (chan.astype(jnp.int32), 1 - up_a, 1 - up_b, zero, zero), (1, QA, QB, BB, KB))[0]
        ket_blk = lax.dynamic_slice(ket_pad, (phys_ket, 1 - up_a, 1 - up_b, zero, zero), (1, QA, QB, KB, KB))[0]
        bra_blk = lax.dynamic_slice(bra_pad, (phys_bra, 1 + out_a, 1 + out_b, zero, zero), (1, QA, QB, BB, BB))[0]
        ket_src = sizes_at(ket_ext, -up_a, -up_b)
        env_blk = keep_block(env_blk, sizes_at(bra_ext, in_a - up_a, in_b - up_b), ket_src)
        ket_blk = keep_block(ket_blk, ket_src, sizes_at(ket_ext, zero, zero))
        bra_blk = keep_block(bra_blk, sizes_at(bra_ext, out_a - phys_bra % 2, out_b - phys_bra // 2), sizes_at(bra_ext, out_a, out_b))
        half = jnp.einsum("abik,abkl->abil", env_blk.astype(jnp.float32), ket_blk.astype(jnp.float32)).astype(jnp.bfloat16)
        term = jnp.einsum("abij,abil->abjl", bra_blk.astype(jnp.float32), half.astype(jnp.float32))
        return out_w, value * term

    def group(index, total):
        def step(inner, partial_value):
            item = (index * CH * EPW + inner).astype(jnp.int32)
            out_w, term = entry_term(item)
            return partial_value.at[out_w].add(term)

        partial_value = lax.fori_loop(0, CH * EPW, step, jnp.zeros((MW, QA, QB, BB, KB), jnp.float32))
        rounded = lax.optimization_barrier(partial_value.astype(jnp.bfloat16))
        return total + rounded.astype(jnp.float32)

    total = lax.fori_loop(0, N_ROW, group, jnp.zeros((MW, QA, QB, BB, KB), jnp.float32))
    return total.astype(jnp.bfloat16)
```

```python
import functools

import jax
import jax.numpy as jnp
import numpy as np
from jax import lax
from jax.experimental import pallas as pl
from jax.experimental.pallas import tpu as pltpu
from jax.sharding import PartitionSpec as P

MW, EPW, CH = 32, 8, 2
NZ, NX = 4, 4
SECS, ROWS = 16, 16
BB, KB = 256, 512
BF, F32 = jnp.bfloat16, jnp.float32
STEPS = (0, -1, 1, 2)
VMEM_BYTES = 56 * 1024 * 1024


def charge(channel):
    klass = channel % 9
    return klass % 3 - 1, klass // 3 - 1


def live_tables():
    order, inverse, count = [], [], []
    for r in range(ROWS):
        cells = [(b, j) for b in range(2) for j in range(CH)]
        live = [(b, j) for b, j in cells if 0 <= b + charge(CH * r + j)[1] < 2]
        rest = [cell for cell in cells if cell not in live]
        line = [j * 2 + b for b, j in live + rest]
        order.append(line)
        inverse.append([line.index(c) if line.index(c) < len(live) else -1 for c in range(4)])
        count.append(len(live))
    return np.array(order, np.int32), np.array(inverse, np.int32), count


ORDER, INVERSE, COUNT = live_tables()


def row_z(r, d):
    return (r // NX + d) % NZ * NX + r % NX


def row_x(r, d):
    return r // NX * NX + (r % NX + d) % NX


def along_rows(move, owner, i):
    return [(r, move(r)) for r in range(ROWS) if COUNT[owner(r)] > i]


def pack_kernel(order, rows, cols, env, *outs):
    row_at = lax.broadcasted_iota(jnp.int32, (BB, KB), 0)
    col_at = lax.broadcasted_iota(jnp.int32, (BB, KB), 1)
    for i in range(4):
        keep = (row_at < rows[i]) & (col_at < cols[i])
        outs[i][...] = jnp.where(keep, env[order[i]], jnp.zeros((BB, KB), BF))


def terms_kernel(ints, values, inv_e, inv_o, place, *refs):
    envs, (ket, bm1, b0, bp1, bp2) = refs[:16], refs[16:21]
    outs = refs[21:37]
    env_all, bra_all, total = refs[37:]
    for n in range(16):
        env_all[n] = envs[n][...]
    for n in range(3):
        bra_all[n] = bm1[n]
        bra_all[18 + 3 + n] = bp2[n]
    for n in range(6):
        bra_all[6 + n] = b0[n]
        bra_all[12 + n] = bp1[n]

    @pl.loop(0, 32)
    def _(n):
        total[n] = jnp.zeros((BB, KB), F32)

    my_z, my_x = place[0], place[1]

    @pl.loop(0, 4 * CH * EPW)
    def _(item):
        out_w = ints[3 * item]

        @pl.when(out_w // (CH * NX) == my_z)
        def _():
            sp = ints[3 * item + 1]
            s = ints[3 * item + 2]
            value = values[item]
            k, j = item // (CH * EPW), item // EPW % CH
            ahead = (out_w % (CH * NX) // CH - my_x + NX) % NX
            slot = jnp.where(ahead == 1, 2, jnp.where(ahead == 3, 1, jnp.where(ahead == 2, 3, 0)))
            out_a, out_b = charge(out_w)
            s_a, s_b = s % 2, s // 2
            sp_a, sp_b = sp % 2, sp // 2
            for q_b in range(2):
                p_b = q_b + s_b
                e_at = inv_e[4 * k + 2 * j + q_b]
                o_at = inv_o[4 * slot + 2 * (out_w % CH) + jnp.minimum(p_b, 1)]

                @pl.when((p_b < 2) & (e_at >= 0) & (o_at >= 0))
                def _(q_b=q_b, p_b=p_b, e_at=e_at, o_at=o_at):
                    half = jnp.dot(env_all[4 * k + e_at], ket[s, q_b], preferred_element_type=F32).astype(BF)
                    b_at = 6 * (s_a + out_a + 1) + 3 * sp_a + p_b + out_b + sp_b
                    term = jnp.dot(bra_all[b_at], half, preferred_element_type=F32)
                    at = 8 * slot + 2 * o_at + s_a
                    total[at] = total[at] + value * term

    for d in range(4):
        for i in range(4):
            for up in range(2):
                outs[4 * d + i][up] = total[8 * d + 2 * i + up].astype(BF)


def body(env_in, ket_mps, bra_mps, ket_sizes, bra_sizes, entries, coeffs):
    my_a = lax.axis_index("sec")
    r = lax.axis_index("row")
    my_z, my_x = r // NX, r % NX
    ket_ext = jnp.pad(ket_sizes, 2)
    bra_ext = jnp.pad(bra_sizes, 2)
    order = lax.dynamic_index_in_dim(jnp.asarray(ORDER), r, keepdims=False)
    inverse = lax.dynamic_index_in_dim(jnp.asarray(INVERSE), r, keepdims=False)
    second = order % 2
    chan_a, chan_b = charge(CH * r + order // 2)
    block_rows = bra_ext[my_a + chan_a + 2, second + chan_b + 2]
    block_cols = ket_ext[my_a + 2, second + 2]

    smem = pl.BlockSpec(memory_space=pltpu.SMEM)
    vmem = pl.BlockSpec(memory_space=pltpu.VMEM)
    block = jax.ShapeDtypeStruct((BB, KB), BF)
    own = pl.pallas_call(
        pack_kernel,
        in_specs=[smem] * 3 + [vmem],
        out_specs=[vmem] * 4,
        out_shape=[block] * 4,
        compiler_params=pltpu.CompilerParams(vmem_limit_bytes=VMEM_BYTES),
    )(order, block_rows, block_cols, env_in.reshape(4, BB, KB))

    items = jnp.concatenate([entries.astype(F32), coeffs[..., None]], axis=-1)
    item_parts = [items] + [
        lax.ppermute(items, "row", [(n, row_z(n, -d)) for n in range(ROWS)]) for d in STEPS[1:]
    ]
    items = jnp.stack(item_parts).reshape(4 * CH * EPW, 4)
    ints = items[:, :3].astype(jnp.int32).reshape(-1)
    values = items[:, 3]

    flipped = jnp.swapaxes(bra_mps[:, 0], -1, -2)
    bra = [
        jnp.stack([flipped[n, 0], flipped[n, 1], flipped[n + 2, 1]]) for n in range(2)
    ]
    up = lambda n: [(i, i + n) for i in range(SECS - n)]
    down = lambda n: [(i + n, i) for i in range(SECS - n)]
    bra_own = jnp.concatenate(bra)

    behind, ahead, across = [], [], []
    for i in range(4):
        behind.append(lax.ppermute(own[i], "row", along_rows(lambda n: row_z(n, 1), lambda n: n, i)))
        ahead.append(lax.ppermute(own[i], "row", along_rows(lambda n: row_z(n, -1), lambda n: n, i)))
    bra_m1 = lax.ppermute(bra[0], "sec", up(1))
    bra_p1 = lax.ppermute(bra_own, "sec", down(1))
    bra_p2 = lax.ppermute(bra[1], "sec", down(2))
    for i in range(4):
        if i % 2 == 0:
            across.append(lax.ppermute(behind[i], "row", along_rows(lambda n: row_z(n, 1), lambda n: row_z(n, -1), i)))
        else:
            across.append(lax.ppermute(ahead[i], "row", along_rows(lambda n: row_z(n, -1), lambda n: row_z(n, 1), i)))

    inv_e = jnp.asarray(INVERSE)[jnp.stack([(my_z + d) % NZ * NX + my_x for d in STEPS])].reshape(-1)
    inv_o = jnp.asarray(INVERSE)[jnp.stack([my_z * NX + (my_x + d) % NX for d in STEPS])].reshape(-1)
    pair = jax.ShapeDtypeStruct((2, BB, KB), BF)
    sums = pl.pallas_call(
        terms_kernel,
        in_specs=[smem] * 5 + [vmem] * 21,
        out_specs=[vmem] * 16,
        out_shape=[pair] * 16,
        scratch_shapes=[
            pltpu.VMEM((16, BB, KB), BF),
            pltpu.VMEM((24, BB, BB), BF),
            pltpu.VMEM((32, BB, KB), F32),
        ],
        compiler_params=pltpu.CompilerParams(vmem_limit_bytes=VMEM_BYTES),
    )(ints, values, inv_e, inv_o, jnp.stack([my_z, my_x]), *own, *behind, *ahead, *across,
      ket_mps[:, 0], bra_m1, bra_own, bra_p1, bra_p2)
    mine, to_left, to_right, to_far = sums[:4], sums[4:8], sums[8:12], sums[12:]

    def added(*parts):
        return functools.reduce(jnp.add, [part.astype(F32) for part in parts])

    to_left, to_right = list(to_left), list(to_right)
    for i in range(4):
        if i % 2 == 0:
            got = lax.ppermute(to_far[i], "row", along_rows(lambda n: row_x(n, 1), lambda n: row_x(n, 2), i))
            to_right[i] = added(to_right[i], got).astype(BF)
        else:
            got = lax.ppermute(to_far[i], "row", along_rows(lambda n: row_x(n, -1), lambda n: row_x(n, 2), i))
            to_left[i] = added(to_left[i], got).astype(BF)
    here, above = [], []
    for i in range(4):
        from_left = lax.ppermute(to_right[i], "row", along_rows(lambda n: row_x(n, 1), lambda n: row_x(n, 1), i))
        from_right = lax.ppermute(to_left[i], "row", along_rows(lambda n: row_x(n, -1), lambda n: row_x(n, -1), i))
        here.append(added(mine[i][0], from_left[0], from_right[0]))
        raised = added(mine[i][1], from_left[1], from_right[1]).astype(BF)
        pairs = [(a * ROWS + n, (a + 1) * ROWS + n) for a in range(SECS - 1) for n in range(ROWS) if COUNT[n] > i]
        above.append(lax.ppermute(raised, ("sec", "row"), pairs))

    row_at = lax.broadcasted_iota(jnp.int32, (BB, KB), 0)
    col_at = lax.broadcasted_iota(jnp.int32, (BB, KB), 1)
    whole = jnp.stack([
        jnp.where((row_at < block_rows[i]) & (col_at < block_cols[i]), added(here[i], above[i]), 0.0).astype(BF)
        for i in range(4)
    ])
    out = [
        jnp.where(inverse[c] >= 0, lax.dynamic_index_in_dim(whole, jnp.maximum(inverse[c], 0), keepdims=False), jnp.zeros((BB, KB), BF))
        for c in range(4)
    ]
    return jnp.stack(out).reshape(CH, 1, 2, BB, KB)


def solution(mesh):
    placed = (
        P("row", "sec", None, None, None),
        P(None, "sec", None, None, None),
        P(None, "sec", None, None, None),
        P(),
        P(),
        P("row", None, None),
        P("row", None),
    )
    return jax.shard_map(
        body,
        mesh=mesh,
        in_specs=placed,
        out_specs=P("row", "sec", None, None, None),
        check_vma=False,
    )
```

```python
import functools

import jax
import jax.numpy as jnp
from jax import lax
from jax.experimental import pallas as pl
from jax.experimental.pallas import tpu as pltpu
from jax.sharding import PartitionSpec as P

EPW, CH = 8, 2
NZ, NX = 4, 4
SECS, ROWS = 16, 16
BB, KB = 256, 512
QUARTER = BB // NX
BF, F32 = jnp.bfloat16, jnp.float32
STEPS = (0, -1, 1, 2)
VMEM_BYTES = 56 * 1024 * 1024
CELLS = [(b, j) for b in range(2) for j in range(CH)]


def charge(channel):
    klass = channel % 9
    return klass % 3 - 1, klass // 3 - 1


def live_at(r, b, j):
    to_b = b + charge(CH * r + j)[1]
    return jnp.where((to_b >= 0) & (to_b < 2), 1, 0)


COUNT = [sum(0 <= b + charge(CH * r + j)[1] < 2 for b, j in CELLS) for r in range(ROWS)]


def row_z(r, d):
    return (r // NX + d) % NZ * NX + r % NX


def row_x(r, d):
    return r // NX * NX + (r % NX + d) % NX


def moved(value, move, owner, i):
    return lax.ppermute(value, "row", [(r, move(r)) for r in range(ROWS) if COUNT[owner(r)] > i])


def after(value, *others):
    return lax.optimization_barrier((value, *others))[0]


def packed_cells(r, a, ket_sizes, bra_sizes):
    places = [(jnp.int32(0), jnp.int32(0), jnp.int32(0)) for _ in range(4)]
    count = jnp.int32(0)
    for b, j in CELLS:
        out_a, out_b = charge(CH * r + j)
        live = live_at(r, b, j)
        at_a, at_b = a + out_a, jnp.clip(b + out_b, 0, 1)
        rows = jnp.where((at_a >= 0) & (at_a < SECS), bra_sizes[2 * jnp.clip(at_a, 0, SECS - 1) + at_b], 0)
        cols = ket_sizes[2 * a + b]
        for i in range(4):
            hit = (live == 1) & (count == i)
            places[i] = tuple(jnp.where(hit, new, old) for new, old in zip((2 * j + b, rows, cols), places[i]))
        count = count + live
    return places


def keep(rows, cols):
    row_at = lax.broadcasted_iota(jnp.int32, (BB, KB), 0)
    col_at = lax.broadcasted_iota(jnp.int32, (BB, KB), 1)
    return (row_at < rows) & (col_at < cols)


def pack_kernel(place, ket_sizes, bra_sizes, env, *outs):
    for i, (cell, rows, cols) in enumerate(packed_cells(place[0], place[1], ket_sizes, bra_sizes)):
        value = jnp.where(keep(rows, cols), env[cell], jnp.zeros((BB, KB), BF))
        if i < 2:
            outs[0][i] = value
        else:
            outs[i - 1][...] = value


def unpack_kernel(place, ket_sizes, bra_sizes, *refs):
    here, above, out = refs[:4], refs[4:8], refs[8]
    out[...] = jnp.zeros_like(out)
    for i, (cell, rows, cols) in enumerate(packed_cells(place[0], place[1], ket_sizes, bra_sizes)):
        value = here[i][...] + above[i][...].astype(F32)

        @pl.when(rows > 0)
        def _(value=value, cell=cell, rows=rows, cols=cols):
            out[cell] = jnp.where(keep(rows, cols), value, 0.0).astype(BF)


def terms_kernel(place, ints, values, own01, own2, own3, behind01, behind2, behind3, ahead01, ahead2, ahead3,
                 across0, across1, across2, across3, ket, bra_own, bra_rim, *refs):
    outs = refs[:16]
    env_all, bra_all, total = refs[16:]
    for k, (first, third, fourth) in enumerate(((own01, own2, own3), (behind01, behind2, behind3), (ahead01, ahead2, ahead3))):
        env_all[4 * k] = first[0]
        env_all[4 * k + 1] = first[1]
        env_all[4 * k + 2] = third[...]
        env_all[4 * k + 3] = fourth[...]
    for n, ref in enumerate((across0, across1, across2, across3)):
        env_all[12 + n] = ref[...]
    for n in range(6):
        bra_all[6 + n] = bra_own[n]
    for x in range(NX):
        lines = pl.ds(QUARTER * x, QUARTER)
        for n in range(3):
            bra_all[n, lines] = bra_rim[x, n]
            bra_all[21 + n, lines] = bra_rim[x, 9 + n]
        for n in range(6):
            bra_all[12 + n, lines] = bra_rim[x, 3 + n]

    @pl.loop(0, 32)
    def _(n):
        total[n] = jnp.zeros((BB, KB), F32)

    r = place[0]
    my_z, my_x = r // NX, r % NX

    @pl.loop(0, 4 * CH * EPW)
    def _(item):
        out_w = ints[4 * item]

        @pl.when(out_w // (CH * NX) == my_z)
        def _():
            sp = ints[4 * item + 1]
            s = ints[4 * item + 2]
            value = values[4 * item + 3]
            k, j = item // (CH * EPW), item // EPW % CH
            from_z = (my_z + jnp.where(k == 1, 3, jnp.where(k == 2, 1, jnp.where(k == 3, 2, 0)))) % NZ
            from_r = from_z * NX + my_x
            out_r, out_j = out_w // CH, out_w % CH
            forward = (out_r % NX - my_x + NX) % NX
            slot = jnp.where(forward == 1, 2, jnp.where(forward == 3, 1, jnp.where(forward == 2, 3, 0)))
            out_a, out_b = charge(out_w)
            s_a, s_b = s % 2, s // 2
            sp_a, sp_b = sp % 2, sp // 2

            def position(row, b, jj):
                low = live_at(row, 0, 0)
                inside = low + live_at(row, 0, 1) + jj * live_at(row, 1, 0)
                return jnp.where(b == 0, jj * low, inside)

            for q_b in range(2):
                p_b = q_b + s_b
                live = (p_b < 2) & (live_at(from_r, q_b, j) == 1) & (live_at(out_r, p_b, out_j) == 1)

                @pl.when(live)
                def _(q_b=q_b, p_b=p_b):
                    e_at = 4 * k + position(from_r, q_b, j)
                    half = jnp.dot(env_all[e_at], ket[s, q_b], preferred_element_type=F32).astype(BF)
                    b_at = 6 * (s_a + out_a + 1) + 3 * sp_a + p_b + out_b + sp_b
                    term = jnp.dot(bra_all[b_at], half, preferred_element_type=F32)
                    at = 8 * slot + 2 * position(out_r, p_b, out_j) + s_a
                    total[at] = total[at] + value * term

    for d in range(4):
        for i in range(4):
            for up in range(2):
                outs[4 * d + i][up] = total[8 * d + 2 * i + up].astype(BF)


def body(env_in, ket_mps, bra_mps, ket_sizes, bra_sizes, entries, coeffs):
    my_a = lax.axis_index("sec")
    r = lax.axis_index("row")
    my_x = r % NX
    place = jnp.stack([r, my_a])
    ket_flat, bra_flat = ket_sizes.reshape(-1), bra_sizes.reshape(-1)

    smem = pl.BlockSpec(memory_space=pltpu.SMEM)
    vmem = pl.BlockSpec(memory_space=pltpu.VMEM)
    block = jax.ShapeDtypeStruct((BB, KB), BF)
    pair = jax.ShapeDtypeStruct((2, BB, KB), BF)
    params = pltpu.CompilerParams(vmem_limit_bytes=VMEM_BYTES)
    own01, own2, own3 = pl.pallas_call(
        pack_kernel,
        in_specs=[smem] * 3 + [vmem],
        out_specs=[vmem] * 3,
        out_shape=[pair, block, block],
        compiler_params=params,
    )(place, ket_flat, bra_flat, env_in.reshape(4, BB, KB))

    same = lambda n: n
    z_up, z_down = (lambda n: row_z(n, 1)), (lambda n: row_z(n, -1))
    x_up, x_down, x_far = (lambda n: row_x(n, 1)), (lambda n: row_x(n, -1)), (lambda n: row_x(n, 2))

    behind01 = moved(own01, z_up, same, 0)
    ahead01 = moved(own01, z_down, same, 0)

    flipped = jnp.swapaxes(bra_mps[:, 0], -1, -2)
    six = lambda f: jnp.stack([f[0, 0], f[0, 1], f[2, 1], f[1, 0], f[1, 1], f[3, 1]])
    bra_own = six(flipped)
    strip = six(lax.dynamic_slice_in_dim(flipped, QUARTER * my_x, QUARTER, axis=2))
    up = lambda n: [(i, i + n) for i in range(SECS - n)]
    down = lambda n: [(i + n, i) for i in range(SECS - n)]
    rim = jnp.concatenate([
        lax.ppermute(strip[:3], "sec", up(1)),
        lax.ppermute(strip, "sec", down(1)),
        lax.ppermute(strip[3:], "sec", down(2)),
    ])
    bra_rim = lax.all_gather(rim, "row", axis_index_groups=[[NX * z + x for x in range(NX)] for z in range(NZ)])

    behind2 = moved(own2, z_up, same, 2)
    ahead3 = moved(own3, z_down, same, 3)
    ahead2 = moved(after(own2, ahead01), z_down, same, 2)
    behind3 = moved(after(own3, behind01), z_up, same, 3)
    across0 = moved(behind01[0], z_up, z_down, 0)
    across1 = moved(ahead01[1], z_down, z_up, 1)
    across2 = moved(behind2, z_up, z_down, 2)
    across3 = moved(ahead3, z_down, z_up, 3)

    items = jnp.concatenate([entries.reshape(-1, 3).astype(F32), coeffs.reshape(-1, 1)], axis=-1).reshape(-1)
    items = after(items, behind01, ahead01)
    values = jnp.concatenate(
        [items] + [lax.ppermute(items, "row", [(n, row_z(n, -d)) for n in range(ROWS)]) for d in STEPS[1:]]
    )
    ints = values.astype(jnp.int32)

    sums = pl.pallas_call(
        terms_kernel,
        in_specs=[smem] * 3 + [vmem] * 16,
        out_specs=[vmem] * 16,
        out_shape=[pair] * 16,
        scratch_shapes=[
            pltpu.VMEM((16, BB, KB), BF),
            pltpu.VMEM((24, BB, BB), BF),
            pltpu.VMEM((32, BB, KB), F32),
        ],
        compiler_params=params,
    )(place, ints, values, own01, own2, own3, behind01, behind2, behind3, ahead01, ahead2, ahead3,
      across0, across1, across2, across3, ket_mps[:, 0], bra_own, bra_rim)
    mine, left, right, far = sums[:4], sums[4:8], sums[8:12], sums[12:]

    def added(*parts):
        return functools.reduce(jnp.add, [part.astype(F32) for part in parts])

    far_up = {0: moved(far[0], x_up, x_far, 0)}
    far_down = {1: moved(far[1], x_down, x_far, 1)}
    from_left, from_right = {}, {}
    from_left[1] = moved(right[1], x_up, x_up, 1)
    from_right[0] = moved(left[0], x_down, x_down, 0)
    far_up[2] = moved(after(far[2], far_up[0]), x_up, x_far, 2)
    far_down[3] = moved(after(far[3], far_down[1]), x_down, x_far, 3)
    from_left[0] = moved(added(after(right[0], from_left[1]), far_up[0]).astype(BF), x_up, x_up, 0)
    from_right[1] = moved(added(after(left[1], from_right[0]), far_down[1]).astype(BF), x_down, x_down, 1)
    from_left[3] = moved(after(right[3], far_up[2]), x_up, x_up, 3)
    from_right[2] = moved(after(left[2], far_down[3]), x_down, x_down, 2)
    from_left[2] = moved(added(after(right[2], from_left[0]), far_up[2]).astype(BF), x_up, x_up, 2)
    from_right[3] = moved(added(after(left[3], from_right[1]), far_down[3]).astype(BF), x_down, x_down, 3)

    here, above = [], []
    for i in range(4):
        raised = added(mine[i][1], from_left[i][1], from_right[i][1]).astype(BF)
        pairs = [(a * ROWS + n, (a + 1) * ROWS + n) for a in range(SECS - 1) for n in range(ROWS) if COUNT[n] > i]
        above.append(lax.ppermute(raised, ("sec", "row"), pairs))
        here.append(added(mine[i][0], from_left[i][0], from_right[i][0]))

    out = pl.pallas_call(
        unpack_kernel,
        in_specs=[smem] * 3 + [vmem] * 8,
        out_specs=vmem,
        out_shape=jax.ShapeDtypeStruct((4, BB, KB), BF),
        compiler_params=params,
    )(place, ket_flat, bra_flat, *here, *above)
    return out.reshape(CH, 1, 2, BB, KB)


def solution(mesh):
    placed = (
        P("row", "sec", None, None, None),
        P(None, "sec", None, None, None),
        P(None, "sec", None, None, None),
        P(),
        P(),
        P("row", None, None),
        P("row", None),
    )
    return jax.shard_map(
        body,
        mesh=mesh,
        in_specs=placed,
        out_specs=P("row", "sec", None, None, None),
        check_vma=False,
    )
```

```python
import functools

import jax
import jax.numpy as jnp
from jax import lax
from jax.experimental import pallas as pl
from jax.experimental.pallas import tpu as pltpu
from jax.sharding import PartitionSpec as P

EPW, CH = 8, 2
NZ, NX = 4, 4
SECS, ROWS = 16, 16
BB, KB = 256, 512
QUARTER = BB // NX
TR, TC = 64, 128
SHARD = 4 * (BB // TR) * (KB // TC)
SIZES = (16, 24, 32, 36, 40, 44, 48, 52, 56, 64)
BF, F32 = jnp.bfloat16, jnp.float32
STEPS = (0, -1, 1, 2)
VMEM_BYTES = 56 * 1024 * 1024
CELLS = [(b, j) for b in range(2) for j in range(CH)]


def charge(channel):
    klass = channel % 9
    return klass % 3 - 1, klass // 3 - 1


def live_at(r, b, j):
    to_b = b + charge(CH * r + j)[1]
    return jnp.where((to_b >= 0) & (to_b < 2), 1, 0)


COUNT = [sum(0 <= b + charge(CH * r + j)[1] < 2 for b, j in CELLS) for r in range(ROWS)]


def row_z(r, d):
    return (r // NX + d) % NZ * NX + r % NX


def row_x(r, d):
    return r // NX * NX + (r % NX + d) % NX


def moved(value, move):
    return lax.ppermute(value, "row", [(r, move(r)) for r in range(ROWS)])


def cell_sizes(r, a, b, j, ket_sizes, bra_sizes):
    out_a, out_b = charge(CH * r + j)
    at_a, at_b = a + out_a, b + out_b
    inside = (at_a >= 0) & (at_a < SECS) & (at_b >= 0) & (at_b < 2) & (a < SECS)
    rows = jnp.where(inside, bra_sizes[2 * jnp.clip(at_a, 0, SECS - 1) + jnp.clip(at_b, 0, 1)], 0)
    cols = ket_sizes[2 * jnp.minimum(a, SECS - 1) + b]
    return rows, cols


def tiling(r, a, first, ket_sizes, bra_sizes):
    blocks = []
    for b, j in CELLS:
        rows, cols = cell_sizes(r, a, b, j, ket_sizes, bra_sizes)
        down, over = (rows + TR - 1) // TR, (cols + TC - 1) // TC
        blocks.append((rows, cols, down, over, first))
        first = first + down * over
    return blocks, first


def each_tile(down, over, first, visit):
    @pl.loop(0, down)
    def _(i):
        lines = pl.ds(pl.multiple_of(i * TR, TR), TR)
        for c in range(KB // TC):

            @pl.when(c < over)
            def _(c=c):
                visit(first + i * over + c, i, c, lines, pl.ds(c * TC, TC))


def kept(rows, cols, i, c):
    row_at = lax.broadcasted_iota(jnp.int32, (TR, TC), 0) + i * TR
    col_at = lax.broadcasted_iota(jnp.int32, (TR, TC), 1) + c * TC
    return (row_at < rows) & (col_at < cols)


def prepare_kernel(place, ket_sizes, bra_sizes, env, bra, tiles, strip, strip_low, strip_high, classes):
    r, a = place[0], place[1]
    for n, (rows, cols, down, over, first) in enumerate(tiling(r, a, 0, ket_sizes, bra_sizes)[0]):
        b, j = CELLS[n]

        def visit(t, i, c, lines, columns, rows=rows, cols=cols, cell=2 * j + b):
            tiles[t] = jnp.where(kept(rows, cols, i, c), env[cell, lines, columns], jnp.zeros((TR, TC), BF))

        each_tile(down, over, first, visit)

    lines = pl.ds(pl.multiple_of(r % NX * QUARTER, QUARTER), QUARTER)
    for n, (sp, to_b) in enumerate(((0, 0), (0, 1), (2, 1), (1, 0), (1, 1), (3, 1))):
        value = bra[sp, to_b, lines]
        strip[n] = value
        if n < 3:
            strip_low[n] = value
        else:
            strip_high[n - 3] = value

    gathered, reduced = jnp.int32(1), jnp.int32(1)
    for d in range(4):
        gathered = jnp.maximum(gathered, tiling(row_z(r, d), a, 0, ket_sizes, bra_sizes)[1])
        own_end = tiling(row_x(r, d), a, 0, ket_sizes, bra_sizes)[1]
        reduced = jnp.maximum(reduced, tiling(row_x(r, d), a + 1, own_end, ket_sizes, bra_sizes)[1])
    classes[0] = sum(jnp.where(gathered > size, 1, 0) for size in SIZES[:-1])
    classes[1] = sum(jnp.where(reduced > 2 * size, 1, 0) for size in SIZES[:-1])


def terms_kernel(place, ket_sizes, bra_sizes, ints, values, own, behind, ahead, across, ket, bra_own, bra_rim, *refs):
    outs = refs[:4]
    env_all, bra_all, total = refs[4:]
    r, a = place[0], place[1]
    my_z, my_x = r // NX, r % NX

    @pl.loop(0, 16)
    def _(n):
        env_all[n] = jnp.zeros((BB, KB), BF)

    for k, source in enumerate((own, behind, ahead, across)):
        for n, (_, _, down, over, first) in enumerate(tiling(row_z(r, STEPS[k]), a, 0, ket_sizes, bra_sizes)[0]):

            def visit(t, i, c, lines, columns, source=source, at=4 * k + n):
                env_all[at, lines, columns] = source[t]

            each_tile(down, over, first, visit)

    for n, (sp, to_b) in enumerate(((0, 0), (0, 1), (2, 1), (1, 0), (1, 1), (3, 1))):
        bra_all[6 + n] = bra_own[sp, to_b]
    for x in range(NX):
        lines = pl.ds(QUARTER * x, QUARTER)
        for n in range(3):
            bra_all[n, lines] = bra_rim[x, n]
            bra_all[21 + n, lines] = bra_rim[x, 9 + n]
        for n in range(6):
            bra_all[12 + n, lines] = bra_rim[x, 3 + n]

    for d in range(4):
        for n, (b, j) in enumerate(CELLS):

            @pl.when(live_at(row_x(r, STEPS[d]), b, j) == 1)
            def _(at=8 * d + 2 * n):
                total[at] = jnp.zeros((BB, KB), F32)
                total[at + 1] = jnp.zeros((BB, KB), F32)

    @pl.loop(0, 4 * CH * EPW)
    def _(item):
        out_w = ints[4 * item]

        @pl.when(out_w // (CH * NX) == my_z)
        def _():
            sp = ints[4 * item + 1]
            s = ints[4 * item + 2]
            value = values[4 * item + 3]
            k, j = item // (CH * EPW), item // EPW % CH
            from_r = row_z(r, jnp.where(k == 1, 3, jnp.where(k == 2, 1, jnp.where(k == 3, 2, 0))))
            out_r, out_j = out_w // CH, out_w % CH
            forward = (out_r % NX - my_x + NX) % NX
            slot = jnp.where(forward == 1, 2, jnp.where(forward == 3, 1, jnp.where(forward == 2, 3, 0)))
            out_a, out_b = charge(out_w)
            s_a, s_b = s % 2, s // 2
            sp_a, sp_b = sp % 2, sp // 2
            for q_b in range(2):
                p_b = q_b + s_b
                live = (p_b < 2) & (live_at(from_r, q_b, j) == 1) & (live_at(out_r, p_b, out_j) == 1)

                @pl.when(live)
                def _(q_b=q_b, p_b=p_b):
                    half = jnp.dot(env_all[4 * k + 2 * q_b + j], ket[s, q_b], preferred_element_type=F32).astype(BF)
                    b_at = 6 * (s_a + out_a + 1) + 3 * sp_a + p_b + out_b + sp_b
                    term = lax.dot_general(bra_all[b_at], half, (((0,), (0,)), ((), ())), preferred_element_type=F32)
                    at = 8 * slot + 2 * (2 * p_b + out_j) + s_a
                    total[at] = total[at] + value * term

    for d in range(4):
        end = jnp.int32(0)
        for up in range(2):
            blocks, end = tiling(row_x(r, STEPS[d]), a + up, end, ket_sizes, bra_sizes)
            for n, (_, _, down, over, first) in enumerate(blocks):

                def visit(t, i, c, lines, columns, d=d, at=8 * d + 2 * n + up):
                    outs[d][t] = total[at, lines, columns].astype(BF)

                each_tile(down, over, first, visit)


def fold_kernel(half, place, ket_sizes, bra_sizes, mine, left0, left1, right0, right1, here, raised0, raised1):
    r, a = place[0], place[1]
    middle = tiling(r, a, 0, ket_sizes, bra_sizes)[1]
    end = tiling(r, a + 1, middle, ket_sizes, bra_sizes)[1]

    def put(t, left, right):
        value = mine[t].astype(F32) + left.astype(F32) + right.astype(F32)

        @pl.when(t < middle)
        def _():
            here[t] = value

        u = t - middle

        @pl.when((u >= 0) & (u < SHARD // 2))
        def _():
            raised0[u] = value.astype(BF)

        @pl.when(u >= SHARD // 2)
        def _():
            raised1[u - SHARD // 2] = value.astype(BF)

    @pl.loop(0, jnp.minimum(end, half))
    def _(t):
        put(t, left0[t], right0[t])

    @pl.loop(half, jnp.maximum(end, half))
    def _(t):
        put(t, left1[t - half], right1[t - half])


def finish_kernel(place, ket_sizes, bra_sizes, here, above0, above1, out):
    out[...] = jnp.zeros_like(out)
    r, a = place[0], place[1]
    for n, (rows, cols, down, over, first) in enumerate(tiling(r, a, 0, ket_sizes, bra_sizes)[0]):
        b, j = CELLS[n]

        def visit(t, i, c, lines, columns, rows=rows, cols=cols, cell=2 * j + b):
            def put(above):
                value = here[t] + above.astype(F32)
                out[cell, lines, columns] = jnp.where(kept(rows, cols, i, c), value, 0.0).astype(BF)

            @pl.when(t < SHARD // 2)
            def _():
                put(above0[t])

            @pl.when(t >= SHARD // 2)
            def _():
                put(above1[t - SHARD // 2])

        each_tile(down, over, first, visit)


def body(env_in, ket_mps, bra_mps, ket_sizes, bra_sizes, entries, coeffs):
    my_a = lax.axis_index("sec")
    r = lax.axis_index("row")
    place = jnp.stack([r, my_a])
    ket_flat, bra_flat = ket_sizes.reshape(-1), bra_sizes.reshape(-1)

    smem = pl.BlockSpec(memory_space=pltpu.SMEM)
    vmem = pl.BlockSpec(memory_space=pltpu.VMEM)
    shape = jax.ShapeDtypeStruct
    params = pltpu.CompilerParams(vmem_limit_bytes=VMEM_BYTES)
    own, strip, strip_low, strip_high, classes = pl.pallas_call(
        prepare_kernel,
        in_specs=[smem] * 3 + [vmem] * 2,
        out_specs=[vmem] * 4 + [smem],
        out_shape=[
            shape((SHARD, TR, TC), BF),
            shape((6, QUARTER, BB), BF),
            shape((3, QUARTER, BB), BF),
            shape((3, QUARTER, BB), BF),
            shape((2,), jnp.int32),
        ],
        compiler_params=params,
    )(place, ket_flat, bra_flat, env_in.reshape(4, BB, KB), bra_mps[:, 0])

    up = lambda n: [(i, i + n) for i in range(SECS - n)]
    down = lambda n: [(i + n, i) for i in range(SECS - n)]
    rim = jnp.concatenate([
        lax.ppermute(strip_low, "sec", up(1)),
        lax.ppermute(strip, "sec", down(1)),
        lax.ppermute(strip_high, "sec", down(2)),
    ])
    own, rim = lax.optimization_barrier((own, rim))
    bra_rim = lax.all_gather(rim, "row", axis_index_groups=[[NX * z + x for x in range(NX)] for z in range(NZ)])

    z_up, z_down, z_far = (functools.partial(row_z, d=d) for d in (1, -1, 2))
    x_up, x_down = (functools.partial(row_x, d=d) for d in (1, -1))

    def padded(parts, count):
        missing = count - sum(part.shape[0] for part in parts)
        if missing:
            parts = parts + [jnp.zeros((missing, *parts[0].shape[1:]), parts[0].dtype)]
        return jnp.concatenate(parts)

    def gather(size):
        def branch(own, items):
            first, second = own[: size // 2], own[size // 2 : size]
            behind0 = moved(first, z_up)
            ahead1 = moved(second, z_down)
            behind1 = moved(second, z_up)
            ahead0 = moved(first, z_down)
            across0 = moved(behind0, z_up)
            across1 = moved(ahead1, z_down)
            values = jnp.concatenate([items, moved(items, z_up), moved(items, z_down), moved(items, z_far)])
            return (
                padded([behind0, behind1], SHARD),
                padded([ahead0, ahead1], SHARD),
                padded([across0, across1], SHARD),
                values,
            )

        return branch

    items = jnp.concatenate([entries.reshape(-1, 3).astype(F32), coeffs.reshape(-1, 1)], axis=-1).reshape(-1)
    behind, ahead, across, values = lax.switch(classes[0], [gather(size) for size in SIZES], own, items)

    mine, left, right, far = pl.pallas_call(
        terms_kernel,
        in_specs=[smem] * 5 + [vmem] * 7,
        out_specs=[vmem] * 4,
        out_shape=[shape((2 * SHARD, TR, TC), BF)] * 4,
        scratch_shapes=[
            pltpu.VMEM((16, BB, KB), BF),
            pltpu.VMEM((24, BB, BB), BF),
            pltpu.VMEM((32, BB, KB), F32),
        ],
        compiler_params=params,
    )(place, ket_flat, bra_flat, values.astype(jnp.int32), values, own, behind, ahead, across,
      ket_mps[:, 0], bra_mps[:, 0], bra_rim)

    def reduce(size):
        half = size // 2

        def added(one, other):
            return (one.astype(F32) + other.astype(F32)).astype(BF)

        def branch(mine, left, right, far):
            far0 = moved(far[:half], x_up)
            far1 = moved(far[half:size], x_down)
            from_left1 = moved(right[half:size], x_up)
            from_right0 = moved(left[:half], x_down)
            from_left0 = moved(added(right[:half], far0), x_up)
            from_right1 = moved(added(left[half:size], far1), x_down)
            return pl.pallas_call(
                functools.partial(fold_kernel, half),
                in_specs=[smem] * 3 + [vmem] * 5,
                out_specs=[vmem] * 3,
                out_shape=[
                    shape((SHARD, TR, TC), F32),
                    shape((SHARD // 2, TR, TC), BF),
                    shape((SHARD // 2, TR, TC), BF),
                ],
                compiler_params=params,
            )(place, ket_flat, bra_flat, mine, from_left0, from_left1, from_right0, from_right1)

        return branch

    here, raised0, raised1 = lax.switch(
        classes[1], [reduce(2 * size) for size in SIZES], mine, left, right, far
    )
    above0 = lax.ppermute(raised0, "sec", up(1))
    many = [n for n in range(ROWS) if COUNT[n] > 2]
    above1 = lax.ppermute(raised1, ("sec", "row"), [(a * ROWS + n, b * ROWS + n) for a, b in up(1) for n in many])

    out = pl.pallas_call(
        finish_kernel,
        in_specs=[smem] * 3 + [vmem] * 3,
        out_specs=vmem,
        out_shape=shape((4, BB, KB), BF),
        compiler_params=params,
    )(place, ket_flat, bra_flat, here, above0, above1)
    return out.reshape(CH, 1, 2, BB, KB)


def solution(mesh):
    placed = (
        P("row", "sec", None, None, None),
        P(None, "sec", None, None, None),
        P(None, "sec", None, None, None),
        P(),
        P(),
        P("row", None, None),
        P("row", None),
    )
    return jax.shard_map(
        body,
        mesh=mesh,
        in_specs=placed,
        out_specs=P("row", "sec", None, None, None),
        check_vma=False,
    )
```

```python
import functools

import jax
import jax.numpy as jnp
from jax import lax
from jax.experimental import pallas as pl
from jax.experimental.pallas import tpu as pltpu
from jax.sharding import PartitionSpec as P

EPW, CH = 8, 2
NZ, NX = 4, 4
SECS, ROWS = 16, 16
BB, KB = 256, 512
QUARTER = BB // NX
BF, F32 = jnp.bfloat16, jnp.float32
STEPS = (0, -1, 1, 2)
VMEM_BYTES = 56 * 1024 * 1024
HEAD = 16
BRA_CELLS = ((0, 0), (0, 1), (2, 1), (1, 0), (1, 1), (3, 1))
CELLS = [(b, j) for b in range(2) for j in range(CH)]


def charge(channel):
    klass = channel % 9
    return klass % 3 - 1, klass // 3 - 1


def live_at(r, b, j):
    to_b = b + charge(CH * r + j)[1]
    return jnp.where((to_b >= 0) & (to_b < 2), 1, 0)


COUNT = [sum(0 <= b + charge(CH * r + j)[1] < 2 for b, j in CELLS) for r in range(ROWS)]


def row_z(r, d):
    return (r // NX + d) % NZ * NX + r % NX


def row_x(r, d):
    return r // NX * NX + (r % NX + d) % NX


def packed_cells(r, a, ket_sizes, bra_sizes):
    places = [(jnp.int32(0), jnp.int32(0), jnp.int32(0)) for _ in range(4)]
    count = jnp.int32(0)
    for b, j in CELLS:
        out_a, out_b = charge(CH * r + j)
        live = live_at(r, b, j)
        at_a, at_b = a + out_a, jnp.clip(b + out_b, 0, 1)
        rows = jnp.where((at_a >= 0) & (at_a < SECS), bra_sizes[2 * jnp.clip(at_a, 0, SECS - 1) + at_b], 0)
        cols = ket_sizes[2 * a + b]
        for i in range(4):
            hit = (live == 1) & (count == i)
            places[i] = tuple(jnp.where(hit, new, old) for new, old in zip((2 * j + b, rows, cols), places[i]))
        count = count + live
    return places, count


def live_count(r):
    return sum(live_at(r, b, j) for b, j in CELLS)


def keep(rows, cols):
    row_at = lax.broadcasted_iota(jnp.int32, (BB, KB), 0)
    col_at = lax.broadcasted_iota(jnp.int32, (BB, KB), 1)
    return (row_at < rows) & (col_at < cols)


def prepare_kernel(place, ket_sizes, bra_sizes, entries, coeffs, env, bra, pair, third, moving, strip, strip_low, strip_high):
    r, a = place[0], place[1]
    lane = lax.broadcasted_iota(jnp.int32, (HEAD, KB), 1)
    slot, field = lane // 8, lane % 8
    targets = (pair.at[0], pair.at[1], third, moving)
    places, count = packed_cells(r, a, ket_sizes, bra_sizes)
    for i, (cell, rows, cols) in enumerate(places):
        j, b = cell // 2, cell % 2
        head = jnp.zeros((HEAD, KB), F32)
        for n in range(EPW):
            at = EPW * j + n
            part = jnp.where(field < 3, 0.0, coeffs[at])
            for f in range(3):
                part = jnp.where(field == f, entries[3 * at + f].astype(F32), part)
            part = jnp.where(field == 7, (b + 1).astype(F32), part)
            head = jnp.where(slot == n, part, head)
        first = head.astype(BF).astype(F32)
        second = (head - first).astype(BF).astype(F32)
        last = head - first - second
        head = jnp.where(field == 4, second, jnp.where(field == 5, last, first))
        head = jnp.where(i < count, head, 0.0)
        targets[i][:HEAD] = head.astype(BF)
        targets[i][HEAD:] = jnp.where(keep(rows, cols), env[cell], jnp.zeros((BB, KB), BF))

    lines = pl.ds(pl.multiple_of(r % NX * QUARTER, QUARTER), QUARTER)
    for n, (sp, to_b) in enumerate(BRA_CELLS):
        value = bra[sp, to_b, lines]
        strip[n] = value
        if n < 3:
            strip_low[n] = value
        else:
            strip_high[n - 3] = value


def unpack_kernel(place, ket_sizes, bra_sizes, *refs):
    here, above, out = refs[:4], refs[4:8], refs[8]
    out[...] = jnp.zeros_like(out)
    for i, (cell, rows, cols) in enumerate(packed_cells(place[0], place[1], ket_sizes, bra_sizes)[0]):

        @pl.when(rows > 0)
        def _(i=i, cell=cell, rows=rows, cols=cols):
            value = here[i][...] + above[i][...].astype(F32)
            out[cell] = jnp.where(keep(rows, cols), value, 0.0).astype(BF)


def terms_kernel(place, ket_sizes, ints, values, own01, own2, behind01, behind2, ahead01, ahead2,
                 across0, across1, across2a, across2b, ket, bra_own, bra_rim, *refs):
    outs = refs[:16]
    env_all, bra_all, total = refs[16:]
    for k, (two, third) in enumerate(((own01, own2), (behind01, behind2), (ahead01, ahead2))):
        env_all[3 * k] = two[0, HEAD:]
        env_all[3 * k + 1] = two[1, HEAD:]
        env_all[3 * k + 2] = third[HEAD:]
    env_all[9] = across0[HEAD:]
    env_all[10] = across1[HEAD:]
    env_all[11, : BB // 2] = across2a[HEAD:]
    env_all[11, BB // 2 :] = across2b[...]
    for n, (sp, to_b) in enumerate(BRA_CELLS):
        bra_all[6 + n] = bra_own[sp, to_b]
    for x in range(NX):
        lines = pl.ds(QUARTER * x, QUARTER)
        for n in range(3):
            bra_all[n, lines] = bra_rim[x, n]
            bra_all[21 + n, lines] = bra_rim[x, 9 + n]
        for n in range(6):
            bra_all[12 + n, lines] = bra_rim[x, 3 + n]

    r, a = place[0], place[1]
    my_z, my_x = r // NX, r % NX
    for d in range(4):
        for i in range(4):

            @pl.when(i < live_count(row_x(r, STEPS[d])))
            def _(at=8 * d + 2 * i):
                total[at] = jnp.zeros((BB, KB), F32)
                total[at + 1] = jnp.zeros((BB, KB), F32)

    @pl.loop(0, 12 * EPW)
    def _(item):
        base = 64 * (item // EPW) + 8 * (item % EPW)
        out_w, s, code = ints[base], ints[base + 2], ints[base + 7]
        p_b, s_a = code - 1 + s // 2, s % 2
        out_r, out_j = out_w // CH, out_w % CH

        @pl.when((code > 0) & (out_w // (CH * NX) == my_z) & (p_b < 2) & (a + s_a < SECS))
        def _():
            q_b = code - 1

            @pl.when(live_at(out_r, p_b, out_j) == 1)
            def _():
                sp = ints[base + 1]
                value = values[base + 3] + values[base + 4] + values[base + 5]
                forward = (out_r % NX - my_x + NX) % NX
                slot = jnp.where(forward == 1, 2, jnp.where(forward == 3, 1, jnp.where(forward == 2, 3, 0)))
                out_a, out_b = charge(out_w)
                low = live_at(out_r, 0, 0)
                inside = low + live_at(out_r, 0, 1) + out_j * live_at(out_r, 1, 0)
                position = jnp.where(p_b == 0, out_j * low, inside)
                b_at = 6 * (s_a + out_a + 1) + 3 * (sp % 2) + p_b + out_b + sp // 2
                at = 8 * slot + 2 * position + s_a
                e_at = item // EPW
                to_size = ket_sizes[2 * (a + s_a) + p_b]
                from_size = ket_sizes[2 * a + q_b]
                for n in range(2):
                    cols = pl.ds(n * (KB // 2), KB // 2)

                    def run(depth, cols=cols):
                        half = jnp.dot(env_all[e_at, :, :depth], ket[s, q_b, :depth, cols], preferred_element_type=F32)
                        term = lax.dot_general(
                            bra_all[b_at], half.astype(BF), (((0,), (0,)), ((), ())), preferred_element_type=F32
                        )
                        total[at, :, cols] = total[at, :, cols] + value * term

                    wide = to_size > n * (KB // 2)
                    pl.when(wide & (from_size > KB // 2))(functools.partial(run, KB))
                    pl.when(wide & (from_size <= KB // 2))(functools.partial(run, KB // 2))

    for d in (3, 2, 1, 0):
        for i in range(4):

            @pl.when(i < live_count(row_x(r, STEPS[d])))
            def _(d=d, i=i):
                for up in range(2):
                    outs[4 * d + i][up] = total[8 * d + 2 * i + up].astype(BF)


def body(env_in, ket_mps, bra_mps, ket_sizes, bra_sizes, entries, coeffs):
    my_a = lax.axis_index("sec")
    r = lax.axis_index("row")
    place = jnp.stack([r, my_a])
    ket_flat, bra_flat = ket_sizes.reshape(-1), bra_sizes.reshape(-1)

    smem = pl.BlockSpec(memory_space=pltpu.SMEM)
    vmem = pl.BlockSpec(memory_space=pltpu.VMEM)
    shape = jax.ShapeDtypeStruct
    pair = shape((2, BB, KB), BF)
    params = pltpu.CompilerParams(vmem_limit_bytes=VMEM_BYTES)
    own01, own2, moving, strip, strip_low, strip_high = pl.pallas_call(
        prepare_kernel,
        in_specs=[smem] * 5 + [vmem] * 2,
        out_specs=[vmem] * 6,
        out_shape=[
            shape((2, HEAD + BB, KB), BF),
            shape((HEAD + BB, KB), BF),
            shape((HEAD + BB, KB), BF),
            shape((6, QUARTER, BB), BF),
            shape((3, QUARTER, BB), BF),
            shape((3, QUARTER, BB), BF),
        ],
        compiler_params=params,
    )(place, ket_flat, bra_flat, entries.reshape(-1), coeffs.reshape(-1), env_in.reshape(4, BB, KB), bra_mps[:, 0])

    same = lambda n: n
    z_up, z_down = (lambda n: row_z(n, 1)), (lambda n: row_z(n, -1))
    x_up, x_down, x_far = (lambda n: row_x(n, 1)), (lambda n: row_x(n, -1)), (lambda n: row_x(n, 2))

    def sent(value, move, owner, rows):
        return lax.ppermute(value, "row", [(n, move(n)) for n in range(ROWS) if owner(n) in rows])

    everyone = set(range(ROWS))
    full = [n for n in range(ROWS) if COUNT[n] == 4]
    takers, lent = set(), []
    for n in full:
        taker = next(m for m in (row_x(n, 1), row_x(n, -1)) if COUNT[m] == 2 and m not in takers)
        takers.add(taker)
        lent.append((n, taker))
    three = {n for n in range(ROWS) if COUNT[n] > 2} | takers
    behind01 = sent(own01, z_up, same, everyone)
    ahead01 = sent(own01, z_down, same, everyone)
    own2 = own2 + lax.ppermute(moving, "row", lent)
    behind2 = sent(own2, z_up, same, three)
    ahead2 = sent(own2, z_down, same, three)
    across0 = sent(behind01[0], z_up, z_down, everyone)
    across1 = sent(ahead01[1], z_down, z_up, everyone)
    across2a = sent(behind2[: HEAD + BB // 2], z_up, z_down, three)
    across2b = sent(ahead2[HEAD + BB // 2 :], z_down, z_up, three)

    up = lambda n: [(i, i + n) for i in range(SECS - n)]
    down = lambda n: [(i + n, i) for i in range(SECS - n)]
    rim = jnp.concatenate([
        lax.ppermute(strip_low, "sec", up(1)),
        lax.ppermute(strip, "sec", down(1)),
        lax.ppermute(strip_high, "sec", down(2)),
    ])
    bra_rim = lax.all_gather(rim, "row", axis_index_groups=[[NX * z + x for x in range(NX)] for z in range(NZ)])

    heads = [own01[0], own01[1], own2, behind01[0], behind01[1], behind2, ahead01[0], ahead01[1], ahead2,
             across0, across1, across2a]
    values = jnp.concatenate([head[0, :64] for head in heads]).astype(F32)

    sums = pl.pallas_call(
        terms_kernel,
        in_specs=[smem] * 4 + [vmem] * 13,
        out_specs=[vmem] * 16,
        out_shape=[pair] * 16,
        scratch_shapes=[
            pltpu.VMEM((12, BB, KB), BF),
            pltpu.VMEM((24, BB, BB), BF),
            pltpu.VMEM((32, BB, KB), F32),
        ],
        compiler_params=params,
    )(place, ket_flat, values.astype(jnp.int32), values, own01, own2, behind01, behind2, ahead01, ahead2,
      across0, across1, across2a, across2b, ket_mps[:, 0], bra_mps[:, 0], bra_rim)
    mine, left, right, far = sums[:4], sums[4:8], sums[8:12], sums[12:]

    def added(*parts):
        return functools.reduce(jnp.add, [part.astype(F32) for part in parts])

    def moved(value, move, owner, i):
        return sent(value, move, owner, {n for n in range(ROWS) if COUNT[n] > i})

    far_up = {i: moved(far[i], x_up, x_far, i) for i in (0, 2)}
    far_down = {i: moved(far[i], x_down, x_far, i) for i in (1, 3)}
    from_left = {i: moved(right[i], x_up, x_up, i) for i in (1, 3)}
    from_right = {i: moved(left[i], x_down, x_down, i) for i in (0, 2)}
    for i in (0, 2):
        from_left[i] = moved(added(right[i], far_up[i]).astype(BF), x_up, x_up, i)
    for i in (1, 3):
        from_right[i] = moved(added(left[i], far_down[i]).astype(BF), x_down, x_down, i)

    here, above = [], []
    for i in range(4):
        raised = added(mine[i][1], from_left[i][1], from_right[i][1]).astype(BF)
        pairs = [(a * ROWS + n, (a + 1) * ROWS + n) for a in range(SECS - 1) for n in range(ROWS) if COUNT[n] > i]
        above.append(lax.ppermute(raised, ("sec", "row"), pairs))
        here.append(added(mine[i][0], from_left[i][0], from_right[i][0]))

    out = pl.pallas_call(
        unpack_kernel,
        in_specs=[smem] * 3 + [vmem] * 8,
        out_specs=vmem,
        out_shape=shape((4, BB, KB), BF),
        compiler_params=params,
    )(place, ket_flat, bra_flat, *here, *above)
    return out.reshape(CH, 1, 2, BB, KB)


def solution(mesh):
    placed = (
        P("row", "sec", None, None, None),
        P(None, "sec", None, None, None),
        P(None, "sec", None, None, None),
        P(),
        P(),
        P("row", None, None),
        P("row", None),
    )
    return jax.shard_map(
        body,
        mesh=mesh,
        in_specs=placed,
        out_specs=P("row", "sec", None, None, None),
        check_vma=False,
    )
```

```python
import functools

import jax
import jax.numpy as jnp
from jax import lax
from jax.experimental import pallas as pl
from jax.experimental.pallas import tpu as pltpu
from jax.sharding import PartitionSpec as P

EPW, CH = 8, 2
NZ, NX = 4, 4
SECS, ROWS = 16, 16
BB, KB = 256, 512
QUARTER = BB // NX
BF, F32 = jnp.bfloat16, jnp.float32
STEPS = (0, -1, 1, 2)
VMEM_BYTES = 56 * 1024 * 1024
HEAD = 16
BRA_CELLS = ((0, 0), (0, 1), (2, 1), (1, 0), (1, 1), (3, 1))
CELLS = [(b, j) for b in range(2) for j in range(CH)]


def charge(channel):
    klass = channel % 9
    return klass % 3 - 1, klass // 3 - 1


def live_at(r, b, j):
    to_b = b + charge(CH * r + j)[1]
    return jnp.where((to_b >= 0) & (to_b < 2), 1, 0)


COUNT = [sum(0 <= b + charge(CH * r + j)[1] < 2 for b, j in CELLS) for r in range(ROWS)]


def row_z(r, d):
    return (r // NX + d) % NZ * NX + r % NX


def row_x(r, d):
    return r // NX * NX + (r % NX + d) % NX


def packed_cells(r, a, ket_sizes, bra_sizes):
    places = [(jnp.int32(0), jnp.int32(0), jnp.int32(0)) for _ in range(4)]
    count = jnp.int32(0)
    for b, j in CELLS:
        out_a, out_b = charge(CH * r + j)
        live = live_at(r, b, j)
        at_a, at_b = a + out_a, jnp.clip(b + out_b, 0, 1)
        rows = jnp.where((at_a >= 0) & (at_a < SECS), bra_sizes[at_b, jnp.clip(at_a, 0, SECS - 1)], 0)
        cols = ket_sizes[b, a]
        for i in range(4):
            hit = (live == 1) & (count == i)
            places[i] = tuple(jnp.where(hit, new, old) for new, old in zip((2 * j + b, rows, cols), places[i]))
        count = count + live
    return places, count


def live_count(r):
    return sum(live_at(r, b, j) for b, j in CELLS)


def keep(rows, cols):
    row_at = lax.broadcasted_iota(jnp.int32, (BB, KB), 0)
    col_at = lax.broadcasted_iota(jnp.int32, (BB, KB), 1)
    return (row_at < rows) & (col_at < cols)


def prepare_kernel(place, ket_sizes, bra_sizes, entries, coeffs, env, first_out, second_out, third_out, moving):
    r, a = place[0], place[1]
    lane = lax.broadcasted_iota(jnp.int32, (HEAD, KB), 1)
    slot, field = lane // 8, lane % 8
    places, count = packed_cells(r, a, ket_sizes, bra_sizes)
    for i, (cell, rows, cols) in enumerate(places):
        target = (first_out, second_out, third_out, moving)[i]
        j, b = cell // 2, cell % 2
        head = jnp.zeros((HEAD, KB), F32)
        for n in range(EPW):
            part = jnp.where(field < 3, 0.0, coeffs[j, n])
            for f in range(3):
                part = jnp.where(field == f, entries[f, j, n].astype(F32), part)
            part = jnp.where(field == 7, (b + 1).astype(F32), part)
            head = jnp.where(slot == n, part, head)
        first = head.astype(BF).astype(F32)
        second = (head - first).astype(BF).astype(F32)
        last = head - first - second
        head = jnp.where(field == 4, second, jnp.where(field == 5, last, first))
        head = jnp.where(i < count, head, 0.0)
        target[:HEAD] = head.astype(BF)
        target[HEAD:] = jnp.where(keep(rows, cols), env[cell], jnp.zeros((BB, KB), BF))


def bra_kernel(place, bra, flipped, strip, strip_low, strip_high):
    r = place[0]
    lines = pl.ds(pl.multiple_of(r % NX * QUARTER, QUARTER), QUARTER)
    for n, (sp, to_b) in enumerate(BRA_CELLS):
        flipped[n] = bra[sp, to_b].T
        value = flipped[n, lines]
        strip[n] = value
        if n < 3:
            strip_low[n] = value
        else:
            strip_high[n - 3] = value


def unpack_kernel(place, ket_sizes, bra_sizes, *refs):
    here, above, out = refs[:4], refs[4:6], refs[6]
    out[...] = jnp.zeros_like(out)
    for i, (cell, rows, cols) in enumerate(packed_cells(place[0], place[1], ket_sizes, bra_sizes)[0]):

        @pl.when(rows > 0)
        def _(i=i, cell=cell, rows=rows, cols=cols):
            value = here[i][...] + above[i // 2][i % 2].astype(F32)
            out[cell] = jnp.where(keep(rows, cols), value, 0.0).astype(BF)


def terms_kernel(place, ket_sizes, ints, values, *refs):
    envs, across2b, ket_in, bra_own, rim0, rim1, rim2 = refs[:12], *refs[12:18]
    outs = refs[18:34]
    env_all, ket, bra_all, total, rounded, env_sem, ket_sem, bra_sem, out_sem = refs[34:]
    x = place[0] % NX
    copies = []
    for n in range(12):
        rows = BB if n < 11 else BB // 2
        copies.append(pltpu.make_async_copy(envs[n].at[pl.ds(HEAD, rows)], env_all.at[n, pl.ds(0, rows)], env_sem.at[n]))
    copies.append(pltpu.make_async_copy(across2b, env_all.at[11, pl.ds(BB // 2, BB // 2)], env_sem.at[12]))
    copies += [pltpu.make_async_copy(ket_in.at[s], ket.at[s], ket_sem.at[s]) for s in range(4)]
    copies.append(pltpu.make_async_copy(bra_own, bra_all.at[pl.ds(6, 6)], bra_sem.at[0]))
    y = NX - 1 - x
    for n, (ref, at, owner) in enumerate(((rim0, 0, x), (rim1, 0, x + 1 - 2 * (x % 2)), (rim2, 0, y), (rim2, 12, y + 1 - 2 * (y % 2)))):
        lines = pl.ds(pl.multiple_of(QUARTER * owner, QUARTER), QUARTER)
        for m, (first, count, to) in enumerate(((0, 3, 0), (3, 6, 12), (9, 3, 21))):
            copies.append(pltpu.make_async_copy(
                ref.at[pl.ds(at + first, count)], bra_all.at[pl.ds(to, count), lines], bra_sem.at[1 + 3 * n + m]
            ))
    for copy in copies:
        copy.start()

    r, a = place[0], place[1]
    my_z, my_x = r // NX, r % NX
    for d in range(4):
        for i in range(4):

            @pl.when(i < live_count(row_x(r, STEPS[d])))
            def _(at=8 * d + 2 * i):
                total[at] = jnp.zeros((BB, KB), F32)
                total[at + 1] = jnp.zeros((BB, KB), F32)

    for copy in copies:
        copy.wait()

    @pl.loop(0, 12 * EPW)
    def _(item):
        base = 64 * (item // EPW) + 8 * (item % EPW)
        out_w, s, code = ints[base], ints[base + 2], ints[base + 7]
        p_b, s_a = code - 1 + s // 2, s % 2
        out_r, out_j = out_w // CH, out_w % CH

        @pl.when((code > 0) & (out_w // (CH * NX) == my_z) & (p_b < 2) & (a + s_a < SECS))
        def _():
            q_b = code - 1

            @pl.when(live_at(out_r, p_b, out_j) == 1)
            def _():
                sp = ints[base + 1]
                value = values[base + 3] + values[base + 4] + values[base + 5]
                forward = (out_r % NX - my_x + NX) % NX
                slot = jnp.where(forward == 1, 2, jnp.where(forward == 3, 1, jnp.where(forward == 2, 3, 0)))
                out_a, out_b = charge(out_w)
                low = live_at(out_r, 0, 0)
                inside = low + live_at(out_r, 0, 1) + out_j * live_at(out_r, 1, 0)
                position = jnp.where(p_b == 0, out_j * low, inside)
                b_at = 6 * (s_a + out_a + 1) + 3 * (sp % 2) + p_b + out_b + sp // 2
                at = 8 * slot + 2 * position + s_a
                e_at = item // EPW
                to_size = ket_sizes[p_b, a + s_a]
                from_size = ket_sizes[q_b, a]
                for n in range(2):
                    cols = pl.ds(n * (KB // 2), KB // 2)

                    def run(depth, cols=cols):
                        half = jnp.dot(env_all[e_at, :, :depth], ket[s, q_b, :depth, cols], preferred_element_type=F32)
                        term = jnp.dot(bra_all[b_at], half.astype(BF), preferred_element_type=F32)
                        total[at, :, cols] = total[at, :, cols] + value * term

                    wide = to_size > n * (KB // 2)
                    pl.when(wide & (from_size > KB // 2))(functools.partial(run, KB))
                    pl.when(wide & (from_size <= KB // 2))(functools.partial(run, KB // 2))

    def stored(d, i):
        return pltpu.make_async_copy(rounded.at[4 * d + i], outs[4 * d + i], out_sem.at[4 * d + i])

    for d in (3, 2, 1, 0):
        for i in range(4):

            @pl.when(i < live_count(row_x(r, STEPS[d])))
            def _(d=d, i=i):
                for up in range(2):
                    rounded[4 * d + i, up] = total[8 * d + 2 * i + up].astype(BF)
                stored(d, i).start()

    for d in (3, 2, 1, 0):
        for i in range(4):

            @pl.when(i < live_count(row_x(r, STEPS[d])))
            def _(d=d, i=i):
                stored(d, i).wait()


def body(env_in, ket_mps, bra_mps, ket_sizes, bra_sizes, entries, coeffs):
    my_a = lax.axis_index("sec")
    r = lax.axis_index("row")
    place = jnp.stack([r, my_a])
    ket_flat, bra_flat = ket_sizes.T, bra_sizes.T

    smem = pl.BlockSpec(memory_space=pltpu.SMEM)
    vmem = pl.BlockSpec(memory_space=pltpu.VMEM)
    shape = jax.ShapeDtypeStruct
    pair = shape((2, BB, KB), BF)
    params = pltpu.CompilerParams(vmem_limit_bytes=VMEM_BYTES)
    payload = shape((HEAD + BB, KB), BF)
    own0, own1, own2, moving = pl.pallas_call(
        prepare_kernel,
        in_specs=[smem] * 5 + [vmem],
        out_specs=[vmem] * 4,
        out_shape=[payload] * 4,
        compiler_params=params,
    )(place, ket_flat, bra_flat, entries.transpose(2, 0, 1), coeffs, env_in.reshape(4, BB, KB))

    same = lambda n: n
    z_up, z_down = (lambda n: row_z(n, 1)), (lambda n: row_z(n, -1))
    x_up, x_down, x_far = (lambda n: row_x(n, 1)), (lambda n: row_x(n, -1)), (lambda n: row_x(n, 2))

    def sent(value, move, owner, rows):
        return lax.ppermute(value, "row", [(n, move(n)) for n in range(ROWS) if owner(n) in rows])

    everyone = set(range(ROWS))
    full = [n for n in range(ROWS) if COUNT[n] == 4]
    takers, lent = set(), []
    for n in full:
        taker = next(m for m in (row_x(n, 1), row_x(n, -1)) if COUNT[m] == 2 and m not in takers)
        takers.add(taker)
        lent.append((n, taker))
    three = {n for n in range(ROWS) if COUNT[n] > 2} | takers
    behind0 = sent(own0, z_up, same, everyone)
    ahead1 = sent(own1, z_down, same, everyone)
    own2 = own2 + lax.ppermute(moving, "row", lent)
    behind1 = sent(own1, z_up, same, everyone)
    ahead0 = sent(own0, z_down, same, everyone)
    behind2 = sent(own2, z_up, same, three)
    ahead2 = sent(own2, z_down, same, three)
    across0 = sent(behind0, z_up, z_down, everyone)
    across1 = sent(ahead1, z_down, z_up, everyone)
    across2a = sent(behind2[: HEAD + BB // 2], z_up, z_down, three)
    across2b = sent(ahead2[HEAD + BB // 2 :], z_down, z_up, three)

    bra_in = lax.optimization_barrier((bra_mps, behind0, ahead1))[0]
    bra_own, strip, strip_low, strip_high = pl.pallas_call(
        bra_kernel,
        in_specs=[smem, vmem],
        out_specs=[vmem] * 4,
        out_shape=[
            shape((6, BB, BB), BF),
            shape((6, QUARTER, BB), BF),
            shape((3, QUARTER, BB), BF),
            shape((3, QUARTER, BB), BF),
        ],
        compiler_params=params,
    )(place, bra_in[:, 0])
    up = lambda n: [(i, i + n) for i in range(SECS - n)]
    down = lambda n: [(i + n, i) for i in range(SECS - n)]
    rim0 = jnp.concatenate([
        lax.ppermute(strip_low, "sec", up(1)),
        lax.ppermute(strip, "sec", down(1)),
        lax.ppermute(strip_high, "sec", down(2)),
    ])
    rim1 = lax.ppermute(rim0, "row", [(n, n ^ 1) for n in range(ROWS)])
    rim2 = lax.ppermute(jnp.concatenate([rim0, rim1]), "row", [(n, n ^ 3) for n in range(ROWS)])

    envs = [own0, own1, own2, behind0, behind1, behind2, ahead0, ahead1, ahead2, across0, across1, across2a]
    values = jnp.concatenate([part[0, :64] for part in envs]).astype(F32)

    hbm = pl.BlockSpec(memory_space=pl.ANY)
    sums = pl.pallas_call(
        terms_kernel,
        in_specs=[smem] * 4 + [hbm] * 18,
        out_specs=[hbm] * 16,
        out_shape=[pair] * 16,
        scratch_shapes=[
            pltpu.VMEM((12, BB, KB), BF),
            pltpu.VMEM((4, 2, KB, KB), BF),
            pltpu.VMEM((24, BB, BB), BF),
            pltpu.VMEM((32, BB, KB), F32),
            pltpu.VMEM((16, 2, BB, KB), BF),
            pltpu.SemaphoreType.DMA((13,)),
            pltpu.SemaphoreType.DMA((4,)),
            pltpu.SemaphoreType.DMA((13,)),
            pltpu.SemaphoreType.DMA((16,)),
        ],
        compiler_params=params,
    )(place, ket_flat, values.astype(jnp.int32), values, *envs, across2b, ket_mps[:, 0], bra_own, rim0, rim1, rim2)
    mine, left, right, far = sums[:4], sums[4:8], sums[8:12], sums[12:]

    def added(*parts):
        return functools.reduce(jnp.add, [part.astype(F32) for part in parts])

    def moved(value, move, owner, i):
        return sent(value, move, owner, {n for n in range(ROWS) if COUNT[n] > i})

    far_up = {i: moved(far[i], x_up, x_far, i) for i in (0, 2)}
    far_down = {i: moved(far[i], x_down, x_far, i) for i in (1, 3)}
    from_left = {i: moved(right[i], x_up, x_up, i) for i in (1, 3)}
    from_right = {i: moved(left[i], x_down, x_down, i) for i in (0, 2)}
    for i in (0, 2):
        from_left[i] = moved(added(right[i], far_up[i]).astype(BF), x_up, x_up, i)
    for i in (1, 3):
        from_right[i] = moved(added(left[i], far_down[i]).astype(BF), x_down, x_down, i)

    here = [added(mine[i][0], from_left[i][0], from_right[i][0]) for i in range(4)]
    raised = [added(mine[i][1], from_left[i][1], from_right[i][1]).astype(BF) for i in range(4)]
    above = []
    for i in (0, 2):
        pairs = [(a * ROWS + n, (a + 1) * ROWS + n) for a in range(SECS - 1) for n in range(ROWS) if COUNT[n] > i]
        above.append(lax.ppermute(jnp.stack(raised[i : i + 2]), ("sec", "row"), pairs))

    out = pl.pallas_call(
        unpack_kernel,
        in_specs=[smem] * 3 + [vmem] * 6,
        out_specs=vmem,
        out_shape=shape((4, BB, KB), BF),
        compiler_params=params,
    )(place, ket_flat, bra_flat, *here, *above)
    return out.reshape(CH, 1, 2, BB, KB)


def solution(mesh):
    placed = (
        P("row", "sec", None, None, None),
        P(None, "sec", None, None, None),
        P(None, "sec", None, None, None),
        P(),
        P(),
        P("row", None, None),
        P("row", None),
    )
    return jax.shard_map(
        body,
        mesh=mesh,
        in_specs=placed,
        out_specs=P("row", "sec", None, None, None),
        check_vma=False,
    )
```

```python
import functools

import jax
import jax.numpy as jnp
from jax import lax
from jax.experimental import pallas as pl
from jax.experimental.pallas import tpu as pltpu
from jax.sharding import PartitionSpec as P

EPW, CH = 8, 2
NZ, NX = 4, 4
SECS, ROWS = 16, 16
BB, KB = 256, 512
QUARTER = BB // NX
TOGETHER = 2
BF, F32 = jnp.bfloat16, jnp.float32
STEPS = (0, -1, 1, 2)
VMEM_BYTES = 56 * 1024 * 1024
HEAD = 16
BRA_CELLS = ((0, 0), (0, 1), (2, 1), (1, 0), (1, 1), (3, 1))
CELLS = [(b, j) for b in range(2) for j in range(CH)]


def after(value, *others):
    return lax.optimization_barrier((value, *others))[0] if others else value


def charge(channel):
    klass = channel % 9
    return klass % 3 - 1, klass // 3 - 1


def live_at(r, b, j):
    to_b = b + charge(CH * r + j)[1]
    return jnp.where((to_b >= 0) & (to_b < 2), 1, 0)


COUNT = [sum(0 <= b + charge(CH * r + j)[1] < 2 for b, j in CELLS) for r in range(ROWS)]


def row_z(r, d):
    return (r // NX + d) % NZ * NX + r % NX


def row_x(r, d):
    return r // NX * NX + (r % NX + d) % NX


def packed_cells(r, a, ket_sizes, bra_sizes):
    places = [(jnp.int32(0), jnp.int32(0), jnp.int32(0)) for _ in range(4)]
    count = jnp.int32(0)
    for b, j in CELLS:
        out_a, out_b = charge(CH * r + j)
        live = live_at(r, b, j)
        at_a, at_b = a + out_a, jnp.clip(b + out_b, 0, 1)
        rows = jnp.where((at_a >= 0) & (at_a < SECS), bra_sizes[at_b, jnp.clip(at_a, 0, SECS - 1)], 0)
        cols = ket_sizes[b, a]
        for i in range(4):
            hit = (live == 1) & (count == i)
            places[i] = tuple(jnp.where(hit, new, old) for new, old in zip((2 * j + b, rows, cols), places[i]))
        count = count + live
    return places, count


def live_count(r):
    return sum(live_at(r, b, j) for b, j in CELLS)


def keep(rows, cols):
    row_at = lax.broadcasted_iota(jnp.int32, (BB, KB), 0)
    col_at = lax.broadcasted_iota(jnp.int32, (BB, KB), 1)
    return (row_at < rows) & (col_at < cols)


def prepare_kernel(place, ket_sizes, bra_sizes, entries, coeffs, env, first_out, second_out, third_out, moving):
    r, a = place[0], place[1]
    lane = lax.broadcasted_iota(jnp.int32, (HEAD, KB), 1)
    slot, field = lane // 8, lane % 8
    places, count = packed_cells(r, a, ket_sizes, bra_sizes)
    for i, (cell, rows, cols) in enumerate(places):
        target = (first_out, second_out, third_out, moving)[i]
        j, b = cell // 2, cell % 2
        head = jnp.zeros((HEAD, KB), F32)
        for n in range(EPW):
            part = jnp.where(field < 3, 0.0, coeffs[j, n])
            for f in range(3):
                part = jnp.where(field == f, entries[f, j, n].astype(F32), part)
            part = jnp.where(field == 7, (b + 1).astype(F32), part)
            head = jnp.where(slot == n, part, head)
        first = head.astype(BF).astype(F32)
        second = (head - first).astype(BF).astype(F32)
        last = head - first - second
        head = jnp.where(field == 4, second, jnp.where(field == 5, last, first))
        head = jnp.where(i < count, head, 0.0)
        target[:HEAD] = head.astype(BF)
        target[HEAD:] = jnp.where(keep(rows, cols), env[cell], jnp.zeros((BB, KB), BF))


def bra_kernel(place, bra, flipped, strip, strip_low, strip_high):
    r = place[0]
    lines = pl.ds(pl.multiple_of(r % NX * QUARTER, QUARTER), QUARTER)
    for n, (sp, to_b) in enumerate(BRA_CELLS):
        flipped[n] = bra[sp, to_b].T
        value = flipped[n, lines]
        strip[n] = value
        if n < 3:
            strip_low[n] = value
        else:
            strip_high[n - 3] = value


def unpack_kernel(place, ket_sizes, bra_sizes, *refs):
    here, above, out = refs[:4], refs[4:6], refs[6]
    out[...] = jnp.zeros_like(out)
    for i, (cell, rows, cols) in enumerate(packed_cells(place[0], place[1], ket_sizes, bra_sizes)[0]):

        @pl.when(rows > 0)
        def _(i=i, cell=cell, rows=rows, cols=cols):
            value = here[i][...] + above[i // 2][i % 2].astype(F32)
            out[cell] = jnp.where(keep(rows, cols), value, 0.0).astype(BF)


def terms_kernel(place, ints, values, *refs):
    envs, across2b, ket_in, bra_own, rim0, rim1, rim2 = refs[:12], *refs[12:18]
    outs = refs[18:34]
    env_all, ket, bra_all, total, rounded, todo, scale, env_sem, ket_sem, bra_sem, out_sem = refs[34:]
    x = place[0] % NX
    copies = []
    for n in range(12):
        rows = BB if n < 11 else BB // 2
        copies.append(pltpu.make_async_copy(envs[n].at[pl.ds(HEAD, rows)], env_all.at[n, pl.ds(0, rows)], env_sem.at[n]))
    copies.append(pltpu.make_async_copy(across2b, env_all.at[11, pl.ds(BB // 2, BB // 2)], env_sem.at[12]))
    copies += [pltpu.make_async_copy(ket_in.at[s], ket.at[pl.ds(2 * s, 2)], ket_sem.at[s]) for s in range(4)]
    copies.append(pltpu.make_async_copy(bra_own, bra_all.at[pl.ds(6, 6)], bra_sem.at[0]))
    y = NX - 1 - x
    for n, (ref, at, owner) in enumerate(((rim0, 0, x), (rim1, 0, x + 1 - 2 * (x % 2)), (rim2, 0, y), (rim2, 12, y + 1 - 2 * (y % 2)))):
        lines = pl.ds(pl.multiple_of(QUARTER * owner, QUARTER), QUARTER)
        for m, (first, count, to) in enumerate(((0, 3, 0), (3, 6, 12), (9, 3, 21))):
            copies.append(pltpu.make_async_copy(
                ref.at[pl.ds(at + first, count)], bra_all.at[pl.ds(to, count), lines], bra_sem.at[1 + 3 * n + m]
            ))
    for copy in copies:
        copy.start()

    r, a = place[0], place[1]
    my_z, my_x = r // NX, r % NX
    for d in range(4):
        for i in range(4):

            @pl.when(i < live_count(row_x(r, STEPS[d])))
            def _(at=8 * d + 2 * i):
                total[at] = jnp.zeros((BB, KB), F32)
                total[at + 1] = jnp.zeros((BB, KB), F32)

    def listed(item, count):
        base = 64 * (item // EPW) + 8 * (item % EPW)
        out_w, sp, s, code = ints[base], ints[base + 1], ints[base + 2], ints[base + 7]
        q_b = code - 1
        p_b, s_a = q_b + s // 2, s % 2
        out_r, out_j = out_w // CH, out_w % CH
        forward = (out_r % NX - my_x + NX) % NX
        slot = jnp.where(forward == 1, 2, jnp.where(forward == 3, 1, jnp.where(forward == 2, 3, 0)))
        out_a, out_b = charge(out_w)
        low = live_at(out_r, 0, 0)
        inside = low + live_at(out_r, 0, 1) + out_j * live_at(out_r, 1, 0)
        position = jnp.where(p_b == 0, out_j * low, inside)
        live = (code > 0) & (out_w // (CH * NX) == my_z) & (p_b < 2) & (a + s_a < SECS)
        live = live & (live_at(out_r, p_b, out_j) == 1)

        @pl.when(live)
        def _():
            todo[4 * count] = item // EPW
            todo[4 * count + 1] = 2 * s + q_b
            todo[4 * count + 2] = 6 * (s_a + out_a + 1) + 3 * (sp % 2) + p_b + out_b + sp // 2
            todo[4 * count + 3] = 8 * slot + 2 * position + s_a
            scale[count] = values[base + 3] + values[base + 4] + values[base + 5]

        return count + jnp.where(live, 1, 0)

    count = lax.fori_loop(0, 12 * EPW, listed, jnp.int32(0))
    for n in range(TOGETHER - 1):
        for field in range(3):
            todo[4 * (count + n) + field] = 0
        todo[4 * (count + n) + 3] = 32
        scale[count + n] = 0.0

    for copy in copies:
        copy.wait()

    @pl.loop(0, (count + TOGETHER - 1) // TOGETHER)
    def _(step):
        places = [step * TOGETHER + n for n in range(TOGETHER)]
        halves = [
            jnp.dot(env_all[todo[4 * n]], ket[todo[4 * n + 1]], preferred_element_type=F32).astype(BF) for n in places
        ]
        terms = [
            jnp.dot(bra_all[todo[4 * n + 2]], half, preferred_element_type=F32) for n, half in zip(places, halves)
        ]
        for n, term in zip(places, terms):
            at = todo[4 * n + 3]
            total[at] = total[at] + scale[n] * term

    def stored(d, i):
        return pltpu.make_async_copy(rounded.at[4 * d + i], outs[4 * d + i], out_sem.at[4 * d + i])

    for d in (3, 2, 1, 0):
        for i in range(4):

            @pl.when(i < live_count(row_x(r, STEPS[d])))
            def _(d=d, i=i):
                for up in range(2):
                    rounded[4 * d + i, up] = total[8 * d + 2 * i + up].astype(BF)
                stored(d, i).start()

    for d in (3, 2, 1, 0):
        for i in range(4):

            @pl.when(i < live_count(row_x(r, STEPS[d])))
            def _(d=d, i=i):
                stored(d, i).wait()


def body(env_in, ket_mps, bra_mps, ket_sizes, bra_sizes, entries, coeffs):
    my_a = lax.axis_index("sec")
    r = lax.axis_index("row")
    place = jnp.stack([r, my_a])
    ket_flat, bra_flat = ket_sizes.T, bra_sizes.T

    smem = pl.BlockSpec(memory_space=pltpu.SMEM)
    vmem = pl.BlockSpec(memory_space=pltpu.VMEM)
    shape = jax.ShapeDtypeStruct
    pair = shape((2, BB, KB), BF)
    params = pltpu.CompilerParams(vmem_limit_bytes=VMEM_BYTES)
    payload = shape((HEAD + BB, KB), BF)
    own0, own1, own2, moving = pl.pallas_call(
        prepare_kernel,
        in_specs=[smem] * 5 + [vmem],
        out_specs=[vmem] * 4,
        out_shape=[payload] * 4,
        compiler_params=params,
    )(place, ket_flat, bra_flat, entries.transpose(2, 0, 1), coeffs, env_in.reshape(4, BB, KB))

    same = lambda n: n
    z_up, z_down = (lambda n: row_z(n, 1)), (lambda n: row_z(n, -1))
    x_up, x_down, x_far = (lambda n: row_x(n, 1)), (lambda n: row_x(n, -1)), (lambda n: row_x(n, 2))

    def sent(value, move, owner, rows):
        return lax.ppermute(value, "row", [(n, move(n)) for n in range(ROWS) if owner(n) in rows])

    everyone = set(range(ROWS))
    full = [n for n in range(ROWS) if COUNT[n] == 4]
    takers, lent = set(), []
    for n in full:
        taker = next(m for m in (row_x(n, 1), row_x(n, -1)) if COUNT[m] == 2 and m not in takers)
        takers.add(taker)
        lent.append((n, taker))
    three = {n for n in range(ROWS) if COUNT[n] > 2} | takers
    behind0 = sent(own0, z_up, same, everyone)
    ahead1 = sent(own1, z_down, same, everyone)
    own2 = own2 + lax.ppermute(moving, "row", lent)
    behind1 = sent(after(own1, behind0, ahead1), z_up, same, everyone)
    ahead0 = sent(after(own0, behind0, ahead1), z_down, same, everyone)
    behind2 = sent(own2, z_up, same, three)
    ahead2 = sent(own2, z_down, same, three)
    across0 = sent(behind0, z_up, z_down, everyone)
    across1 = sent(ahead1, z_down, z_up, everyone)
    across2a = sent(behind2[: HEAD + BB // 2], z_up, z_down, three)
    across2b = sent(ahead2[HEAD + BB // 2 :], z_down, z_up, three)

    bra_in = lax.optimization_barrier((bra_mps, behind0, ahead1))[0]
    bra_own, strip, strip_low, strip_high = pl.pallas_call(
        bra_kernel,
        in_specs=[smem, vmem],
        out_specs=[vmem] * 4,
        out_shape=[
            shape((6, BB, BB), BF),
            shape((6, QUARTER, BB), BF),
            shape((3, QUARTER, BB), BF),
            shape((3, QUARTER, BB), BF),
        ],
        compiler_params=params,
    )(place, bra_in[:, 0])
    up = lambda n: [(i, i + n) for i in range(SECS - n)]
    down = lambda n: [(i + n, i) for i in range(SECS - n)]
    rim0 = jnp.concatenate([
        lax.ppermute(strip_low, "sec", up(1)),
        lax.ppermute(strip, "sec", down(1)),
        lax.ppermute(strip_high, "sec", down(2)),
    ])
    rim1 = lax.ppermute(rim0, "row", [(n, n ^ 1) for n in range(ROWS)])
    rim2 = lax.ppermute(jnp.concatenate([rim0, rim1]), "row", [(n, n ^ 3) for n in range(ROWS)])

    envs = [own0, own1, own2, behind0, behind1, behind2, ahead0, ahead1, ahead2, across0, across1, across2a]
    values = jnp.concatenate([part[0, :64] for part in envs]).astype(F32)

    hbm = pl.BlockSpec(memory_space=pl.ANY)
    sums = pl.pallas_call(
        terms_kernel,
        in_specs=[smem] * 3 + [hbm] * 18,
        out_specs=[hbm] * 16,
        out_shape=[pair] * 16,
        scratch_shapes=[
            pltpu.VMEM((12, BB, KB), BF),
            pltpu.VMEM((8, KB, KB), BF),
            pltpu.VMEM((24, BB, BB), BF),
            pltpu.VMEM((33, BB, KB), F32),
            pltpu.VMEM((16, 2, BB, KB), BF),
            pltpu.SMEM((4 * (12 * EPW + TOGETHER),), jnp.int32),
            pltpu.SMEM((12 * EPW + TOGETHER,), F32),
            pltpu.SemaphoreType.DMA((13,)),
            pltpu.SemaphoreType.DMA((4,)),
            pltpu.SemaphoreType.DMA((13,)),
            pltpu.SemaphoreType.DMA((16,)),
        ],
        compiler_params=params,
    )(place, values.astype(jnp.int32), values, *envs, across2b, ket_mps[:, 0], bra_own, rim0, rim1, rim2)
    mine, left, right, far = sums[:4], sums[4:8], sums[8:12], sums[12:]

    def added(*parts):
        return functools.reduce(jnp.add, [part.astype(F32) for part in parts])

    def moved(value, move, owner, i):
        return sent(value, move, owner, {n for n in range(ROWS) if COUNT[n] > i})

    far_up, far_down, from_left, from_right = {}, {}, {}, {}
    gate = ()
    above = []
    for i in (0, 2):
        far_up[i] = moved(after(far[i], *gate), x_up, x_far, i)
        far_down[i + 1] = moved(after(far[i + 1], *gate), x_down, x_far, i + 1)
        from_left[i + 1] = moved(after(right[i + 1], *gate), x_up, x_up, i + 1)
        from_right[i] = moved(after(left[i], *gate), x_down, x_down, i)
        from_left[i] = moved(added(right[i], far_up[i]).astype(BF), x_up, x_up, i)
        from_right[i + 1] = moved(added(left[i + 1], far_down[i + 1]).astype(BF), x_down, x_down, i + 1)
        gate = (far_up[i], far_down[i + 1])
        raised = [added(mine[n][1], from_left[n][1], from_right[n][1]).astype(BF) for n in (i, i + 1)]
        pairs = [(a * ROWS + n, (a + 1) * ROWS + n) for a in range(SECS - 1) for n in range(ROWS) if COUNT[n] > i]
        above.append(lax.ppermute(jnp.stack(raised), ("sec", "row"), pairs))
    here = [added(mine[n][0], from_left[n][0], from_right[n][0]) for n in range(4)]

    out = pl.pallas_call(
        unpack_kernel,
        in_specs=[smem] * 3 + [vmem] * 6,
        out_specs=vmem,
        out_shape=shape((4, BB, KB), BF),
        compiler_params=params,
    )(place, ket_flat, bra_flat, *here, *above)
    return out.reshape(CH, 1, 2, BB, KB)


def solution(mesh):
    placed = (
        P("row", "sec", None, None, None),
        P(None, "sec", None, None, None),
        P(None, "sec", None, None, None),
        P(),
        P(),
        P("row", None, None),
        P("row", None),
    )
    return jax.shard_map(
        body,
        mesh=mesh,
        in_specs=placed,
        out_specs=P("row", "sec", None, None, None),
        check_vma=False,
    )
```

```python
import functools

import jax
import jax.numpy as jnp
from jax import lax
from jax.experimental import pallas as pl
from jax.experimental.pallas import tpu as pltpu
from jax.sharding import PartitionSpec as P

EPW, CH = 8, 2
NZ, NX = 4, 4
SECS, ROWS = 16, 16
BB, KB = 256, 512
QUARTER = BB // NX
TOGETHER = 2
BF, F32 = jnp.bfloat16, jnp.float32
STEPS = (0, -1, 1, 2)
VMEM_BYTES = 56 * 1024 * 1024
HEAD = 16
BRA_CELLS = ((0, 0), (0, 1), (2, 1), (1, 0), (1, 1), (3, 1))
CELLS = [(b, j) for b in range(2) for j in range(CH)]


def after(value, *others):
    return lax.optimization_barrier((value, *others))[0] if others else value


def charge(channel):
    klass = channel % 9
    return klass % 3 - 1, klass // 3 - 1


def live_at(r, b, j):
    to_b = b + charge(CH * r + j)[1]
    return jnp.where((to_b >= 0) & (to_b < 2), 1, 0)


COUNT = [sum(0 <= b + charge(CH * r + j)[1] < 2 for b, j in CELLS) for r in range(ROWS)]


def row_z(r, d):
    return (r // NX + d) % NZ * NX + r % NX


def row_x(r, d):
    return r // NX * NX + (r % NX + d) % NX


def packed_cells(r, a, ket_sizes, bra_sizes):
    places = [(jnp.int32(0), jnp.int32(0), jnp.int32(0)) for _ in range(4)]
    count = jnp.int32(0)
    for b, j in CELLS:
        out_a, out_b = charge(CH * r + j)
        live = live_at(r, b, j)
        at_a, at_b = a + out_a, jnp.clip(b + out_b, 0, 1)
        rows = jnp.where((at_a >= 0) & (at_a < SECS), bra_sizes[at_b, jnp.clip(at_a, 0, SECS - 1)], 0)
        cols = ket_sizes[b, a]
        for i in range(4):
            hit = (live == 1) & (count == i)
            places[i] = tuple(jnp.where(hit, new, old) for new, old in zip((2 * j + b, rows, cols), places[i]))
        count = count + live
    return places, count


def live_count(r):
    return sum(live_at(r, b, j) for b, j in CELLS)


def keep(rows, cols):
    row_at = lax.broadcasted_iota(jnp.int32, (BB, KB), 0)
    col_at = lax.broadcasted_iota(jnp.int32, (BB, KB), 1)
    return (row_at < rows) & (col_at < cols)


def prepare_kernel(place, ket_sizes, bra_sizes, entries, coeffs, env, first_out, second_out, third_out, moving):
    r, a = place[0], place[1]
    lane = lax.broadcasted_iota(jnp.int32, (HEAD, KB), 1)
    slot, field = lane // 8, lane % 8
    places, count = packed_cells(r, a, ket_sizes, bra_sizes)
    for i, (cell, rows, cols) in enumerate(places):
        target = (first_out, second_out, third_out, moving)[i]
        j, b = cell // 2, cell % 2
        head = jnp.zeros((HEAD, KB), F32)
        for n in range(EPW):
            part = jnp.where(field < 3, 0.0, coeffs[j, n])
            for f in range(3):
                part = jnp.where(field == f, entries[f, j, n].astype(F32), part)
            part = jnp.where(field == 7, (b + 1).astype(F32), part)
            head = jnp.where(slot == n, part, head)
        first = head.astype(BF).astype(F32)
        second = (head - first).astype(BF).astype(F32)
        last = head - first - second
        head = jnp.where(field == 4, second, jnp.where(field == 5, last, first))
        head = jnp.where(i < count, head, 0.0)
        target[:HEAD] = head.astype(BF)
        target[HEAD:] = jnp.where(keep(rows, cols), env[cell], jnp.zeros((BB, KB), BF))


def bra_kernel(place, bra, flipped, strip, strip_low, strip_high):
    r = place[0]
    lines = pl.ds(pl.multiple_of(r % NX * QUARTER, QUARTER), QUARTER)
    for n, (sp, to_b) in enumerate(BRA_CELLS):
        flipped[n] = bra[sp, to_b].T
        value = flipped[n, lines]
        strip[n] = value
        if n < 3:
            strip_low[n] = value
        else:
            strip_high[n - 3] = value


def unpack_kernel(place, ket_sizes, bra_sizes, *refs):
    here, above, out = refs[:4], refs[4:6], refs[6]
    out[...] = jnp.zeros_like(out)
    for i, (cell, rows, cols) in enumerate(packed_cells(place[0], place[1], ket_sizes, bra_sizes)[0]):

        @pl.when(rows > 0)
        def _(i=i, cell=cell, rows=rows, cols=cols):
            value = here[i][...] + above[i // 2][i % 2].astype(F32)
            out[cell] = jnp.where(keep(rows, cols), value, 0.0).astype(BF)


def terms_kernel(place, ints, values, *refs):
    envs, across2b, ket_in, bra_own, rim0, rim1, rim2 = refs[:12], *refs[12:18]
    outs = refs[18:34]
    env_all, ket, bra_all, total, rounded, todo, scale, size, env_sem, ket_sem, bra_sem, out_sem = refs[34:]
    x = place[0] % NX
    copies = []
    for n in range(12):
        rows = BB if n < 11 else BB // 2
        copies.append(pltpu.make_async_copy(envs[n].at[pl.ds(HEAD, rows)], env_all.at[n, pl.ds(0, rows)], env_sem.at[n]))
    copies.append(pltpu.make_async_copy(across2b, env_all.at[11, pl.ds(BB // 2, BB // 2)], env_sem.at[12]))
    copies += [pltpu.make_async_copy(ket_in.at[s], ket.at[pl.ds(2 * s, 2)], ket_sem.at[s]) for s in range(4)]
    copies.append(pltpu.make_async_copy(bra_own, bra_all.at[pl.ds(6, 6)], bra_sem.at[0]))
    y = NX - 1 - x
    for n, (ref, at, owner) in enumerate(((rim0, 0, x), (rim1, 0, x + 1 - 2 * (x % 2)), (rim2, 0, y), (rim2, 12, y + 1 - 2 * (y % 2)))):
        lines = pl.ds(pl.multiple_of(QUARTER * owner, QUARTER), QUARTER)
        for m, (first, count, to) in enumerate(((0, 3, 0), (3, 6, 12), (9, 3, 21))):
            copies.append(pltpu.make_async_copy(
                ref.at[pl.ds(at + first, count)], bra_all.at[pl.ds(to, count), lines], bra_sem.at[1 + 3 * n + m]
            ))
    for copy in copies:
        copy.start()

    r, a = place[0], place[1]
    my_z, my_x = r // NX, r % NX
    for d in range(4):
        for i in range(4):

            @pl.when(i < live_count(row_x(r, STEPS[d])))
            def _(at=8 * d + 2 * i):
                total[at] = jnp.zeros((BB, KB), F32)
                total[at + 1] = jnp.zeros((BB, KB), F32)

    size[0] = 0

    @pl.loop(0, 12 * EPW)
    def _(item):
        base = 64 * (item // EPW) + 8 * (item % EPW)
        out_w, s, code = ints[base], ints[base + 2], ints[base + 7]
        q_b = code - 1
        p_b, s_a = q_b + s // 2, s % 2

        @pl.when((code > 0) & (out_w // (CH * NX) == my_z) & (p_b < 2) & (a + s_a < SECS))
        def _():
            out_r, out_j = out_w // CH, out_w % CH

            @pl.when(live_at(out_r, p_b, out_j) == 1)
            def _():
                sp, at = ints[base + 1], size[0]
                forward = (out_r % NX - my_x + NX) % NX
                slot = jnp.where(forward == 1, 2, jnp.where(forward == 3, 1, jnp.where(forward == 2, 3, 0)))
                out_a, out_b = charge(out_w)
                low = live_at(out_r, 0, 0)
                inside = low + live_at(out_r, 0, 1) + out_j * live_at(out_r, 1, 0)
                position = jnp.where(p_b == 0, out_j * low, inside)
                todo[4 * at] = item // EPW
                todo[4 * at + 1] = 2 * s + q_b
                todo[4 * at + 2] = 6 * (s_a + out_a + 1) + 3 * (sp % 2) + p_b + out_b + sp // 2
                todo[4 * at + 3] = 8 * slot + 2 * position + s_a
                scale[at] = values[base + 3] + values[base + 4] + values[base + 5]
                size[0] = at + 1

    count = size[0]
    for n in range(TOGETHER - 1):
        for field in range(3):
            todo[4 * (count + n) + field] = 0
        todo[4 * (count + n) + 3] = 32
        scale[count + n] = 0.0

    for copy in copies:
        copy.wait()

    @pl.loop(0, (count + TOGETHER - 1) // TOGETHER)
    def _(step):
        places = [step * TOGETHER + n for n in range(TOGETHER)]
        halves = [
            jnp.dot(env_all[todo[4 * n]], ket[todo[4 * n + 1]], preferred_element_type=F32).astype(BF) for n in places
        ]
        terms = [
            jnp.dot(bra_all[todo[4 * n + 2]], half, preferred_element_type=F32) for n, half in zip(places, halves)
        ]
        for n, term in zip(places, terms):
            at = todo[4 * n + 3]
            total[at] = total[at] + scale[n] * term

    def stored(d, i):
        return pltpu.make_async_copy(rounded.at[4 * d + i], outs[4 * d + i], out_sem.at[4 * d + i])

    for d in (3, 2, 1, 0):
        for i in range(4):

            @pl.when(i < live_count(row_x(r, STEPS[d])))
            def _(d=d, i=i):
                for up in range(2):
                    rounded[4 * d + i, up] = total[8 * d + 2 * i + up].astype(BF)
                stored(d, i).start()

    for d in (3, 2, 1, 0):
        for i in range(4):

            @pl.when(i < live_count(row_x(r, STEPS[d])))
            def _(d=d, i=i):
                stored(d, i).wait()


def body(env_in, ket_mps, bra_mps, ket_sizes, bra_sizes, entries, coeffs):
    my_a = lax.axis_index("sec")
    r = lax.axis_index("row")
    place = jnp.stack([r, my_a])
    ket_flat, bra_flat = ket_sizes.T, bra_sizes.T

    smem = pl.BlockSpec(memory_space=pltpu.SMEM)
    vmem = pl.BlockSpec(memory_space=pltpu.VMEM)
    shape = jax.ShapeDtypeStruct
    pair = shape((2, BB, KB), BF)
    params = pltpu.CompilerParams(vmem_limit_bytes=VMEM_BYTES)
    payload = shape((HEAD + BB, KB), BF)
    own0, own1, own2, moving = pl.pallas_call(
        prepare_kernel,
        in_specs=[smem] * 5 + [vmem],
        out_specs=[vmem] * 4,
        out_shape=[payload] * 4,
        compiler_params=params,
    )(place, ket_flat, bra_flat, entries.transpose(2, 0, 1), coeffs, env_in.reshape(4, BB, KB))

    same = lambda n: n
    z_up, z_down = (lambda n: row_z(n, 1)), (lambda n: row_z(n, -1))
    x_up, x_down, x_far = (lambda n: row_x(n, 1)), (lambda n: row_x(n, -1)), (lambda n: row_x(n, 2))

    def sent(value, move, owner, rows):
        return lax.ppermute(value, "row", [(n, move(n)) for n in range(ROWS) if owner(n) in rows])

    everyone = set(range(ROWS))
    full = [n for n in range(ROWS) if COUNT[n] == 4]
    takers, lent = set(), []
    for n in full:
        taker = next(m for m in (row_x(n, 1), row_x(n, -1)) if COUNT[m] == 2 and m not in takers)
        takers.add(taker)
        lent.append((n, taker))
    three = {n for n in range(ROWS) if COUNT[n] > 2} | takers
    behind0 = sent(own0, z_up, same, everyone)
    ahead1 = sent(own1, z_down, same, everyone)
    borrowed = lax.ppermute(moving, "row", lent)
    own2 = own2 + borrowed
    behind1 = sent(after(own1, behind0, ahead1), z_up, same, everyone)
    ahead0 = sent(after(own0, behind0, ahead1), z_down, same, everyone)
    behind2 = sent(own2, z_up, same, three)
    ahead2 = sent(own2, z_down, same, three)
    across0 = sent(behind0, z_up, z_down, everyone)
    across1 = sent(ahead1, z_down, z_up, everyone)
    across2a = sent(behind2[: HEAD + BB // 2], z_up, z_down, three)
    across2b = sent(ahead2[HEAD + BB // 2 :], z_down, z_up, three)

    bra_in = after(bra_mps, borrowed)
    bra_own, strip, strip_low, strip_high = pl.pallas_call(
        bra_kernel,
        in_specs=[smem, vmem],
        out_specs=[vmem] * 4,
        out_shape=[
            shape((6, BB, BB), BF),
            shape((6, QUARTER, BB), BF),
            shape((3, QUARTER, BB), BF),
            shape((3, QUARTER, BB), BF),
        ],
        compiler_params=params,
    )(place, bra_in[:, 0])
    up = lambda n: [(i, i + n) for i in range(SECS - n)]
    down = lambda n: [(i + n, i) for i in range(SECS - n)]
    rim0 = jnp.concatenate([
        lax.ppermute(strip_low, "sec", up(1)),
        lax.ppermute(strip, "sec", down(1)),
        lax.ppermute(strip_high, "sec", down(2)),
    ])
    rim1 = lax.ppermute(rim0, "row", [(n, n ^ 1) for n in range(ROWS)])
    rim2 = lax.ppermute(jnp.concatenate([rim0, rim1]), "row", [(n, n ^ 3) for n in range(ROWS)])

    envs = [own0, own1, own2, behind0, behind1, behind2, ahead0, ahead1, ahead2, across0, across1, across2a]
    values = jnp.concatenate([part[0, :64] for part in envs]).astype(F32)

    hbm = pl.BlockSpec(memory_space=pl.ANY)
    sums = pl.pallas_call(
        terms_kernel,
        in_specs=[smem] * 3 + [hbm] * 18,
        out_specs=[hbm] * 16,
        out_shape=[pair] * 16,
        scratch_shapes=[
            pltpu.VMEM((12, BB, KB), BF),
            pltpu.VMEM((8, KB, KB), BF),
            pltpu.VMEM((24, BB, BB), BF),
            pltpu.VMEM((33, BB, KB), F32),
            pltpu.VMEM((16, 2, BB, KB), BF),
            pltpu.SMEM((4 * (12 * EPW + TOGETHER),), jnp.int32),
            pltpu.SMEM((12 * EPW + TOGETHER,), F32),
            pltpu.SMEM((1,), jnp.int32),
            pltpu.SemaphoreType.DMA((13,)),
            pltpu.SemaphoreType.DMA((4,)),
            pltpu.SemaphoreType.DMA((13,)),
            pltpu.SemaphoreType.DMA((16,)),
        ],
        compiler_params=params,
    )(place, values.astype(jnp.int32), values, *envs, across2b, ket_mps[:, 0], bra_own, rim0, rim1, rim2)
    mine, left, right, far = sums[:4], sums[4:8], sums[8:12], sums[12:]

    def added(*parts):
        return functools.reduce(jnp.add, [part.astype(F32) for part in parts])

    def moved(value, move, owner, i):
        return sent(value, move, owner, {n for n in range(ROWS) if COUNT[n] > i})

    far_up, far_down, from_left, from_right = {}, {}, {}, {}
    gate = ()
    above = []
    for i in (0, 2):
        far_up[i] = moved(after(far[i], *gate), x_up, x_far, i)
        far_down[i + 1] = moved(after(far[i + 1], *gate), x_down, x_far, i + 1)
        from_left[i + 1] = moved(after(right[i + 1], *gate), x_up, x_up, i + 1)
        from_right[i] = moved(after(left[i], *gate), x_down, x_down, i)
        from_left[i] = moved(added(right[i], far_up[i]).astype(BF), x_up, x_up, i)
        from_right[i + 1] = moved(added(left[i + 1], far_down[i + 1]).astype(BF), x_down, x_down, i + 1)
        gate = (far_up[i], far_down[i + 1])
        raised = [added(mine[n][1], from_left[n][1], from_right[n][1]).astype(BF) for n in (i, i + 1)]
        pairs = [(a * ROWS + n, (a + 1) * ROWS + n) for a in range(SECS - 1) for n in range(ROWS) if COUNT[n] > i]
        above.append(lax.ppermute(jnp.stack(raised), ("sec", "row"), pairs))
    here = [added(mine[n][0], from_left[n][0], from_right[n][0]) for n in range(4)]

    out = pl.pallas_call(
        unpack_kernel,
        in_specs=[smem] * 3 + [vmem] * 6,
        out_specs=vmem,
        out_shape=shape((4, BB, KB), BF),
        compiler_params=params,
    )(place, ket_flat, bra_flat, *here, *above)
    return out.reshape(CH, 1, 2, BB, KB)


def solution(mesh):
    placed = (
        P("row", "sec", None, None, None),
        P(None, "sec", None, None, None),
        P(None, "sec", None, None, None),
        P(),
        P(),
        P("row", None, None),
        P("row", None),
    )
    return jax.shard_map(
        body,
        mesh=mesh,
        in_specs=placed,
        out_specs=P("row", "sec", None, None, None),
        check_vma=False,
    )
```

```python
import functools

import jax
import jax.numpy as jnp
from jax import lax
from jax.experimental import pallas as pl
from jax.experimental.pallas import tpu as pltpu
from jax.sharding import PartitionSpec as P

EPW, CH = 8, 2
NZ, NX = 4, 4
SECS, ROWS = 16, 16
BB, KB = 256, 512
QUARTER = BB // NX
TOGETHER = 2
BF, F32 = jnp.bfloat16, jnp.float32
STEPS = (0, -1, 1, 2)
VMEM_BYTES = 56 * 1024 * 1024
HEAD = 16
BRA_CELLS = ((0, 0), (0, 1), (2, 1), (1, 0), (1, 1), (3, 1))
CELLS = [(b, j) for b in range(2) for j in range(CH)]


def after(value, *others):
    return lax.optimization_barrier((value, *others))[0] if others else value


def charge(channel):
    klass = channel % 9
    return klass % 3 - 1, klass // 3 - 1


def live_at(r, b, j):
    to_b = b + charge(CH * r + j)[1]
    return jnp.where((to_b >= 0) & (to_b < 2), 1, 0)


COUNT = [[sum(0 <= b + charge(CH * r + j)[1] < 2 for j in range(CH)) for r in range(ROWS)] for b in range(2)]


def row_z(r, d):
    return (r // NX + d) % NZ * NX + r % NX


def row_x(r, d):
    return r // NX * NX + (r % NX + d) % NX


def packed_cells(r, a, ket_sizes, bra_sizes):
    places = []
    for b in range(2):
        first, second = live_at(r, b, 0), live_at(r, b, 1)
        for j, live in ((1 - first, first + second > 0), (jnp.int32(1), first + second > 1)):
            out_a, out_b = charge(CH * r + j)
            at_a, at_b = a + out_a, jnp.clip(b + out_b, 0, 1)
            rows = jnp.where(live & (at_a >= 0) & (at_a < SECS), bra_sizes[at_b, jnp.clip(at_a, 0, SECS - 1)], 0)
            places.append((2 * j + b, rows, ket_sizes[b, a], live))
    return places


def live_count(r, b):
    return live_at(r, b, 0) + live_at(r, b, 1)


def keep(rows, cols):
    row_at = lax.broadcasted_iota(jnp.int32, (BB, KB), 0)
    col_at = lax.broadcasted_iota(jnp.int32, (BB, KB), 1)
    return (row_at < rows) & (col_at < cols)


def prepare_kernel(place, ket_sizes, bra_sizes, entries, coeffs, env, *outs):
    r, a = place[0], place[1]
    lane = lax.broadcasted_iota(jnp.int32, (HEAD, KB), 1)
    slot, field = lane // 8, lane % 8
    for i, (cell, rows, cols, live) in enumerate(packed_cells(r, a, ket_sizes, bra_sizes)):
        target = outs[i]
        j, b = cell // 2, cell % 2
        head = jnp.zeros((HEAD, KB), F32)
        for n in range(EPW):
            part = jnp.where(field < 3, 0.0, coeffs[j, n])
            for f in range(3):
                part = jnp.where(field == f, entries[f, j, n].astype(F32), part)
            part = jnp.where(field == 7, (b + 1).astype(F32), part)
            head = jnp.where(slot == n, part, head)
        first = head.astype(BF).astype(F32)
        second = (head - first).astype(BF).astype(F32)
        last = head - first - second
        head = jnp.where(field == 4, second, jnp.where(field == 5, last, first))
        head = jnp.where(live, head, 0.0)
        target[:HEAD] = head.astype(BF)
        target[HEAD:] = jnp.where(keep(rows, cols), env[cell], jnp.zeros((BB, KB), BF))


def bra_kernel(place, bra, flipped, strip, strip_low, strip_high):
    r = place[0]
    lines = pl.ds(pl.multiple_of(r % NX * QUARTER, QUARTER), QUARTER)
    for n, (sp, to_b) in enumerate(BRA_CELLS):
        flipped[n] = bra[sp, to_b].T
        value = flipped[n, lines]
        strip[n] = value
        if n < 3:
            strip_low[n] = value
        else:
            strip_high[n - 3] = value


def unpack_kernel(place, ket_sizes, bra_sizes, *refs):
    here, above, out = refs[:4], refs[4:6], refs[6]
    out[...] = jnp.zeros_like(out)
    for i, (cell, rows, cols, _) in enumerate(packed_cells(place[0], place[1], ket_sizes, bra_sizes)):

        @pl.when(rows > 0)
        def _(i=i, cell=cell, rows=rows, cols=cols):
            value = here[i][...] + above[i // 2][i % 2].astype(F32)
            out[cell] = jnp.where(keep(rows, cols), value, 0.0).astype(BF)


def terms_kernel(to_b, place, ints, values, *refs):
    envs = refs[: 8 * (to_b + 1)]
    ket_in, bra_own, rim0, rim1, rim2 = refs[len(envs) : len(envs) + 5]
    outs = refs[len(envs) + 5 : len(envs) + 13]
    env_all, ket, bra_all, total, rounded, todo, scale, size, env_sem, ket_sem, bra_sem, out_sem = refs[len(envs) + 13 :]
    x = place[0] % NX
    copies = [
        pltpu.make_async_copy(ref.at[pl.ds(HEAD, BB)], env_all.at[n], env_sem.at[n]) for n, ref in enumerate(envs)
    ]
    for from_b in range(to_b + 1):
        for n in range(2):
            at = 2 * from_b + n
            copies.append(pltpu.make_async_copy(ket_in.at[2 * (to_b - from_b) + n, from_b], ket.at[at], ket_sem.at[at]))
    copies.append(pltpu.make_async_copy(bra_own, bra_all.at[pl.ds(6, 6)], bra_sem.at[0]))
    y = NX - 1 - x
    for n, (ref, at, owner) in enumerate(((rim0, 0, x), (rim1, 0, x + 1 - 2 * (x % 2)), (rim2, 0, y), (rim2, 12, y + 1 - 2 * (y % 2)))):
        lines = pl.ds(pl.multiple_of(QUARTER * owner, QUARTER), QUARTER)
        for m, (first, count, to) in enumerate(((0, 3, 0), (3, 6, 12), (9, 3, 21))):
            copies.append(pltpu.make_async_copy(
                ref.at[pl.ds(at + first, count)], bra_all.at[pl.ds(to, count), lines], bra_sem.at[1 + 3 * n + m]
            ))
    for copy in copies:
        copy.start()

    r, a = place[0], place[1]
    my_z, my_x = r // NX, r % NX
    for d in range(4):
        for i in range(2):

            @pl.when(i < live_count(row_x(r, STEPS[d]), to_b))
            def _(at=4 * d + 2 * i):
                total[at] = jnp.zeros((BB, KB), F32)
                total[at + 1] = jnp.zeros((BB, KB), F32)

    size[0] = 0

    @pl.loop(0, len(envs) * EPW)
    def _(item):
        base = 64 * (item // EPW) + 8 * (item % EPW)
        out_w, s, code = ints[base], ints[base + 2], ints[base + 7]
        q_b = code - 1
        s_a = s % 2

        @pl.when((code > 0) & (out_w // (CH * NX) == my_z) & (q_b + s // 2 == to_b) & (a + s_a < SECS))
        def _():
            out_r, out_j = out_w // CH, out_w % CH

            @pl.when(live_at(out_r, to_b, out_j) == 1)
            def _():
                sp, at = ints[base + 1], size[0]
                forward = (out_r % NX - my_x + NX) % NX
                slot = jnp.where(forward == 1, 2, jnp.where(forward == 3, 1, jnp.where(forward == 2, 3, 0)))
                out_a, out_b = charge(out_w)
                todo[4 * at] = item // EPW
                todo[4 * at + 1] = 2 * q_b + s_a
                todo[4 * at + 2] = 6 * (s_a + out_a + 1) + 3 * (sp % 2) + to_b + out_b + sp // 2
                todo[4 * at + 3] = 4 * slot + 2 * out_j * live_at(out_r, to_b, 0) + s_a
                scale[at] = values[base + 3] + values[base + 4] + values[base + 5]
                size[0] = at + 1

    count = size[0]
    for n in range(TOGETHER - 1):
        for field in range(3):
            todo[4 * (count + n) + field] = 0
        todo[4 * (count + n) + 3] = 16
        scale[count + n] = 0.0

    for copy in copies:
        copy.wait()

    @pl.loop(0, (count + TOGETHER - 1) // TOGETHER)
    def _(step):
        places = [step * TOGETHER + n for n in range(TOGETHER)]
        halves = [
            jnp.dot(env_all[todo[4 * n]], ket[todo[4 * n + 1]], preferred_element_type=F32).astype(BF) for n in places
        ]
        terms = [
            jnp.dot(bra_all[todo[4 * n + 2]], half, preferred_element_type=F32) for n, half in zip(places, halves)
        ]
        for n, term in zip(places, terms):
            at = todo[4 * n + 3]
            total[at] = total[at] + scale[n] * term

    def stored(d, i):
        return pltpu.make_async_copy(rounded.at[2 * d + i], outs[2 * d + i], out_sem.at[2 * d + i])

    for d in (3, 2, 1, 0):
        for i in range(2):

            @pl.when(i < live_count(row_x(r, STEPS[d]), to_b))
            def _(d=d, i=i):
                for up in range(2):
                    rounded[2 * d + i, up] = total[4 * d + 2 * i + up].astype(BF)
                stored(d, i).start()

    for d in (3, 2, 1, 0):
        for i in range(2):

            @pl.when(i < live_count(row_x(r, STEPS[d]), to_b))
            def _(d=d, i=i):
                stored(d, i).wait()


def body(env_in, ket_mps, bra_mps, ket_sizes, bra_sizes, entries, coeffs):
    my_a = lax.axis_index("sec")
    r = lax.axis_index("row")
    place = jnp.stack([r, my_a])
    ket_flat, bra_flat = ket_sizes.T, bra_sizes.T

    smem = pl.BlockSpec(memory_space=pltpu.SMEM)
    vmem = pl.BlockSpec(memory_space=pltpu.VMEM)
    shape = jax.ShapeDtypeStruct
    pair = shape((2, BB, KB), BF)
    params = pltpu.CompilerParams(vmem_limit_bytes=VMEM_BYTES)
    payload = shape((HEAD + BB, KB), BF)
    packed = pl.pallas_call(
        prepare_kernel,
        in_specs=[smem] * 5 + [vmem],
        out_specs=[vmem] * 4,
        out_shape=[payload] * 4,
        compiler_params=params,
    )(place, ket_flat, bra_flat, entries.transpose(2, 0, 1), coeffs, env_in.reshape(4, BB, KB))

    same = lambda n: n
    z_up, z_down = (lambda n: row_z(n, 1)), (lambda n: row_z(n, -1))
    x_up, x_down, x_far = (lambda n: row_x(n, 1)), (lambda n: row_x(n, -1)), (lambda n: row_x(n, 2))

    def sent(value, move, owner, b, i):
        return lax.ppermute(value, "row", [(n, move(n)) for n in range(ROWS) if COUNT[b][owner(n)] > i])

    def gathered(b, *gates):
        gate, late = gates if gates else ((), ())
        own0, own1 = packed[2 * b : 2 * b + 2]
        behind0 = sent(after(own0, *gate), z_up, same, b, 0)
        ahead1 = sent(after(own1, *gate), z_down, same, b, 1)
        behind1 = sent(after(own1, *late), z_up, same, b, 1)
        ahead0 = sent(after(own0, *late), z_down, same, b, 0)
        across0 = sent(behind0, z_up, z_down, b, 0)
        across1 = sent(ahead1, z_down, z_up, b, 1)
        return [own0, own1, behind0, behind1, ahead0, ahead1, across0, across1]

    low = gathered(0)

    bra_own, strip, strip_low, strip_high = pl.pallas_call(
        bra_kernel,
        in_specs=[smem, vmem],
        out_specs=[vmem] * 4,
        out_shape=[
            shape((6, BB, BB), BF),
            shape((6, QUARTER, BB), BF),
            shape((3, QUARTER, BB), BF),
            shape((3, QUARTER, BB), BF),
        ],
        compiler_params=params,
    )(place, after(bra_mps, packed[0])[:, 0])
    up = lambda n: [(i, i + n) for i in range(SECS - n)]
    down = lambda n: [(i + n, i) for i in range(SECS - n)]
    rim0 = jnp.concatenate([
        lax.ppermute(strip_low, "sec", up(1)),
        lax.ppermute(strip, "sec", down(1)),
        lax.ppermute(strip_high, "sec", down(2)),
    ])
    rim1 = lax.ppermute(rim0, "row", [(n, n ^ 1) for n in range(ROWS)])
    rim2 = lax.ppermute(jnp.concatenate([rim0, rim1]), "row", [(n, n ^ 3) for n in range(ROWS)])

    hbm = pl.BlockSpec(memory_space=pl.ANY)

    def terms(b, envs):
        values = jnp.concatenate([part[0, :64] for part in envs]).astype(F32)
        return pl.pallas_call(
            functools.partial(terms_kernel, b),
            in_specs=[smem] * 3 + [hbm] * (len(envs) + 5),
            out_specs=[hbm] * 8,
            out_shape=[pair] * 8,
            scratch_shapes=[
                pltpu.VMEM((len(envs), BB, KB), BF),
                pltpu.VMEM((4, KB, KB), BF),
                pltpu.VMEM((24, BB, BB), BF),
                pltpu.VMEM((17, BB, KB), F32),
                pltpu.VMEM((8, 2, BB, KB), BF),
                pltpu.SMEM((4 * (len(envs) * EPW + TOGETHER),), jnp.int32),
                pltpu.SMEM((len(envs) * EPW + TOGETHER,), F32),
                pltpu.SMEM((1,), jnp.int32),
                pltpu.SemaphoreType.DMA((len(envs),)),
                pltpu.SemaphoreType.DMA((4,)),
                pltpu.SemaphoreType.DMA((13,)),
                pltpu.SemaphoreType.DMA((8,)),
            ],
            compiler_params=params,
        )(place, values.astype(jnp.int32), values, *envs, ket_mps[:, 0], bra_own, rim0, rim1, rim2)

    def added(*parts):
        return functools.reduce(jnp.add, [part.astype(F32) for part in parts])

    def reduced(b, sums):
        mine, left, right, far = (sums[2 * d : 2 * d + 2] for d in range(4))
        far_up = sent(far[0], x_up, x_far, b, 0)
        far_down = sent(far[1], x_down, x_far, b, 1)
        from_left = [None, sent(right[1], x_up, x_up, b, 1)]
        from_right = [sent(left[0], x_down, x_down, b, 0), None]
        from_left[0] = sent(added(right[0], far_up).astype(BF), x_up, x_up, b, 0)
        from_right[1] = sent(added(left[1], far_down).astype(BF), x_down, x_down, b, 1)
        raised = [added(mine[n][1], from_left[n][1], from_right[n][1]).astype(BF) for n in range(2)]
        pairs = [(a * ROWS + n, (a + 1) * ROWS + n) for a in range(SECS - 1) for n in range(ROWS) if COUNT[b][n]]
        above = lax.ppermute(jnp.stack(raised), ("sec", "row"), pairs)
        here = [added(mine[n][0], from_left[n][0], from_right[n][0]) for n in range(2)]
        return here, above, from_left + from_right

    sums0 = terms(0, low)
    high = gathered(1, [low[3], low[4]], sums0[6:])
    here0, above0, arrived = reduced(0, sums0)
    low[0] = after(low[0], *arrived)
    here1, above1, _ = reduced(1, terms(1, low + high))
    here, above = here0 + here1, [above0, above1]

    out = pl.pallas_call(
        unpack_kernel,
        in_specs=[smem] * 3 + [vmem] * 6,
        out_specs=vmem,
        out_shape=shape((4, BB, KB), BF),
        compiler_params=params,
    )(place, ket_flat, bra_flat, *here, *above)
    return out.reshape(CH, 1, 2, BB, KB)


def solution(mesh):
    placed = (
        P("row", "sec", None, None, None),
        P(None, "sec", None, None, None),
        P(None, "sec", None, None, None),
        P(),
        P(),
        P("row", None, None),
        P("row", None),
    )
    return jax.shard_map(
        body,
        mesh=mesh,
        in_specs=placed,
        out_specs=P("row", "sec", None, None, None),
        check_vma=False,
    )
```

```python
import functools

import jax
import jax.numpy as jnp
from jax import lax
from jax.experimental import pallas as pl
from jax.experimental.pallas import tpu as pltpu
from jax.sharding import PartitionSpec as P

EPW, CH = 8, 2
NZ, NX = 4, 4
SECS, ROWS = 16, 16
BB, KB = 256, 512
QUARTER = BB // NX
TOGETHER = 2
BF, F32 = jnp.bfloat16, jnp.float32
STEPS = (0, -1, 1, 2)
VMEM_BYTES = 56 * 1024 * 1024
HEAD = 16
BRA_CELLS = ((0, 0), (0, 1), (2, 1), (1, 0), (1, 1), (3, 1))
CELLS = [(b, j) for b in range(2) for j in range(CH)]


def after(value, *others):
    return lax.optimization_barrier((value, *others))[0] if others else value


def charge(channel):
    klass = channel % 9
    return klass % 3 - 1, klass // 3 - 1


def live_at(r, b, j):
    to_b = b + charge(CH * r + j)[1]
    return jnp.where((to_b >= 0) & (to_b < 2), 1, 0)


COUNT = [sum(0 <= b + charge(CH * r + j)[1] < 2 for b, j in CELLS) for r in range(ROWS)]


def row_z(r, d):
    return (r // NX + d) % NZ * NX + r % NX


def row_x(r, d):
    return r // NX * NX + (r % NX + d) % NX


def packed_cells(r, a, ket_sizes, bra_sizes):
    places = [(jnp.int32(0), jnp.int32(0), jnp.int32(0)) for _ in range(4)]
    count = jnp.int32(0)
    for b, j in CELLS:
        out_a, out_b = charge(CH * r + j)
        live = live_at(r, b, j)
        at_a, at_b = a + out_a, jnp.clip(b + out_b, 0, 1)
        rows = jnp.where((at_a >= 0) & (at_a < SECS), bra_sizes[at_b, jnp.clip(at_a, 0, SECS - 1)], 0)
        cols = ket_sizes[b, a]
        for i in range(4):
            hit = (live == 1) & (count == i)
            places[i] = tuple(jnp.where(hit, new, old) for new, old in zip((2 * j + b, rows, cols), places[i]))
        count = count + live
    return places, count


def live_count(r):
    return sum(live_at(r, b, j) for b, j in CELLS)


def keep(rows, cols):
    row_at = lax.broadcasted_iota(jnp.int32, (BB, KB), 0)
    col_at = lax.broadcasted_iota(jnp.int32, (BB, KB), 1)
    return (row_at < rows) & (col_at < cols)


def prepare_kernel(place, ket_sizes, bra_sizes, entries, coeffs, env, pair_out, third_out, moving):
    r, a = place[0], place[1]
    lane = lax.broadcasted_iota(jnp.int32, (HEAD, KB), 1)
    slot, field = lane // 8, lane % 8
    places, count = packed_cells(r, a, ket_sizes, bra_sizes)
    for i, (cell, rows, cols) in enumerate(places):
        target = (pair_out.at[0], pair_out.at[1], third_out, moving)[i]
        j, b = cell // 2, cell % 2
        head = jnp.zeros((HEAD, KB), F32)
        for n in range(EPW):
            part = jnp.where(field < 3, 0.0, coeffs[j, n])
            for f in range(3):
                part = jnp.where(field == f, entries[f, j, n].astype(F32), part)
            part = jnp.where(field == 7, (b + 1).astype(F32), part)
            head = jnp.where(slot == n, part, head)
        first = head.astype(BF).astype(F32)
        second = (head - first).astype(BF).astype(F32)
        last = head - first - second
        head = jnp.where(field == 4, second, jnp.where(field == 5, last, first))
        head = jnp.where(i < count, head, 0.0)
        target[:HEAD] = head.astype(BF)
        target[HEAD:] = jnp.where(keep(rows, cols), env[cell], jnp.zeros((BB, KB), BF))


def bra_kernel(place, bra, flipped, strip, strip_low, strip_high):
    r = place[0]
    lines = pl.ds(pl.multiple_of(r % NX * QUARTER, QUARTER), QUARTER)
    for n, (sp, to_b) in enumerate(BRA_CELLS):
        flipped[n] = bra[sp, to_b].T
        value = flipped[n, lines]
        strip[n] = value
        if n < 3:
            strip_low[n] = value
        else:
            strip_high[n - 3] = value


def unpack_kernel(place, ket_sizes, bra_sizes, *refs):
    here, above, out = refs[:4], refs[4:6], refs[6]
    out[...] = jnp.zeros_like(out)
    for i, (cell, rows, cols) in enumerate(packed_cells(place[0], place[1], ket_sizes, bra_sizes)[0]):

        @pl.when(rows > 0)
        def _(i=i, cell=cell, rows=rows, cols=cols):
            value = here[i][...] + above[i // 2][i % 2].astype(F32)
            out[cell] = jnp.where(keep(rows, cols), value, 0.0).astype(BF)


def terms_kernel(place, ints, values, *refs):
    two, three, lone = (refs[0], refs[2], refs[4]), (refs[1], refs[3], refs[5]), refs[6:9]
    across2b, ket_in, bra_own, rim = refs[9:13]
    outs = refs[13:29]
    env_all, ket, bra_all, total, rounded, todo, scale, size, env_sem, ket_sem, bra_sem, out_sem = refs[29:]
    copies = []
    body_rows = pl.ds(HEAD, BB)
    views = []
    for first, third in zip(two, three):
        views += [first.at[0, body_rows], first.at[1, body_rows], third.at[body_rows]]
    views += [lone[0].at[body_rows], lone[1].at[body_rows]]
    copies += [pltpu.make_async_copy(view, env_all.at[n], env_sem.at[n]) for n, view in enumerate(views)]
    half_rows = pl.ds(0, BB // 2)
    copies.append(pltpu.make_async_copy(lone[2].at[pl.ds(HEAD, BB // 2)], env_all.at[11, half_rows], env_sem.at[11]))
    copies.append(pltpu.make_async_copy(across2b, env_all.at[11, pl.ds(BB // 2, BB // 2)], env_sem.at[12]))
    copies += [pltpu.make_async_copy(ket_in.at[s], ket.at[pl.ds(2 * s, 2)], ket_sem.at[s]) for s in range(4)]
    copies.append(pltpu.make_async_copy(bra_own, bra_all.at[pl.ds(6, 6)], bra_sem.at[0]))
    for n in range(NX):
        lines = pl.ds(QUARTER * n, QUARTER)
        for m, (first, count, to) in enumerate(((0, 3, 0), (3, 6, 12), (9, 3, 21))):
            copies.append(pltpu.make_async_copy(
                rim.at[n, pl.ds(first, count)], bra_all.at[pl.ds(to, count), lines], bra_sem.at[1 + 3 * n + m]
            ))
    for copy in copies:
        copy.start()

    r, a = place[0], place[1]
    my_z, my_x = r // NX, r % NX
    for d in range(4):
        for i in range(4):

            @pl.when(i < live_count(row_x(r, STEPS[d])))
            def _(at=8 * d + 2 * i):
                total[at] = jnp.zeros((BB, KB), F32)
                total[at + 1] = jnp.zeros((BB, KB), F32)

    size[0] = 0

    @pl.loop(0, 12 * EPW)
    def _(item):
        base = 64 * (item // EPW) + 8 * (item % EPW)
        out_w, s, code = ints[base], ints[base + 2], ints[base + 7]
        q_b = code - 1
        p_b, s_a = q_b + s // 2, s % 2

        @pl.when((code > 0) & (out_w // (CH * NX) == my_z) & (p_b < 2) & (a + s_a < SECS))
        def _():
            out_r, out_j = out_w // CH, out_w % CH

            @pl.when(live_at(out_r, p_b, out_j) == 1)
            def _():
                sp, at = ints[base + 1], size[0]
                forward = (out_r % NX - my_x + NX) % NX
                slot = jnp.where(forward == 1, 2, jnp.where(forward == 3, 1, jnp.where(forward == 2, 3, 0)))
                out_a, out_b = charge(out_w)
                low = live_at(out_r, 0, 0)
                inside = low + live_at(out_r, 0, 1) + out_j * live_at(out_r, 1, 0)
                position = jnp.where(p_b == 0, out_j * low, inside)
                todo[4 * at] = item // EPW
                todo[4 * at + 1] = 2 * s + q_b
                todo[4 * at + 2] = 6 * (s_a + out_a + 1) + 3 * (sp % 2) + p_b + out_b + sp // 2
                todo[4 * at + 3] = 8 * slot + 2 * position + s_a
                scale[at] = values[base + 3] + values[base + 4] + values[base + 5]
                size[0] = at + 1

    count = size[0]
    for n in range(TOGETHER - 1):
        for field in range(3):
            todo[4 * (count + n) + field] = 0
        todo[4 * (count + n) + 3] = 32
        scale[count + n] = 0.0

    for copy in copies:
        copy.wait()

    @pl.loop(0, (count + TOGETHER - 1) // TOGETHER)
    def _(step):
        places = [step * TOGETHER + n for n in range(TOGETHER)]
        halves = [
            jnp.dot(env_all[todo[4 * n]], ket[todo[4 * n + 1]], preferred_element_type=F32).astype(BF) for n in places
        ]
        terms = [
            jnp.dot(bra_all[todo[4 * n + 2]], half, preferred_element_type=F32) for n, half in zip(places, halves)
        ]
        for n, term in zip(places, terms):
            at = todo[4 * n + 3]
            total[at] = total[at] + scale[n] * term

    def stored(d, i):
        return pltpu.make_async_copy(rounded.at[4 * d + i], outs[4 * d + i], out_sem.at[4 * d + i])

    for d in (3, 2, 1, 0):
        for i in range(4):

            @pl.when(i < live_count(row_x(r, STEPS[d])))
            def _(d=d, i=i):
                for up in range(2):
                    rounded[4 * d + i, up] = total[8 * d + 2 * i + up].astype(BF)
                stored(d, i).start()

    for d in (3, 2, 1, 0):
        for i in range(4):

            @pl.when(i < live_count(row_x(r, STEPS[d])))
            def _(d=d, i=i):
                stored(d, i).wait()


def body(env_in, ket_mps, bra_mps, ket_sizes, bra_sizes, entries, coeffs):
    my_a = lax.axis_index("sec")
    r = lax.axis_index("row")
    place = jnp.stack([r, my_a])
    ket_flat, bra_flat = ket_sizes.T, bra_sizes.T

    smem = pl.BlockSpec(memory_space=pltpu.SMEM)
    vmem = pl.BlockSpec(memory_space=pltpu.VMEM)
    shape = jax.ShapeDtypeStruct
    pair = shape((2, BB, KB), BF)
    params = pltpu.CompilerParams(vmem_limit_bytes=VMEM_BYTES)
    payload = shape((HEAD + BB, KB), BF)
    own01, own2, moving = pl.pallas_call(
        prepare_kernel,
        in_specs=[smem] * 5 + [vmem],
        out_specs=[vmem] * 3,
        out_shape=[shape((2, HEAD + BB, KB), BF), payload, payload],
        compiler_params=params,
    )(place, ket_flat, bra_flat, entries.transpose(2, 0, 1), coeffs, env_in.reshape(4, BB, KB))

    same = lambda n: n
    z_up, z_down = (lambda n: row_z(n, 1)), (lambda n: row_z(n, -1))
    x_up, x_down, x_far = (lambda n: row_x(n, 1)), (lambda n: row_x(n, -1)), (lambda n: row_x(n, 2))

    def sent(value, move, owner, rows):
        return lax.ppermute(value, "row", [(n, move(n)) for n in range(ROWS) if owner(n) in rows])

    everyone = set(range(ROWS))
    full = [n for n in range(ROWS) if COUNT[n] == 4]
    takers, lent = set(), []
    for n in full:
        taker = next(m for m in (row_x(n, 1), row_x(n, -1)) if COUNT[m] == 2 and m not in takers)
        takers.add(taker)
        lent.append((n, taker))
    three = {n for n in range(ROWS) if COUNT[n] > 2} | takers
    behind01 = sent(own01, z_up, same, everyone)
    ahead01 = sent(own01, z_down, same, everyone)

    bra_own, strip, strip_low, strip_high = pl.pallas_call(
        bra_kernel,
        in_specs=[smem, vmem],
        out_specs=[vmem] * 4,
        out_shape=[
            shape((6, BB, BB), BF),
            shape((6, QUARTER, BB), BF),
            shape((3, QUARTER, BB), BF),
            shape((3, QUARTER, BB), BF),
        ],
        compiler_params=params,
    )(place, after(bra_mps, own01)[:, 0])
    up = lambda n: [(i, i + n) for i in range(SECS - n)]
    down = lambda n: [(i + n, i) for i in range(SECS - n)]
    rim_low = lax.ppermute(strip_low, "sec", up(1))
    borrowed = lax.ppermute(after(moving, rim_low), "row", lent)
    own2 = own2 + borrowed
    behind2 = sent(own2, z_up, same, three)
    ahead2 = sent(own2, z_down, same, three)
    across0 = sent(behind01[0], z_up, z_down, everyone)
    across1 = sent(ahead01[1], z_down, z_up, everyone)
    across2a = sent(behind2[: HEAD + BB // 2], z_up, z_down, three)
    across2b = sent(ahead2[HEAD + BB // 2 :], z_down, z_up, three)
    rim = jnp.concatenate([
        rim_low,
        lax.ppermute(strip, "sec", down(1)),
        lax.ppermute(strip_high, "sec", down(2)),
    ])
    bra_rim = lax.all_gather(rim, "row", axis_index_groups=[[NX * z + x for x in range(NX)] for z in range(NZ)])

    heads = [own01[0], own01[1], own2, behind01[0], behind01[1], behind2, ahead01[0], ahead01[1], ahead2,
             across0, across1, across2a]
    values = jnp.concatenate([head[0, :64] for head in heads]).astype(F32)

    hbm = pl.BlockSpec(memory_space=pl.ANY)
    sums = pl.pallas_call(
        terms_kernel,
        in_specs=[smem] * 3 + [hbm] * 13,
        out_specs=[hbm] * 16,
        out_shape=[pair] * 16,
        scratch_shapes=[
            pltpu.VMEM((12, BB, KB), BF),
            pltpu.VMEM((8, KB, KB), BF),
            pltpu.VMEM((24, BB, BB), BF),
            pltpu.VMEM((33, BB, KB), F32),
            pltpu.VMEM((16, 2, BB, KB), BF),
            pltpu.SMEM((4 * (12 * EPW + TOGETHER),), jnp.int32),
            pltpu.SMEM((12 * EPW + TOGETHER,), F32),
            pltpu.SMEM((1,), jnp.int32),
            pltpu.SemaphoreType.DMA((13,)),
            pltpu.SemaphoreType.DMA((4,)),
            pltpu.SemaphoreType.DMA((13,)),
            pltpu.SemaphoreType.DMA((16,)),
        ],
        compiler_params=params,
    )(place, values.astype(jnp.int32), values, own01, own2, behind01, behind2, ahead01, ahead2,
      across0, across1, across2a, across2b, ket_mps[:, 0], bra_own, bra_rim)
    mine, left, right, far = sums[:4], sums[4:8], sums[8:12], sums[12:]

    def added(*parts):
        return functools.reduce(jnp.add, [part.astype(F32) for part in parts])

    def moved(value, move, owner, i):
        return sent(value, move, owner, {n for n in range(ROWS) if COUNT[n] > i})

    far_up = {i: moved(far[i], x_up, x_far, i) for i in (0, 2)}
    far_down = {i: moved(far[i], x_down, x_far, i) for i in (1, 3)}
    from_left = {i: moved(right[i], x_up, x_up, i) for i in (1, 3)}
    from_right = {i: moved(left[i], x_down, x_down, i) for i in (0, 2)}
    for i in (0, 2):
        from_left[i] = moved(added(right[i], far_up[i]).astype(BF), x_up, x_up, i)
    for i in (1, 3):
        from_right[i] = moved(added(left[i], far_down[i]).astype(BF), x_down, x_down, i)

    here = [added(mine[i][0], from_left[i][0], from_right[i][0]) for i in range(4)]
    raised = [added(mine[i][1], from_left[i][1], from_right[i][1]).astype(BF) for i in range(4)]
    above = []
    for i in (0, 2):
        pairs = [(a * ROWS + n, (a + 1) * ROWS + n) for a in range(SECS - 1) for n in range(ROWS) if COUNT[n] > i]
        above.append(lax.ppermute(jnp.stack(raised[i : i + 2]), ("sec", "row"), pairs))

    out = pl.pallas_call(
        unpack_kernel,
        in_specs=[smem] * 3 + [vmem] * 6,
        out_specs=vmem,
        out_shape=shape((4, BB, KB), BF),
        compiler_params=params,
    )(place, ket_flat, bra_flat, *here, *above)
    return out.reshape(CH, 1, 2, BB, KB)


def solution(mesh):
    placed = (
        P("row", "sec", None, None, None),
        P(None, "sec", None, None, None),
        P(None, "sec", None, None, None),
        P(),
        P(),
        P("row", None, None),
        P("row", None),
    )
    return jax.shard_map(
        body,
        mesh=mesh,
        in_specs=placed,
        out_specs=P("row", "sec", None, None, None),
        check_vma=False,
    )
```

```python
import functools

import jax
import jax.numpy as jnp
from jax import lax
from jax.experimental import pallas as pl
from jax.experimental.pallas import tpu as pltpu
from jax.sharding import PartitionSpec as P

EPW, CH = 8, 2
NZ, NX = 4, 4
SECS, ROWS = 16, 16
BB, KB = 256, 512
QUARTER = BB // NX
TOGETHER = 2
BF, F32 = jnp.bfloat16, jnp.float32
STEPS = (0, -1, 1, 2)
VMEM_BYTES = 56 * 1024 * 1024
HEAD = 16
BRA_CELLS = ((0, 0), (0, 1), (2, 1), (1, 0), (1, 1), (3, 1))
CELLS = [(b, j) for b in range(2) for j in range(CH)]


def after(value, *others):
    return lax.optimization_barrier((value, *others))[0] if others else value


def charge(channel):
    klass = channel % 9
    return klass % 3 - 1, klass // 3 - 1


def live_at(r, b, j):
    to_b = b + charge(CH * r + j)[1]
    return jnp.where((to_b >= 0) & (to_b < 2), 1, 0)


COUNT = [sum(0 <= b + charge(CH * r + j)[1] < 2 for b, j in CELLS) for r in range(ROWS)]


def row_z(r, d):
    return (r // NX + d) % NZ * NX + r % NX


def row_x(r, d):
    return r // NX * NX + (r % NX + d) % NX


def packed_cells(r, a, ket_sizes, bra_sizes):
    places = [(jnp.int32(0), jnp.int32(0), jnp.int32(0)) for _ in range(4)]
    count = jnp.int32(0)
    for b, j in CELLS:
        out_a, out_b = charge(CH * r + j)
        live = live_at(r, b, j)
        at_a, at_b = a + out_a, jnp.clip(b + out_b, 0, 1)
        rows = jnp.where((at_a >= 0) & (at_a < SECS), bra_sizes[at_b, jnp.clip(at_a, 0, SECS - 1)], 0)
        cols = ket_sizes[b, a]
        for i in range(4):
            hit = (live == 1) & (count == i)
            places[i] = tuple(jnp.where(hit, new, old) for new, old in zip((2 * j + b, rows, cols), places[i]))
        count = count + live
    return places, count


def live_count(r):
    return sum(live_at(r, b, j) for b, j in CELLS)


def keep(rows, cols):
    row_at = lax.broadcasted_iota(jnp.int32, (BB, KB), 0)
    col_at = lax.broadcasted_iota(jnp.int32, (BB, KB), 1)
    return (row_at < rows) & (col_at < cols)


def prepare_kernel(place, ket_sizes, bra_sizes, entries, coeffs, env, pair_out, third_out, moving):
    r, a = place[0], place[1]
    lane = lax.broadcasted_iota(jnp.int32, (HEAD, KB), 1)
    slot, field = lane // 8, lane % 8
    places, count = packed_cells(r, a, ket_sizes, bra_sizes)
    for i, (cell, rows, cols) in enumerate(places):
        target = (pair_out.at[0], pair_out.at[1], third_out, moving)[i]
        j, b = cell // 2, cell % 2
        head = jnp.zeros((HEAD, KB), F32)
        for n in range(EPW):
            part = jnp.where(field < 3, 0.0, coeffs[j, n])
            for f in range(3):
                part = jnp.where(field == f, entries[f, j, n].astype(F32), part)
            part = jnp.where(field == 7, (b + 1).astype(F32), part)
            head = jnp.where(slot == n, part, head)
        first = head.astype(BF).astype(F32)
        second = (head - first).astype(BF).astype(F32)
        last = head - first - second
        head = jnp.where(field == 4, second, jnp.where(field == 5, last, first))
        head = jnp.where(i < count, head, 0.0)
        target[:HEAD] = head.astype(BF)
        target[HEAD:] = jnp.where(keep(rows, cols), env[cell], jnp.zeros((BB, KB), BF))


def bra_kernel(place, bra, flipped, strip, strip_low, strip_high):
    r = place[0]
    lines = pl.ds(pl.multiple_of(r % NX * QUARTER, QUARTER), QUARTER)
    for n, (sp, to_b) in enumerate(BRA_CELLS):
        flipped[n] = bra[sp, to_b].T
        value = flipped[n, lines]
        strip[n] = value
        if n < 3:
            strip_low[n] = value
        else:
            strip_high[n - 3] = value


def unpack_kernel(place, ket_sizes, bra_sizes, *refs):
    here, above, out = refs[:4], refs[4:6], refs[6]
    out[...] = jnp.zeros_like(out)
    for i, (cell, rows, cols) in enumerate(packed_cells(place[0], place[1], ket_sizes, bra_sizes)[0]):

        @pl.when(rows > 0)
        def _(i=i, cell=cell, rows=rows, cols=cols):
            value = here[i][...] + above[i // 2][i % 2].astype(F32)
            out[cell] = jnp.where(keep(rows, cols), value, 0.0).astype(BF)


def terms_kernel(place, ints, values, *refs):
    two, three, lone = (refs[0], refs[2], refs[4]), (refs[1], refs[3], refs[5]), refs[6:9]
    across2b, ket_in, bra_own, rim, swapped, crossed = refs[9:15]
    outs = refs[15:31]
    env_all, ket, bra_all, total, rounded, todo, scale, size, env_sem, ket_sem, bra_sem, out_sem = refs[31:]
    copies = []
    body_rows = pl.ds(HEAD, BB)
    views = []
    for first, third in zip(two, three):
        views += [first.at[0, body_rows], first.at[1, body_rows], third.at[body_rows]]
    views += [lone[0].at[body_rows], lone[1].at[body_rows]]
    copies += [pltpu.make_async_copy(view, env_all.at[n], env_sem.at[n]) for n, view in enumerate(views)]
    half_rows = pl.ds(0, BB // 2)
    copies.append(pltpu.make_async_copy(lone[2].at[pl.ds(HEAD, BB // 2)], env_all.at[11, half_rows], env_sem.at[11]))
    copies.append(pltpu.make_async_copy(across2b, env_all.at[11, pl.ds(BB // 2, BB // 2)], env_sem.at[12]))
    copies += [pltpu.make_async_copy(ket_in.at[s], ket.at[pl.ds(2 * s, 2)], ket_sem.at[s]) for s in range(4)]
    copies.append(pltpu.make_async_copy(bra_own, bra_all.at[pl.ds(6, 6)], bra_sem.at[0]))
    x = place[0] % NX
    y = NX - 1 - x
    quarters = ((rim, 0, x), (swapped, 0, x + 1 - 2 * (x % 2)), (crossed, 0, y), (crossed, 12, y + 1 - 2 * (y % 2)))
    for n, (ref, at, owner) in enumerate(quarters):
        lines = pl.ds(pl.multiple_of(QUARTER * owner, QUARTER), QUARTER)
        for m, (first, count, to) in enumerate(((0, 3, 0), (3, 6, 12), (9, 3, 21))):
            copies.append(pltpu.make_async_copy(
                ref.at[pl.ds(at + first, count)], bra_all.at[pl.ds(to, count), lines], bra_sem.at[1 + 3 * n + m]
            ))
    for copy in copies:
        copy.start()

    r, a = place[0], place[1]
    my_z, my_x = r // NX, r % NX
    for d in range(4):
        for i in range(4):

            @pl.when(i < live_count(row_x(r, STEPS[d])))
            def _(at=8 * d + 2 * i):
                total[at] = jnp.zeros((BB, KB), F32)
                total[at + 1] = jnp.zeros((BB, KB), F32)

    size[0] = 0

    @pl.loop(0, 12 * EPW)
    def _(item):
        base = 64 * (item // EPW) + 8 * (item % EPW)
        out_w, s, code = ints[base], ints[base + 2], ints[base + 7]
        q_b = code - 1
        p_b, s_a = q_b + s // 2, s % 2

        @pl.when((code > 0) & (out_w // (CH * NX) == my_z) & (p_b < 2) & (a + s_a < SECS))
        def _():
            out_r, out_j = out_w // CH, out_w % CH

            @pl.when(live_at(out_r, p_b, out_j) == 1)
            def _():
                sp, at = ints[base + 1], size[0]
                forward = (out_r % NX - my_x + NX) % NX
                slot = jnp.where(forward == 1, 2, jnp.where(forward == 3, 1, jnp.where(forward == 2, 3, 0)))
                out_a, out_b = charge(out_w)
                low = live_at(out_r, 0, 0)
                inside = low + live_at(out_r, 0, 1) + out_j * live_at(out_r, 1, 0)
                position = jnp.where(p_b == 0, out_j * low, inside)
                todo[4 * at] = item // EPW
                todo[4 * at + 1] = 2 * s + q_b
                todo[4 * at + 2] = 6 * (s_a + out_a + 1) + 3 * (sp % 2) + p_b + out_b + sp // 2
                todo[4 * at + 3] = 8 * slot + 2 * position + s_a
                scale[at] = values[base + 3] + values[base + 4] + values[base + 5]
                size[0] = at + 1

    count = size[0]
    for n in range(TOGETHER - 1):
        for field in range(3):
            todo[4 * (count + n) + field] = 0
        todo[4 * (count + n) + 3] = 32
        scale[count + n] = 0.0

    for copy in copies:
        copy.wait()

    @pl.loop(0, (count + TOGETHER - 1) // TOGETHER)
    def _(step):
        places = [step * TOGETHER + n for n in range(TOGETHER)]
        halves = [
            jnp.dot(env_all[todo[4 * n]], ket[todo[4 * n + 1]], preferred_element_type=F32).astype(BF) for n in places
        ]
        terms = [
            jnp.dot(bra_all[todo[4 * n + 2]], half, preferred_element_type=F32) for n, half in zip(places, halves)
        ]
        for n, term in zip(places, terms):
            at = todo[4 * n + 3]
            total[at] = total[at] + scale[n] * term

    def stored(d, i):
        return pltpu.make_async_copy(rounded.at[4 * d + i], outs[4 * d + i], out_sem.at[4 * d + i])

    for d in (3, 2, 1, 0):
        for i in range(4):

            @pl.when(i < live_count(row_x(r, STEPS[d])))
            def _(d=d, i=i):
                for up in range(2):
                    rounded[4 * d + i, up] = total[8 * d + 2 * i + up].astype(BF)
                stored(d, i).start()

    for d in (3, 2, 1, 0):
        for i in range(4):

            @pl.when(i < live_count(row_x(r, STEPS[d])))
            def _(d=d, i=i):
                stored(d, i).wait()


def body(env_in, ket_mps, bra_mps, ket_sizes, bra_sizes, entries, coeffs):
    my_a = lax.axis_index("sec")
    r = lax.axis_index("row")
    place = jnp.stack([r, my_a])
    ket_flat, bra_flat = ket_sizes.T, bra_sizes.T

    smem = pl.BlockSpec(memory_space=pltpu.SMEM)
    vmem = pl.BlockSpec(memory_space=pltpu.VMEM)
    shape = jax.ShapeDtypeStruct
    pair = shape((2, BB, KB), BF)
    params = pltpu.CompilerParams(vmem_limit_bytes=VMEM_BYTES)
    payload = shape((HEAD + BB, KB), BF)
    own01, own2, moving = pl.pallas_call(
        prepare_kernel,
        in_specs=[smem] * 5 + [vmem],
        out_specs=[vmem] * 3,
        out_shape=[shape((2, HEAD + BB, KB), BF), payload, payload],
        compiler_params=params,
    )(place, ket_flat, bra_flat, entries.transpose(2, 0, 1), coeffs, env_in.reshape(4, BB, KB))

    same = lambda n: n
    z_up, z_down = (lambda n: row_z(n, 1)), (lambda n: row_z(n, -1))
    x_up, x_down, x_far = (lambda n: row_x(n, 1)), (lambda n: row_x(n, -1)), (lambda n: row_x(n, 2))

    def sent(value, move, owner, rows):
        return lax.ppermute(value, "row", [(n, move(n)) for n in range(ROWS) if owner(n) in rows])

    everyone = set(range(ROWS))
    full = [n for n in range(ROWS) if COUNT[n] == 4]
    takers, lent = set(), []
    for n in full:
        taker = next(m for m in (row_x(n, 1), row_x(n, -1)) if COUNT[m] == 2 and m not in takers)
        takers.add(taker)
        lent.append((n, taker))
    three = {n for n in range(ROWS) if COUNT[n] > 2} | takers
    behind01 = sent(own01, z_up, same, everyone)
    ahead01 = sent(own01, z_down, same, everyone)

    bra_own, strip, strip_low, strip_high = pl.pallas_call(
        bra_kernel,
        in_specs=[smem, vmem],
        out_specs=[vmem] * 4,
        out_shape=[
            shape((6, BB, BB), BF),
            shape((6, QUARTER, BB), BF),
            shape((3, QUARTER, BB), BF),
            shape((3, QUARTER, BB), BF),
        ],
        compiler_params=params,
    )(place, after(bra_mps, own01)[:, 0])
    up = lambda n: [(i, i + n) for i in range(SECS - n)]
    down = lambda n: [(i + n, i) for i in range(SECS - n)]
    rim_low = lax.ppermute(strip_low, "sec", up(1))
    borrowed = lax.ppermute(after(moving, rim_low), "row", lent)
    own2 = own2 + borrowed
    behind2 = sent(own2, z_up, same, three)
    ahead2 = sent(own2, z_down, same, three)
    across0 = sent(behind01[0], z_up, z_down, everyone)
    across1 = sent(ahead01[1], z_down, z_up, everyone)
    across2a = sent(behind2[: HEAD + BB // 2], z_up, z_down, three)
    across2b = sent(ahead2[HEAD + BB // 2 :], z_down, z_up, three)
    rim = jnp.concatenate([
        rim_low,
        lax.ppermute(strip, "sec", down(1)),
        lax.ppermute(strip_high, "sec", down(2)),
    ])
    swapped = lax.ppermute(rim, "row", [(n, n ^ 1) for n in range(ROWS)])
    crossed = lax.ppermute(jnp.concatenate([rim, swapped]), "row", [(n, n ^ 3) for n in range(ROWS)])

    heads = [own01[0], own01[1], own2, behind01[0], behind01[1], behind2, ahead01[0], ahead01[1], ahead2,
             across0, across1, across2a]
    values = jnp.concatenate([head[0, :64] for head in heads]).astype(F32)

    hbm = pl.BlockSpec(memory_space=pl.ANY)
    sums = pl.pallas_call(
        terms_kernel,
        in_specs=[smem] * 3 + [hbm] * 15,
        out_specs=[hbm] * 16,
        out_shape=[pair] * 16,
        scratch_shapes=[
            pltpu.VMEM((12, BB, KB), BF),
            pltpu.VMEM((8, KB, KB), BF),
            pltpu.VMEM((24, BB, BB), BF),
            pltpu.VMEM((33, BB, KB), F32),
            pltpu.VMEM((16, 2, BB, KB), BF),
            pltpu.SMEM((4 * (12 * EPW + TOGETHER),), jnp.int32),
            pltpu.SMEM((12 * EPW + TOGETHER,), F32),
            pltpu.SMEM((1,), jnp.int32),
            pltpu.SemaphoreType.DMA((13,)),
            pltpu.SemaphoreType.DMA((4,)),
            pltpu.SemaphoreType.DMA((13,)),
            pltpu.SemaphoreType.DMA((16,)),
        ],
        compiler_params=params,
    )(place, values.astype(jnp.int32), values, own01, own2, behind01, behind2, ahead01, ahead2,
      across0, across1, across2a, across2b, ket_mps[:, 0], bra_own, rim, swapped, crossed)
    mine, left, right, far = sums[:4], sums[4:8], sums[8:12], sums[12:]

    def added(*parts):
        return functools.reduce(jnp.add, [part.astype(F32) for part in parts])

    def moved(value, move, owner, i):
        return sent(value, move, owner, {n for n in range(ROWS) if COUNT[n] > i})

    far_up = {i: moved(far[i], x_up, x_far, i) for i in (0, 2)}
    far_down = {i: moved(far[i], x_down, x_far, i) for i in (1, 3)}
    from_left = {i: moved(right[i], x_up, x_up, i) for i in (1, 3)}
    from_right = {i: moved(left[i], x_down, x_down, i) for i in (0, 2)}
    for i in (0, 2):
        from_left[i] = moved(added(right[i], far_up[i]).astype(BF), x_up, x_up, i)
    for i in (1, 3):
        from_right[i] = moved(added(left[i], far_down[i]).astype(BF), x_down, x_down, i)

    here = [added(mine[i][0], from_left[i][0], from_right[i][0]) for i in range(4)]
    raised = [added(mine[i][1], from_left[i][1], from_right[i][1]).astype(BF) for i in range(4)]
    above = []
    for i in (0, 2):
        pairs = [(a * ROWS + n, (a + 1) * ROWS + n) for a in range(SECS - 1) for n in range(ROWS) if COUNT[n] > i]
        above.append(lax.ppermute(jnp.stack(raised[i : i + 2]), ("sec", "row"), pairs))

    out = pl.pallas_call(
        unpack_kernel,
        in_specs=[smem] * 3 + [vmem] * 6,
        out_specs=vmem,
        out_shape=shape((4, BB, KB), BF),
        compiler_params=params,
    )(place, ket_flat, bra_flat, *here, *above)
    return out.reshape(CH, 1, 2, BB, KB)


def solution(mesh):
    placed = (
        P("row", "sec", None, None, None),
        P(None, "sec", None, None, None),
        P(None, "sec", None, None, None),
        P(),
        P(),
        P("row", None, None),
        P("row", None),
    )
    return jax.shard_map(
        body,
        mesh=mesh,
        in_specs=placed,
        out_specs=P("row", "sec", None, None, None),
        check_vma=False,
    )
```

```python
import functools

import jax
import jax.numpy as jnp
from jax import lax
from jax.experimental import pallas as pl
from jax.experimental.pallas import tpu as pltpu
from jax.sharding import PartitionSpec as P

EPW, CH = 8, 2
NZ, NX = 4, 4
SECS, ROWS = 16, 16
BB, KB = 256, 512
QUARTER = BB // NX
TOGETHER = 2
BF, F32 = jnp.bfloat16, jnp.float32
STEPS = (0, -1, 1, 2)
VMEM_BYTES = 56 * 1024 * 1024
HEAD = 16
BRA_CELLS = ((0, 0), (0, 1), (2, 1), (1, 0), (1, 1), (3, 1))
CELLS = [(b, j) for b in range(2) for j in range(CH)]


def after(value, *others):
    return lax.optimization_barrier((value, *others))[0] if others else value


def charge(channel):
    klass = channel % 9
    return klass % 3 - 1, klass // 3 - 1


def live_at(r, b, j):
    to_b = b + charge(CH * r + j)[1]
    return jnp.where((to_b >= 0) & (to_b < 2), 1, 0)


COUNT = [sum(0 <= b + charge(CH * r + j)[1] < 2 for b, j in CELLS) for r in range(ROWS)]


def row_z(r, d):
    return (r // NX + d) % NZ * NX + r % NX


def row_x(r, d):
    return r // NX * NX + (r % NX + d) % NX


def packed_cells(r, a, ket_sizes, bra_sizes):
    places = [(jnp.int32(0), jnp.int32(0), jnp.int32(0)) for _ in range(4)]
    count = jnp.int32(0)
    for b, j in CELLS:
        out_a, out_b = charge(CH * r + j)
        live = live_at(r, b, j)
        at_a, at_b = a + out_a, jnp.clip(b + out_b, 0, 1)
        rows = jnp.where((at_a >= 0) & (at_a < SECS), bra_sizes[at_b, jnp.clip(at_a, 0, SECS - 1)], 0)
        cols = ket_sizes[b, a]
        for i in range(4):
            hit = (live == 1) & (count == i)
            places[i] = tuple(jnp.where(hit, new, old) for new, old in zip((2 * j + b, rows, cols), places[i]))
        count = count + live
    return places, count


def live_count(r):
    return sum(live_at(r, b, j) for b, j in CELLS)


def keep(rows, cols):
    row_at = lax.broadcasted_iota(jnp.int32, (BB, KB), 0)
    col_at = lax.broadcasted_iota(jnp.int32, (BB, KB), 1)
    return (row_at < rows) & (col_at < cols)


def prepare_kernel(place, ket_sizes, bra_sizes, entries, coeffs, env, pair_out, third_out, moving):
    r, a = place[0], place[1]
    lane = lax.broadcasted_iota(jnp.int32, (HEAD, KB), 1)
    slot, field = lane // 8, lane % 8
    places, count = packed_cells(r, a, ket_sizes, bra_sizes)
    for i, (cell, rows, cols) in enumerate(places):
        target = (pair_out.at[0], pair_out.at[1], third_out, moving)[i]
        j, b = cell // 2, cell % 2
        head = jnp.zeros((HEAD, KB), F32)
        for n in range(EPW):
            part = jnp.where(field < 3, 0.0, coeffs[j, n])
            for f in range(3):
                part = jnp.where(field == f, entries[f, j, n].astype(F32), part)
            part = jnp.where(field == 7, (b + 1).astype(F32), part)
            head = jnp.where(slot == n, part, head)
        first = head.astype(BF).astype(F32)
        second = (head - first).astype(BF).astype(F32)
        last = head - first - second
        head = jnp.where(field == 4, second, jnp.where(field == 5, last, first))
        head = jnp.where(i < count, head, 0.0)
        target[:HEAD] = head.astype(BF)
        target[HEAD:] = jnp.where(keep(rows, cols), env[cell], jnp.zeros((BB, KB), BF))


def bra_kernel(place, bra, flipped, strip, strip_low, strip_high):
    r = place[0]
    lines = pl.ds(pl.multiple_of(r % NX * QUARTER, QUARTER), QUARTER)
    for n, (sp, to_b) in enumerate(BRA_CELLS):
        flipped[n] = bra[sp, to_b].T
        value = flipped[n, lines]
        strip[n] = value
        if n < 3:
            strip_low[n] = value
        else:
            strip_high[n - 3] = value


def unpack_kernel(place, ket_sizes, bra_sizes, *refs):
    here, above, out = refs[:4], refs[4:6], refs[6]
    out[...] = jnp.zeros_like(out)
    for i, (cell, rows, cols) in enumerate(packed_cells(place[0], place[1], ket_sizes, bra_sizes)[0]):

        @pl.when(rows > 0)
        def _(i=i, cell=cell, rows=rows, cols=cols):
            value = here[i][...] + above[i // 2][i % 2].astype(F32)
            out[cell] = jnp.where(keep(rows, cols), value, 0.0).astype(BF)


def terms_kernel(slots, place, ints, values, *refs):
    width = 4 * len(slots)
    two, three, lone = (refs[0], refs[2], refs[4]), (refs[1], refs[3], refs[5]), refs[6:9]
    across2b, ket_in, bra_own, rim, swapped, crossed = refs[9:15]
    outs = refs[15 : 15 + width]
    env_all, ket, bra_all, total, rounded, todo, scale, size, env_sem, ket_sem, bra_sem, out_sem = refs[15 + width :]
    copies = []
    body_rows = pl.ds(HEAD, BB)
    views = []
    for first, third in zip(two, three):
        views += [first.at[0, body_rows], first.at[1, body_rows], third.at[body_rows]]
    views += [lone[0].at[body_rows], lone[1].at[body_rows]]
    copies += [pltpu.make_async_copy(view, env_all.at[n], env_sem.at[n]) for n, view in enumerate(views)]
    half_rows = pl.ds(0, BB // 2)
    copies.append(pltpu.make_async_copy(lone[2].at[pl.ds(HEAD, BB // 2)], env_all.at[11, half_rows], env_sem.at[11]))
    copies.append(pltpu.make_async_copy(across2b, env_all.at[11, pl.ds(BB // 2, BB // 2)], env_sem.at[12]))
    copies += [pltpu.make_async_copy(ket_in.at[s], ket.at[pl.ds(2 * s, 2)], ket_sem.at[s]) for s in range(4)]
    copies.append(pltpu.make_async_copy(bra_own, bra_all.at[pl.ds(6, 6)], bra_sem.at[0]))
    x = place[0] % NX
    y = NX - 1 - x
    quarters = ((rim, 0, x), (swapped, 0, x + 1 - 2 * (x % 2)), (crossed, 0, y), (crossed, 12, y + 1 - 2 * (y % 2)))
    for n, (ref, at, owner) in enumerate(quarters):
        lines = pl.ds(pl.multiple_of(QUARTER * owner, QUARTER), QUARTER)
        for m, (first, count, to) in enumerate(((0, 3, 0), (3, 6, 12), (9, 3, 21))):
            copies.append(pltpu.make_async_copy(
                ref.at[pl.ds(at + first, count)], bra_all.at[pl.ds(to, count), lines], bra_sem.at[1 + 3 * n + m]
            ))
    for copy in copies:
        copy.start()

    r, a = place[0], place[1]
    my_z, my_x = r // NX, r % NX
    for d, slot in enumerate(slots):
        for i in range(4):

            @pl.when(i < live_count(row_x(r, STEPS[slot])))
            def _(at=8 * d + 2 * i):
                total[at] = jnp.zeros((BB, KB), F32)
                total[at + 1] = jnp.zeros((BB, KB), F32)

    size[0] = 0

    @pl.loop(0, 12 * EPW)
    def _(item):
        base = 64 * (item // EPW) + 8 * (item % EPW)
        out_w, s, code = ints[base], ints[base + 2], ints[base + 7]
        q_b = code - 1
        p_b, s_a = q_b + s // 2, s % 2

        @pl.when((code > 0) & (out_w // (CH * NX) == my_z) & (p_b < 2) & (a + s_a < SECS))
        def _():
            out_r, out_j = out_w // CH, out_w % CH

            forward = (out_r % NX - my_x + NX) % NX
            slot = jnp.where(forward == 1, 2, jnp.where(forward == 3, 1, jnp.where(forward == 2, 3, 0)))
            inside = (slot >= slots[0]) & (slot <= slots[-1])

            @pl.when(inside & (live_at(out_r, p_b, out_j) == 1))
            def _():
                sp, at = ints[base + 1], size[0]
                out_a, out_b = charge(out_w)
                low = live_at(out_r, 0, 0)
                inside = low + live_at(out_r, 0, 1) + out_j * live_at(out_r, 1, 0)
                position = jnp.where(p_b == 0, out_j * low, inside)
                todo[4 * at] = item // EPW
                todo[4 * at + 1] = 2 * s + q_b
                todo[4 * at + 2] = 6 * (s_a + out_a + 1) + 3 * (sp % 2) + p_b + out_b + sp // 2
                todo[4 * at + 3] = 8 * (slot - slots[0]) + 2 * position + s_a
                scale[at] = values[base + 3] + values[base + 4] + values[base + 5]
                size[0] = at + 1

    count = size[0]
    for n in range(TOGETHER - 1):
        for field in range(3):
            todo[4 * (count + n) + field] = 0
        todo[4 * (count + n) + 3] = 2 * width
        scale[count + n] = 0.0

    for copy in copies:
        copy.wait()

    @pl.loop(0, (count + TOGETHER - 1) // TOGETHER)
    def _(step):
        places = [step * TOGETHER + n for n in range(TOGETHER)]
        halves = [
            jnp.dot(env_all[todo[4 * n]], ket[todo[4 * n + 1]], preferred_element_type=F32).astype(BF) for n in places
        ]
        terms = [
            jnp.dot(bra_all[todo[4 * n + 2]], half, preferred_element_type=F32) for n, half in zip(places, halves)
        ]
        for n, term in zip(places, terms):
            at = todo[4 * n + 3]
            total[at] = total[at] + scale[n] * term

    def stored(d, i):
        return pltpu.make_async_copy(rounded.at[4 * d + i], outs[4 * d + i], out_sem.at[4 * d + i])

    for d in range(len(slots)):
        for i in range(4):

            @pl.when(i < live_count(row_x(r, STEPS[slots[d]])))
            def _(d=d, i=i):
                for up in range(2):
                    rounded[4 * d + i, up] = total[8 * d + 2 * i + up].astype(BF)
                stored(d, i).start()

    for d in range(len(slots)):
        for i in range(4):

            @pl.when(i < live_count(row_x(r, STEPS[slots[d]])))
            def _(d=d, i=i):
                stored(d, i).wait()


def body(env_in, ket_mps, bra_mps, ket_sizes, bra_sizes, entries, coeffs):
    my_a = lax.axis_index("sec")
    r = lax.axis_index("row")
    place = jnp.stack([r, my_a])
    ket_flat, bra_flat = ket_sizes.T, bra_sizes.T

    smem = pl.BlockSpec(memory_space=pltpu.SMEM)
    vmem = pl.BlockSpec(memory_space=pltpu.VMEM)
    shape = jax.ShapeDtypeStruct
    pair = shape((2, BB, KB), BF)
    params = pltpu.CompilerParams(vmem_limit_bytes=VMEM_BYTES)
    payload = shape((HEAD + BB, KB), BF)
    own01, own2, moving = pl.pallas_call(
        prepare_kernel,
        in_specs=[smem] * 5 + [vmem],
        out_specs=[vmem] * 3,
        out_shape=[shape((2, HEAD + BB, KB), BF), payload, payload],
        compiler_params=params,
    )(place, ket_flat, bra_flat, entries.transpose(2, 0, 1), coeffs, env_in.reshape(4, BB, KB))

    same = lambda n: n
    z_up, z_down = (lambda n: row_z(n, 1)), (lambda n: row_z(n, -1))
    x_up, x_down, x_far = (lambda n: row_x(n, 1)), (lambda n: row_x(n, -1)), (lambda n: row_x(n, 2))

    def sent(value, move, owner, rows):
        return lax.ppermute(value, "row", [(n, move(n)) for n in range(ROWS) if owner(n) in rows])

    everyone = set(range(ROWS))
    full = [n for n in range(ROWS) if COUNT[n] == 4]
    takers, lent = set(), []
    for n in full:
        taker = next(m for m in (row_x(n, 1), row_x(n, -1)) if COUNT[m] == 2 and m not in takers)
        takers.add(taker)
        lent.append((n, taker))
    three = {n for n in range(ROWS) if COUNT[n] > 2} | takers
    behind01 = sent(own01, z_up, same, everyone)
    ahead01 = sent(own01, z_down, same, everyone)

    bra_own, strip, strip_low, strip_high = pl.pallas_call(
        bra_kernel,
        in_specs=[smem, vmem],
        out_specs=[vmem] * 4,
        out_shape=[
            shape((6, BB, BB), BF),
            shape((6, QUARTER, BB), BF),
            shape((3, QUARTER, BB), BF),
            shape((3, QUARTER, BB), BF),
        ],
        compiler_params=params,
    )(place, after(bra_mps, own01)[:, 0])
    up = lambda n: [(i, i + n) for i in range(SECS - n)]
    down = lambda n: [(i + n, i) for i in range(SECS - n)]
    rim_low = lax.ppermute(strip_low, "sec", up(1))
    borrowed = lax.ppermute(after(moving, rim_low), "row", lent)
    own2 = own2 + borrowed
    behind2 = sent(own2, z_up, same, three)
    ahead2 = sent(own2, z_down, same, three)
    across0 = sent(behind01[0], z_up, z_down, everyone)
    across1 = sent(ahead01[1], z_down, z_up, everyone)
    across2a = sent(behind2[: HEAD + BB // 2], z_up, z_down, three)
    across2b = sent(ahead2[HEAD + BB // 2 :], z_down, z_up, three)
    rim = jnp.concatenate([
        rim_low,
        lax.ppermute(strip, "sec", down(1)),
        lax.ppermute(strip_high, "sec", down(2)),
    ])
    swapped = lax.ppermute(rim, "row", [(n, n ^ 1) for n in range(ROWS)])
    crossed = lax.ppermute(jnp.concatenate([rim, swapped]), "row", [(n, n ^ 3) for n in range(ROWS)])

    heads = [own01[0], own01[1], own2, behind01[0], behind01[1], behind2, ahead01[0], ahead01[1], ahead2,
             across0, across1, across2a]
    values = jnp.concatenate([head[0, :64] for head in heads]).astype(F32)

    hbm = pl.BlockSpec(memory_space=pl.ANY)
    def terms(slots, own):
        width = 4 * len(slots)
        return pl.pallas_call(
            functools.partial(terms_kernel, slots),
            in_specs=[smem] * 3 + [hbm] * 15,
            out_specs=[hbm] * width,
            out_shape=[pair] * width,
            scratch_shapes=[
                pltpu.VMEM((12, BB, KB), BF),
                pltpu.VMEM((8, KB, KB), BF),
                pltpu.VMEM((24, BB, BB), BF),
                pltpu.VMEM((2 * width + 1, BB, KB), F32),
                pltpu.VMEM((width, 2, BB, KB), BF),
                pltpu.SMEM((4 * (12 * EPW + TOGETHER),), jnp.int32),
                pltpu.SMEM((12 * EPW + TOGETHER,), F32),
                pltpu.SMEM((1,), jnp.int32),
                pltpu.SemaphoreType.DMA((13,)),
                pltpu.SemaphoreType.DMA((4,)),
                pltpu.SemaphoreType.DMA((13,)),
                pltpu.SemaphoreType.DMA((width,)),
            ],
            compiler_params=params,
        )(place, values.astype(jnp.int32), values, own, own2, behind01, behind2, ahead01, ahead2,
          across0, across1, across2a, across2b, ket_mps[:, 0], bra_own, rim, swapped, crossed)

    far = terms((3,), own01)
    sums = terms((0, 1, 2), after(own01, *far))
    mine, left, right = sums[:4], sums[4:8], sums[8:]

    def added(*parts):
        return functools.reduce(jnp.add, [part.astype(F32) for part in parts])

    def moved(value, move, owner, i):
        return sent(value, move, owner, {n for n in range(ROWS) if COUNT[n] > i})

    far_up = {i: moved(far[i], x_up, x_far, i) for i in (0, 2)}
    far_down = {i: moved(far[i], x_down, x_far, i) for i in (1, 3)}
    from_left = {i: moved(right[i], x_up, x_up, i) for i in (1, 3)}
    from_right = {i: moved(left[i], x_down, x_down, i) for i in (0, 2)}
    for i in (0, 2):
        from_left[i] = moved(added(right[i], far_up[i]).astype(BF), x_up, x_up, i)
    for i in (1, 3):
        from_right[i] = moved(added(left[i], far_down[i]).astype(BF), x_down, x_down, i)

    here = [added(mine[i][0], from_left[i][0], from_right[i][0]) for i in range(4)]
    raised = [added(mine[i][1], from_left[i][1], from_right[i][1]).astype(BF) for i in range(4)]
    above = []
    for i in (0, 2):
        pairs = [(a * ROWS + n, (a + 1) * ROWS + n) for a in range(SECS - 1) for n in range(ROWS) if COUNT[n] > i]
        above.append(lax.ppermute(jnp.stack(raised[i : i + 2]), ("sec", "row"), pairs))

    out = pl.pallas_call(
        unpack_kernel,
        in_specs=[smem] * 3 + [vmem] * 6,
        out_specs=vmem,
        out_shape=shape((4, BB, KB), BF),
        compiler_params=params,
    )(place, ket_flat, bra_flat, *here, *above)
    return out.reshape(CH, 1, 2, BB, KB)


def solution(mesh):
    placed = (
        P("row", "sec", None, None, None),
        P(None, "sec", None, None, None),
        P(None, "sec", None, None, None),
        P(),
        P(),
        P("row", None, None),
        P("row", None),
    )
    return jax.shard_map(
        body,
        mesh=mesh,
        in_specs=placed,
        out_specs=P("row", "sec", None, None, None),
        check_vma=False,
    )
```

```python
import functools

import jax
import jax.numpy as jnp
from jax import lax
from jax.experimental import pallas as pl
from jax.experimental.pallas import tpu as pltpu
from jax.sharding import PartitionSpec as P

EPW, CH = 8, 2
NZ, NX = 4, 4
SECS, ROWS = 16, 16
BB, KB = 256, 512
QUARTER = BB // NX
TOGETHER = 2
BF, F32 = jnp.bfloat16, jnp.float32
STEPS = (0, -1, 1, 2)
VMEM_BYTES = 56 * 1024 * 1024
HEAD = 16
LANES = 128
BRA_CELLS = ((0, 0), (0, 1), (2, 1), (1, 0), (1, 1), (3, 1))
CELLS = [(b, j) for b in range(2) for j in range(CH)]


def after(value, *others):
    return lax.optimization_barrier((value, *others))[0] if others else value


def charge(channel):
    klass = channel % 9
    return klass % 3 - 1, klass // 3 - 1


def live_at(r, b, j):
    to_b = b + charge(CH * r + j)[1]
    return jnp.where((to_b >= 0) & (to_b < 2), 1, 0)


COUNT = [sum(0 <= b + charge(CH * r + j)[1] < 2 for b, j in CELLS) for r in range(ROWS)]


def row_z(r, d):
    return (r // NX + d) % NZ * NX + r % NX


def row_x(r, d):
    return r // NX * NX + (r % NX + d) % NX


def packed_cells(r, a, ket_sizes, bra_sizes):
    places = [(jnp.int32(0), jnp.int32(0), jnp.int32(0)) for _ in range(4)]
    count = jnp.int32(0)
    for b, j in CELLS:
        out_a, out_b = charge(CH * r + j)
        live = live_at(r, b, j)
        at_a, at_b = a + out_a, jnp.clip(b + out_b, 0, 1)
        rows = jnp.where((at_a >= 0) & (at_a < SECS), bra_sizes[at_b, jnp.clip(at_a, 0, SECS - 1)], 0)
        cols = ket_sizes[b, a]
        for i in range(4):
            hit = (live == 1) & (count == i)
            places[i] = tuple(jnp.where(hit, new, old) for new, old in zip((2 * j + b, rows, cols), places[i]))
        count = count + live
    return places, count


def live_count(r):
    return sum(live_at(r, b, j) for b, j in CELLS)


def keep(rows, cols):
    row_at = lax.broadcasted_iota(jnp.int32, (BB, KB), 0)
    col_at = lax.broadcasted_iota(jnp.int32, (BB, KB), 1)
    return (row_at < rows) & (col_at < cols)


def prepare_kernel(place, ket_sizes, bra_sizes, entries, coeffs, env, pair_out, third_out, moving):
    r, a = place[0], place[1]
    lane = lax.broadcasted_iota(jnp.int32, (HEAD, KB), 1)
    slot, field = lane // 8, lane % 8
    places, count = packed_cells(r, a, ket_sizes, bra_sizes)
    for i, (cell, rows, cols) in enumerate(places):
        target = (pair_out.at[0], pair_out.at[1], third_out, moving)[i]
        j, b = cell // 2, cell % 2
        head = jnp.zeros((HEAD, KB), F32)
        for n in range(EPW):
            part = jnp.where(field < 3, 0.0, coeffs[j, n])
            for f in range(3):
                part = jnp.where(field == f, entries[f, j, n].astype(F32), part)
            part = jnp.where(field == 7, (b + 1).astype(F32), part)
            head = jnp.where(slot == n, part, head)
        first = head.astype(BF).astype(F32)
        second = (head - first).astype(BF).astype(F32)
        last = head - first - second
        head = jnp.where(field == 4, second, jnp.where(field == 5, last, first))
        head = jnp.where(i < count, head, 0.0)
        target[:HEAD] = head.astype(BF)
        target[HEAD:] = jnp.where(keep(rows, cols), env[cell], jnp.zeros((BB, KB), BF))


def bra_kernel(place, bra, flipped, strip, strip_low, strip_high):
    r = place[0]
    lines = pl.ds(pl.multiple_of(r % NX * QUARTER, QUARTER), QUARTER)
    for n, (sp, to_b) in enumerate(BRA_CELLS):
        flipped[n] = bra[sp, to_b].T
        value = flipped[n, lines]
        strip[n] = value
        if n < 3:
            strip_low[n] = value
        else:
            strip_high[n - 3] = value


def unpack_kernel(place, ket_sizes, bra_sizes, here0, here1, above, out):
    out[...] = jnp.zeros_like(out)
    places = packed_cells(place[0], place[1], ket_sizes, bra_sizes)[0]
    for i, here in enumerate((here0, here1)):
        cell, rows, cols = places[i]

        @pl.when(rows > 0)
        def _(i=i, here=here, cell=cell, rows=rows, cols=cols):
            value = here[...] + above[i].astype(F32)
            out[cell] = jnp.where(keep(rows, cols), value, 0.0).astype(BF)


def finish_kernel(place, ket_sizes, bra_sizes, here2, here3, above, _, out, done, sem):
    places = packed_cells(place[0], place[1], ket_sizes, bra_sizes)[0]
    for i, here in enumerate((here2, here3)):
        cell, rows, cols = places[2 + i]

        @pl.when(rows > 0)
        def _(i=i, here=here, cell=cell, rows=rows, cols=cols):
            value = here[...] + above[i].astype(F32)
            done[i] = jnp.where(keep(rows, cols), value, 0.0).astype(BF)
            pltpu.make_async_copy(done.at[i], out.at[cell], sem.at[i]).start()

    for i in range(2):
        cell, rows, _ = places[2 + i]

        @pl.when(rows > 0)
        def _(i=i, cell=cell):
            pltpu.make_async_copy(done.at[i], out.at[cell], sem.at[i]).wait()


def terms_kernel(slots, place, ints, values, *refs):
    width = 4 * len(slots)
    two, three, lone = (refs[0], refs[2], refs[4]), (refs[1], refs[3], refs[5]), refs[6:9]
    across2b, ket_in, bra_own, rim, swapped, crossed = refs[9:15]
    outs = refs[15 : 15 + width]
    env_all, ket, bra_all, total, rounded, todo, scale, size, env_sem, ket_sem, bra_sem, out_sem = refs[15 + width :]
    copies = []
    body_rows = pl.ds(HEAD, BB)
    views = []
    for first, third in zip(two, three):
        views += [first.at[0, body_rows], first.at[1, body_rows], third.at[body_rows]]
    views += [lone[0].at[body_rows], lone[1].at[body_rows]]
    copies += [pltpu.make_async_copy(view, env_all.at[n], env_sem.at[n]) for n, view in enumerate(views)]
    half_rows = pl.ds(0, BB // 2)
    copies.append(pltpu.make_async_copy(lone[2].at[pl.ds(HEAD, BB // 2)], env_all.at[11, half_rows], env_sem.at[11]))
    copies.append(pltpu.make_async_copy(across2b, env_all.at[11, pl.ds(BB // 2, BB // 2)], env_sem.at[12]))
    copies += [pltpu.make_async_copy(ket_in.at[s], ket.at[pl.ds(2 * s, 2)], ket_sem.at[s]) for s in range(4)]
    copies.append(pltpu.make_async_copy(bra_own, bra_all.at[pl.ds(6, 6)], bra_sem.at[0]))
    x = place[0] % NX
    y = NX - 1 - x
    quarters = ((rim, 0, x), (swapped, 0, x + 1 - 2 * (x % 2)), (crossed, 0, y), (crossed, 12, y + 1 - 2 * (y % 2)))
    for n, (ref, at, owner) in enumerate(quarters):
        lines = pl.ds(pl.multiple_of(QUARTER * owner, QUARTER), QUARTER)
        for m, (first, count, to) in enumerate(((0, 3, 0), (3, 6, 12), (9, 3, 21))):
            copies.append(pltpu.make_async_copy(
                ref.at[pl.ds(at + first, count)], bra_all.at[pl.ds(to, count), lines], bra_sem.at[1 + 3 * n + m]
            ))
    for copy in copies:
        copy.start()

    r, a = place[0], place[1]
    my_z, my_x = r // NX, r % NX
    for d, slot in enumerate(slots):
        for i in range(4):

            @pl.when(i < live_count(row_x(r, STEPS[slot])))
            def _(at=8 * d + 2 * i):
                total[at] = jnp.zeros((BB, KB), F32)
                total[at + 1] = jnp.zeros((BB, KB), F32)

    size[0] = 0

    @pl.loop(0, 12 * EPW)
    def _(item):
        base = LANES * (item // EPW) + 8 * (item % EPW)
        out_w, s, code = ints[base], ints[base + 2], ints[base + 7]
        q_b = code - 1
        p_b, s_a = q_b + s // 2, s % 2

        @pl.when((code > 0) & (out_w // (CH * NX) == my_z) & (p_b < 2) & (a + s_a < SECS))
        def _():
            out_r, out_j = out_w // CH, out_w % CH

            forward = (out_r % NX - my_x + NX) % NX
            slot = jnp.where(forward == 1, 2, jnp.where(forward == 3, 1, jnp.where(forward == 2, 3, 0)))
            inside = (slot >= slots[0]) & (slot <= slots[-1])

            @pl.when(inside & (live_at(out_r, p_b, out_j) == 1))
            def _():
                sp, at = ints[base + 1], size[0]
                out_a, out_b = charge(out_w)
                low = live_at(out_r, 0, 0)
                inside = low + live_at(out_r, 0, 1) + out_j * live_at(out_r, 1, 0)
                position = jnp.where(p_b == 0, out_j * low, inside)
                todo[4 * at] = item // EPW
                todo[4 * at + 1] = 2 * s + q_b
                todo[4 * at + 2] = 6 * (s_a + out_a + 1) + 3 * (sp % 2) + p_b + out_b + sp // 2
                todo[4 * at + 3] = 8 * (slot - slots[0]) + 2 * position + s_a
                scale[at] = values[base + 3] + values[base + 4] + values[base + 5]
                size[0] = at + 1

    count = size[0]
    for n in range(TOGETHER - 1):
        for field in range(3):
            todo[4 * (count + n) + field] = 0
        todo[4 * (count + n) + 3] = 2 * width
        scale[count + n] = 0.0

    for copy in copies:
        copy.wait()

    @pl.loop(0, (count + TOGETHER - 1) // TOGETHER)
    def _(step):
        places = [step * TOGETHER + n for n in range(TOGETHER)]
        halves = [
            jnp.dot(env_all[todo[4 * n]], ket[todo[4 * n + 1]], preferred_element_type=F32).astype(BF) for n in places
        ]
        terms = [
            jnp.dot(bra_all[todo[4 * n + 2]], half, preferred_element_type=F32) for n, half in zip(places, halves)
        ]
        for n, term in zip(places, terms):
            at = todo[4 * n + 3]
            total[at] = total[at] + scale[n] * term

    def stored(d, i):
        return pltpu.make_async_copy(rounded.at[4 * d + i], outs[4 * d + i], out_sem.at[4 * d + i])

    for d in range(len(slots)):
        for i in range(4):

            @pl.when(i < live_count(row_x(r, STEPS[slots[d]])))
            def _(d=d, i=i):
                for up in range(2):
                    rounded[4 * d + i, up] = total[8 * d + 2 * i + up].astype(BF)
                stored(d, i).start()

    for d in range(len(slots)):
        for i in range(4):

            @pl.when(i < live_count(row_x(r, STEPS[slots[d]])))
            def _(d=d, i=i):
                stored(d, i).wait()


def body(env_in, ket_mps, bra_mps, ket_sizes, bra_sizes, entries, coeffs):
    my_a = lax.axis_index("sec")
    r = lax.axis_index("row")
    place = jnp.stack([r, my_a])
    ket_flat, bra_flat = ket_sizes.T, bra_sizes.T

    smem = pl.BlockSpec(memory_space=pltpu.SMEM)
    vmem = pl.BlockSpec(memory_space=pltpu.VMEM)
    shape = jax.ShapeDtypeStruct
    pair = shape((2, BB, KB), BF)
    params = pltpu.CompilerParams(vmem_limit_bytes=VMEM_BYTES)
    payload = shape((HEAD + BB, KB), BF)
    own01, own2, moving = pl.pallas_call(
        prepare_kernel,
        in_specs=[smem] * 5 + [vmem],
        out_specs=[vmem] * 3,
        out_shape=[shape((2, HEAD + BB, KB), BF), payload, payload],
        compiler_params=params,
    )(place, ket_flat, bra_flat, entries.transpose(2, 0, 1), coeffs, env_in.reshape(4, BB, KB))

    same = lambda n: n
    z_up, z_down = (lambda n: row_z(n, 1)), (lambda n: row_z(n, -1))
    x_up, x_down, x_far = (lambda n: row_x(n, 1)), (lambda n: row_x(n, -1)), (lambda n: row_x(n, 2))

    def sent(value, move, owner, rows):
        return lax.ppermute(value, "row", [(n, move(n)) for n in range(ROWS) if owner(n) in rows])

    everyone = set(range(ROWS))
    full = [n for n in range(ROWS) if COUNT[n] == 4]
    takers, lent = set(), []
    for n in full:
        taker = next(m for m in (row_x(n, 1), row_x(n, -1)) if COUNT[m] == 2 and m not in takers)
        takers.add(taker)
        lent.append((n, taker))
    three = {n for n in range(ROWS) if COUNT[n] > 2} | takers
    behind01 = sent(own01, z_up, same, everyone)
    ahead01 = sent(own01, z_down, same, everyone)

    bra_own, strip, strip_low, strip_high = pl.pallas_call(
        bra_kernel,
        in_specs=[smem, vmem],
        out_specs=[vmem] * 4,
        out_shape=[
            shape((6, BB, BB), BF),
            shape((6, QUARTER, BB), BF),
            shape((3, QUARTER, BB), BF),
            shape((3, QUARTER, BB), BF),
        ],
        compiler_params=params,
    )(place, after(bra_mps, own01)[:, 0])
    up = lambda n: [(i, i + n) for i in range(SECS - n)]
    down = lambda n: [(i + n, i) for i in range(SECS - n)]
    rim_low = lax.ppermute(strip_low, "sec", up(1))
    borrowed = lax.ppermute(after(moving, rim_low), "row", lent)
    own2 = own2 + borrowed
    behind2 = sent(own2, z_up, same, three)
    ahead2 = sent(own2, z_down, same, three)
    across0 = sent(behind01[0], z_up, z_down, everyone)
    across1 = sent(ahead01[1], z_down, z_up, everyone)
    across2a = sent(behind2[: HEAD + BB // 2], z_up, z_down, three)
    across2b = sent(ahead2[HEAD + BB // 2 :], z_down, z_up, three)
    rim = jnp.concatenate([
        rim_low,
        lax.ppermute(strip, "sec", down(1)),
        lax.ppermute(strip_high, "sec", down(2)),
    ])
    swapped = lax.ppermute(rim, "row", [(n, n ^ 1) for n in range(ROWS)])
    crossed = lax.ppermute(jnp.concatenate([rim, swapped]), "row", [(n, n ^ 3) for n in range(ROWS)])

    heads = [own01[0], own01[1], own2, behind01[0], behind01[1], behind2, ahead01[0], ahead01[1], ahead2,
             across0, across1, across2a]
    values = jnp.concatenate([lax.optimization_barrier(head[0, :LANES].astype(F32)) for head in heads])

    hbm = pl.BlockSpec(memory_space=pl.ANY)
    def terms(slots, own):
        width = 4 * len(slots)
        return pl.pallas_call(
            functools.partial(terms_kernel, slots),
            in_specs=[smem] * 3 + [hbm] * 15,
            out_specs=[hbm] * width,
            out_shape=[pair] * width,
            scratch_shapes=[
                pltpu.VMEM((12, BB, KB), BF),
                pltpu.VMEM((8, KB, KB), BF),
                pltpu.VMEM((24, BB, BB), BF),
                pltpu.VMEM((2 * width + 1, BB, KB), F32),
                pltpu.VMEM((width, 2, BB, KB), BF),
                pltpu.SMEM((4 * (12 * EPW + TOGETHER),), jnp.int32),
                pltpu.SMEM((12 * EPW + TOGETHER,), F32),
                pltpu.SMEM((1,), jnp.int32),
                pltpu.SemaphoreType.DMA((13,)),
                pltpu.SemaphoreType.DMA((4,)),
                pltpu.SemaphoreType.DMA((13,)),
                pltpu.SemaphoreType.DMA((width,)),
            ],
            compiler_params=params,
        )(place, values.astype(jnp.int32), values, own, own2, behind01, behind2, ahead01, ahead2,
          across0, across1, across2a, across2b, ket_mps[:, 0], bra_own, rim, swapped, crossed)

    far = terms((3,), own01)
    sums = terms((0, 1, 2), after(own01, *far))
    mine, left, right = sums[:4], sums[4:8], sums[8:]

    def added(*parts):
        return functools.reduce(jnp.add, [part.astype(F32) for part in parts])

    def moved(value, move, owner, i):
        return sent(value, move, owner, {n for n in range(ROWS) if COUNT[n] > i})

    far_up = {i: moved(far[i], x_up, x_far, i) for i in (0, 2)}
    far_down = {i: moved(far[i], x_down, x_far, i) for i in (1, 3)}
    from_left = {i: moved(right[i], x_up, x_up, i) for i in (1, 3)}
    from_right = {i: moved(left[i], x_down, x_down, i) for i in (0, 2)}
    for i in (0, 2):
        from_left[i] = moved(added(right[i], far_up[i]).astype(BF), x_up, x_up, i)
    for i in (1, 3):
        from_right[i] = moved(added(left[i], far_down[i]).astype(BF), x_down, x_down, i)

    here = [added(mine[i][0], from_left[i][0], from_right[i][0]) for i in range(4)]
    raised = [added(mine[i][1], from_left[i][1], from_right[i][1]).astype(BF) for i in range(4)]
    above = []
    for i in (0, 2):
        pairs = [(a * ROWS + n, (a + 1) * ROWS + n) for a in range(SECS - 1) for n in range(ROWS) if COUNT[n] > i]
        above.append(lax.ppermute(jnp.stack(raised[i : i + 2]), ("sec", "row"), pairs))

    whole = shape((4, BB, KB), BF)
    out = pl.pallas_call(
        unpack_kernel,
        in_specs=[smem] * 3 + [vmem] * 3,
        out_specs=vmem,
        out_shape=whole,
        compiler_params=params,
    )(place, ket_flat, bra_flat, here[0], here[1], above[0])
    out = pl.pallas_call(
        finish_kernel,
        in_specs=[smem] * 3 + [vmem] * 3 + [hbm],
        out_specs=hbm,
        out_shape=whole,
        scratch_shapes=[pltpu.VMEM((2, BB, KB), BF), pltpu.SemaphoreType.DMA((2,))],
        input_output_aliases={6: 0},
        compiler_params=params,
    )(place, ket_flat, bra_flat, here[2], here[3], above[1], out)
    return out.reshape(CH, 1, 2, BB, KB)


def solution(mesh):
    placed = (
        P("row", "sec", None, None, None),
        P(None, "sec", None, None, None),
        P(None, "sec", None, None, None),
        P(),
        P(),
        P("row", None, None),
        P("row", None),
    )
    return jax.shard_map(
        body,
        mesh=mesh,
        in_specs=placed,
        out_specs=P("row", "sec", None, None, None),
        check_vma=False,
    )
```

```python
import functools

import jax
import jax.numpy as jnp
from jax import lax
from jax.experimental import pallas as pl
from jax.experimental.pallas import tpu as pltpu
from jax.sharding import PartitionSpec as P

EPW, CH = 8, 2
NZ, NX = 4, 4
SECS, ROWS = 16, 16
BB, KB = 256, 512
QUARTER = BB // NX
TOGETHER = 4
BF, F32 = jnp.bfloat16, jnp.float32
STEPS = (0, -1, 1, 2)
VMEM_BYTES = 56 * 1024 * 1024
HEAD = 16
LANES = 128
BRA_CELLS = ((0, 0), (0, 1), (2, 1), (1, 0), (1, 1), (3, 1))
CELLS = [(b, j) for b in range(2) for j in range(CH)]


def after(value, *others):
    return lax.optimization_barrier((value, *others))[0] if others else value


def charge(channel):
    klass = channel % 9
    return klass % 3 - 1, klass // 3 - 1


def live_at(r, b, j):
    to_b = b + charge(CH * r + j)[1]
    return jnp.where((to_b >= 0) & (to_b < 2), 1, 0)


COUNT = [sum(0 <= b + charge(CH * r + j)[1] < 2 for b, j in CELLS) for r in range(ROWS)]


def row_z(r, d):
    return (r // NX + d) % NZ * NX + r % NX


def row_x(r, d):
    return r // NX * NX + (r % NX + d) % NX


def packed_cells(r, a, ket_sizes, bra_sizes):
    places = [(jnp.int32(0), jnp.int32(0), jnp.int32(0)) for _ in range(4)]
    count = jnp.int32(0)
    for b, j in CELLS:
        out_a, out_b = charge(CH * r + j)
        live = live_at(r, b, j)
        at_a, at_b = a + out_a, jnp.clip(b + out_b, 0, 1)
        rows = jnp.where((at_a >= 0) & (at_a < SECS), bra_sizes[at_b, jnp.clip(at_a, 0, SECS - 1)], 0)
        cols = ket_sizes[b, a]
        for i in range(4):
            hit = (live == 1) & (count == i)
            places[i] = tuple(jnp.where(hit, new, old) for new, old in zip((2 * j + b, rows, cols), places[i]))
        count = count + live
    return places, count


def live_count(r):
    return sum(live_at(r, b, j) for b, j in CELLS)


def keep(rows, cols):
    row_at = lax.broadcasted_iota(jnp.int32, (BB, KB), 0)
    col_at = lax.broadcasted_iota(jnp.int32, (BB, KB), 1)
    return (row_at < rows) & (col_at < cols)


def prepare_kernel(place, ket_sizes, bra_sizes, entries, coeffs, env, pair_out, third_out, moving):
    r, a = place[0], place[1]
    lane = lax.broadcasted_iota(jnp.int32, (HEAD, KB), 1)
    slot, field = lane // 8, lane % 8
    places, count = packed_cells(r, a, ket_sizes, bra_sizes)
    for i, (cell, rows, cols) in enumerate(places):
        target = (pair_out.at[0], pair_out.at[1], third_out, moving)[i]
        j, b = cell // 2, cell % 2
        head = jnp.zeros((HEAD, KB), F32)
        for n in range(EPW):
            part = jnp.where(field < 3, 0.0, coeffs[j, n])
            for f in range(3):
                part = jnp.where(field == f, entries[f, j, n].astype(F32), part)
            part = jnp.where(field == 7, (b + 1).astype(F32), part)
            head = jnp.where(slot == n, part, head)
        first = head.astype(BF).astype(F32)
        second = (head - first).astype(BF).astype(F32)
        last = head - first - second
        head = jnp.where(field == 4, second, jnp.where(field == 5, last, first))
        head = jnp.where(i < count, head, 0.0)
        target[:HEAD] = head.astype(BF)
        target[HEAD:] = jnp.where(keep(rows, cols), env[cell], jnp.zeros((BB, KB), BF))


def bra_kernel(place, bra, flipped, strip, strip_low, strip_high):
    r = place[0]
    lines = pl.ds(pl.multiple_of(r % NX * QUARTER, QUARTER), QUARTER)
    for n, (sp, to_b) in enumerate(BRA_CELLS):
        flipped[n] = bra[sp, to_b].T
        value = flipped[n, lines]
        strip[n] = value
        if n < 3:
            strip_low[n] = value
        else:
            strip_high[n - 3] = value


def unpack_kernel(place, ket_sizes, bra_sizes, here0, here1, above, out):
    out[...] = jnp.zeros_like(out)
    places = packed_cells(place[0], place[1], ket_sizes, bra_sizes)[0]
    for i, here in enumerate((here0, here1)):
        cell, rows, cols = places[i]

        @pl.when(rows > 0)
        def _(i=i, here=here, cell=cell, rows=rows, cols=cols):
            value = here[...] + above[i].astype(F32)
            out[cell] = jnp.where(keep(rows, cols), value, 0.0).astype(BF)


def finish_kernel(place, ket_sizes, bra_sizes, here2, here3, above, _, out, done, sem):
    places = packed_cells(place[0], place[1], ket_sizes, bra_sizes)[0]
    for i, here in enumerate((here2, here3)):
        cell, rows, cols = places[2 + i]

        @pl.when(rows > 0)
        def _(i=i, here=here, cell=cell, rows=rows, cols=cols):
            value = here[...] + above[i].astype(F32)
            done[i] = jnp.where(keep(rows, cols), value, 0.0).astype(BF)
            pltpu.make_async_copy(done.at[i], out.at[cell], sem.at[i]).start()

    for i in range(2):
        cell, rows, _ = places[2 + i]

        @pl.when(rows > 0)
        def _(i=i, cell=cell):
            pltpu.make_async_copy(done.at[i], out.at[cell], sem.at[i]).wait()


def terms_kernel(slots, place, ints, values, *refs):
    width = 4 * len(slots)
    two, three, lone = (refs[0], refs[2], refs[4]), (refs[1], refs[3], refs[5]), refs[6:9]
    across2b, ket_in, bra_own, rim, swapped, crossed = refs[9:15]
    outs = refs[15 : 15 + width]
    env_all, ket, bra_all, total, rounded, todo, scale, size, env_sem, ket_sem, bra_sem, out_sem = refs[15 + width :]
    copies = []
    body_rows = pl.ds(HEAD, BB)
    views = []
    for first, third in zip(two, three):
        views += [first.at[0, body_rows], first.at[1, body_rows], third.at[body_rows]]
    views += [lone[0].at[body_rows], lone[1].at[body_rows]]
    copies += [pltpu.make_async_copy(view, env_all.at[n], env_sem.at[n]) for n, view in enumerate(views)]
    half_rows = pl.ds(0, BB // 2)
    copies.append(pltpu.make_async_copy(lone[2].at[pl.ds(HEAD, BB // 2)], env_all.at[11, half_rows], env_sem.at[11]))
    copies.append(pltpu.make_async_copy(across2b, env_all.at[11, pl.ds(BB // 2, BB // 2)], env_sem.at[12]))
    copies += [pltpu.make_async_copy(ket_in.at[s], ket.at[pl.ds(2 * s, 2)], ket_sem.at[s]) for s in range(4)]
    copies.append(pltpu.make_async_copy(bra_own, bra_all.at[pl.ds(6, 6)], bra_sem.at[0]))
    x = place[0] % NX
    y = NX - 1 - x
    quarters = ((rim, 0, x), (swapped, 0, x + 1 - 2 * (x % 2)), (crossed, 0, y), (crossed, 12, y + 1 - 2 * (y % 2)))
    for n, (ref, at, owner) in enumerate(quarters):
        lines = pl.ds(pl.multiple_of(QUARTER * owner, QUARTER), QUARTER)
        for m, (first, count, to) in enumerate(((0, 3, 0), (3, 6, 12), (9, 3, 21))):
            copies.append(pltpu.make_async_copy(
                ref.at[pl.ds(at + first, count)], bra_all.at[pl.ds(to, count), lines], bra_sem.at[1 + 3 * n + m]
            ))
    for copy in copies:
        copy.start()

    r, a = place[0], place[1]
    my_z, my_x = r // NX, r % NX
    for d, slot in enumerate(slots):
        for i in range(4):

            @pl.when(i < live_count(row_x(r, STEPS[slot])))
            def _(at=8 * d + 2 * i):
                total[at] = jnp.zeros((BB, KB), F32)
                total[at + 1] = jnp.zeros((BB, KB), F32)

    size[0] = 0

    @pl.loop(0, 12 * EPW)
    def _(item):
        base = LANES * (item // EPW) + 8 * (item % EPW)
        out_w, s, code = ints[base], ints[base + 2], ints[base + 7]
        q_b = code - 1
        p_b, s_a = q_b + s // 2, s % 2

        @pl.when((code > 0) & (out_w // (CH * NX) == my_z) & (p_b < 2) & (a + s_a < SECS))
        def _():
            out_r, out_j = out_w // CH, out_w % CH

            forward = (out_r % NX - my_x + NX) % NX
            slot = jnp.where(forward == 1, 2, jnp.where(forward == 3, 1, jnp.where(forward == 2, 3, 0)))
            inside = (slot >= slots[0]) & (slot <= slots[-1])

            @pl.when(inside & (live_at(out_r, p_b, out_j) == 1))
            def _():
                sp, at = ints[base + 1], size[0]
                out_a, out_b = charge(out_w)
                low = live_at(out_r, 0, 0)
                inside = low + live_at(out_r, 0, 1) + out_j * live_at(out_r, 1, 0)
                position = jnp.where(p_b == 0, out_j * low, inside)
                todo[4 * at] = item // EPW
                todo[4 * at + 1] = 2 * s + q_b
                todo[4 * at + 2] = 6 * (s_a + out_a + 1) + 3 * (sp % 2) + p_b + out_b + sp // 2
                todo[4 * at + 3] = 8 * (slot - slots[0]) + 2 * position + s_a
                scale[at] = values[base + 3] + values[base + 4] + values[base + 5]
                size[0] = at + 1

    count = size[0]
    for n in range(TOGETHER - 1):
        for field in range(3):
            todo[4 * (count + n) + field] = 0
        todo[4 * (count + n) + 3] = 2 * width
        scale[count + n] = 0.0

    for copy in copies:
        copy.wait()

    @pl.loop(0, (count + TOGETHER - 1) // TOGETHER)
    def _(step):
        places = [step * TOGETHER + n for n in range(TOGETHER)]
        halves = [
            jnp.dot(env_all[todo[4 * n]], ket[todo[4 * n + 1]], preferred_element_type=F32).astype(BF) for n in places
        ]
        terms = [
            jnp.dot(bra_all[todo[4 * n + 2]], half, preferred_element_type=F32) for n, half in zip(places, halves)
        ]
        for n, term in zip(places, terms):
            at = todo[4 * n + 3]
            total[at] = total[at] + scale[n] * term

    def stored(d, i):
        return pltpu.make_async_copy(rounded.at[4 * d + i], outs[4 * d + i], out_sem.at[4 * d + i])

    for d in range(len(slots)):
        for i in range(4):

            @pl.when(i < live_count(row_x(r, STEPS[slots[d]])))
            def _(d=d, i=i):
                for up in range(2):
                    rounded[4 * d + i, up] = total[8 * d + 2 * i + up].astype(BF)
                stored(d, i).start()

    for d in range(len(slots)):
        for i in range(4):

            @pl.when(i < live_count(row_x(r, STEPS[slots[d]])))
            def _(d=d, i=i):
                stored(d, i).wait()


def body(env_in, ket_mps, bra_mps, ket_sizes, bra_sizes, entries, coeffs):
    my_a = lax.axis_index("sec")
    r = lax.axis_index("row")
    place = jnp.stack([r, my_a])
    ket_flat, bra_flat = ket_sizes.T, bra_sizes.T

    smem = pl.BlockSpec(memory_space=pltpu.SMEM)
    vmem = pl.BlockSpec(memory_space=pltpu.VMEM)
    shape = jax.ShapeDtypeStruct
    pair = shape((2, BB, KB), BF)
    params = pltpu.CompilerParams(vmem_limit_bytes=VMEM_BYTES)
    payload = shape((HEAD + BB, KB), BF)
    own01, own2, moving = pl.pallas_call(
        prepare_kernel,
        in_specs=[smem] * 5 + [vmem],
        out_specs=[vmem] * 3,
        out_shape=[shape((2, HEAD + BB, KB), BF), payload, payload],
        compiler_params=params,
    )(place, ket_flat, bra_flat, entries.transpose(2, 0, 1), coeffs, env_in.reshape(4, BB, KB))

    same = lambda n: n
    z_up, z_down = (lambda n: row_z(n, 1)), (lambda n: row_z(n, -1))
    x_up, x_down, x_far = (lambda n: row_x(n, 1)), (lambda n: row_x(n, -1)), (lambda n: row_x(n, 2))

    def sent(value, move, owner, rows):
        return lax.ppermute(value, "row", [(n, move(n)) for n in range(ROWS) if owner(n) in rows])

    everyone = set(range(ROWS))
    full = [n for n in range(ROWS) if COUNT[n] == 4]
    takers, lent = set(), []
    for n in full:
        taker = next(m for m in (row_x(n, 1), row_x(n, -1)) if COUNT[m] == 2 and m not in takers)
        takers.add(taker)
        lent.append((n, taker))
    three = {n for n in range(ROWS) if COUNT[n] > 2} | takers
    behind01 = sent(own01, z_up, same, everyone)
    ahead01 = sent(own01, z_down, same, everyone)

    bra_own, strip, strip_low, strip_high = pl.pallas_call(
        bra_kernel,
        in_specs=[smem, vmem],
        out_specs=[vmem] * 4,
        out_shape=[
            shape((6, BB, BB), BF),
            shape((6, QUARTER, BB), BF),
            shape((3, QUARTER, BB), BF),
            shape((3, QUARTER, BB), BF),
        ],
        compiler_params=params,
    )(place, after(bra_mps, own01)[:, 0])
    up = lambda n: [(i, i + n) for i in range(SECS - n)]
    down = lambda n: [(i + n, i) for i in range(SECS - n)]
    rim_low = lax.ppermute(strip_low, "sec", up(1))
    borrowed = lax.ppermute(after(moving, rim_low), "row", lent)
    own2 = own2 + borrowed
    behind2 = sent(own2, z_up, same, three)
    ahead2 = sent(own2, z_down, same, three)
    across0 = sent(behind01[0], z_up, z_down, everyone)
    across1 = sent(ahead01[1], z_down, z_up, everyone)
    across2a = sent(behind2[: HEAD + BB // 2], z_up, z_down, three)
    across2b = sent(ahead2[HEAD + BB // 2 :], z_down, z_up, three)
    rim = jnp.concatenate([
        rim_low,
        lax.ppermute(strip, "sec", down(1)),
        lax.ppermute(strip_high, "sec", down(2)),
    ])
    swapped = lax.ppermute(rim, "row", [(n, n ^ 1) for n in range(ROWS)])
    crossed = lax.ppermute(jnp.concatenate([rim, swapped]), "row", [(n, n ^ 3) for n in range(ROWS)])

    heads = [own01[0], own01[1], own2, behind01[0], behind01[1], behind2, ahead01[0], ahead01[1], ahead2,
             across0, across1, across2a]
    values = jnp.concatenate([lax.optimization_barrier(head[0, :LANES].astype(F32)) for head in heads])

    hbm = pl.BlockSpec(memory_space=pl.ANY)
    def terms(slots, own):
        width = 4 * len(slots)
        return pl.pallas_call(
            functools.partial(terms_kernel, slots),
            in_specs=[smem] * 3 + [hbm] * 15,
            out_specs=[hbm] * width,
            out_shape=[pair] * width,
            scratch_shapes=[
                pltpu.VMEM((12, BB, KB), BF),
                pltpu.VMEM((8, KB, KB), BF),
                pltpu.VMEM((24, BB, BB), BF),
                pltpu.VMEM((2 * width + 1, BB, KB), F32),
                pltpu.VMEM((width, 2, BB, KB), BF),
                pltpu.SMEM((4 * (12 * EPW + TOGETHER),), jnp.int32),
                pltpu.SMEM((12 * EPW + TOGETHER,), F32),
                pltpu.SMEM((1,), jnp.int32),
                pltpu.SemaphoreType.DMA((13,)),
                pltpu.SemaphoreType.DMA((4,)),
                pltpu.SemaphoreType.DMA((13,)),
                pltpu.SemaphoreType.DMA((width,)),
            ],
            compiler_params=params,
        )(place, values.astype(jnp.int32), values, own, own2, behind01, behind2, ahead01, ahead2,
          across0, across1, across2a, across2b, ket_mps[:, 0], bra_own, rim, swapped, crossed)

    far = terms((3,), own01)
    sides = terms((1, 2), after(own01, *far))
    left, right = sides[:4], sides[4:]

    def added(*parts):
        return functools.reduce(jnp.add, [part.astype(F32) for part in parts])

    def moved(value, move, owner, i):
        return sent(value, move, owner, {n for n in range(ROWS) if COUNT[n] > i})

    far_up = {i: moved(far[i], x_up, x_far, i) for i in (0, 2)}
    far_down = {i: moved(far[i], x_down, x_far, i) for i in (1, 3)}
    mine = terms((0,), after(own01, *sides, far_up[0], far_down[1]))
    from_left = {i: moved(right[i], x_up, x_up, i) for i in (1, 3)}
    from_right = {i: moved(left[i], x_down, x_down, i) for i in (0, 2)}
    for i in (0, 2):
        from_left[i] = moved(added(after(right[i], *mine), far_up[i]).astype(BF), x_up, x_up, i)
    for i in (1, 3):
        from_right[i] = moved(added(after(left[i], *mine), far_down[i]).astype(BF), x_down, x_down, i)

    here = [added(mine[i][0], from_left[i][0], from_right[i][0]) for i in range(4)]
    raised = [added(mine[i][1], from_left[i][1], from_right[i][1]).astype(BF) for i in range(4)]
    above = []
    for i in (0, 2):
        pairs = [(a * ROWS + n, (a + 1) * ROWS + n) for a in range(SECS - 1) for n in range(ROWS) if COUNT[n] > i]
        above.append(lax.ppermute(jnp.stack(raised[i : i + 2]), ("sec", "row"), pairs))

    whole = shape((4, BB, KB), BF)
    out = pl.pallas_call(
        unpack_kernel,
        in_specs=[smem] * 3 + [vmem] * 3,
        out_specs=vmem,
        out_shape=whole,
        compiler_params=params,
    )(place, ket_flat, bra_flat, here[0], here[1], above[0])
    out = pl.pallas_call(
        finish_kernel,
        in_specs=[smem] * 3 + [vmem] * 3 + [hbm],
        out_specs=hbm,
        out_shape=whole,
        scratch_shapes=[pltpu.VMEM((2, BB, KB), BF), pltpu.SemaphoreType.DMA((2,))],
        input_output_aliases={6: 0},
        compiler_params=params,
    )(place, ket_flat, bra_flat, here[2], here[3], above[1], out)
    return out.reshape(CH, 1, 2, BB, KB)


def solution(mesh):
    placed = (
        P("row", "sec", None, None, None),
        P(None, "sec", None, None, None),
        P(None, "sec", None, None, None),
        P(),
        P(),
        P("row", None, None),
        P("row", None),
    )
    return jax.shard_map(
        body,
        mesh=mesh,
        in_specs=placed,
        out_specs=P("row", "sec", None, None, None),
        check_vma=False,
    )
```

```python
import functools

import jax
import jax.numpy as jnp
from jax import lax
from jax.experimental import pallas as pl
from jax.experimental.pallas import tpu as pltpu
from jax.sharding import PartitionSpec as P

EPW, CH = 8, 2
NZ, NX = 4, 4
SECS, ROWS = 16, 16
BB, KB = 256, 512
QUARTER = BB // NX
TOGETHER = 4
BF, F32 = jnp.bfloat16, jnp.float32
STEPS = (0, -1, 1, 2)
VMEM_BYTES = 56 * 1024 * 1024
HEAD = 16
LANES = 128
BRA_CELLS = ((0, 0), (0, 1), (2, 1), (1, 0), (1, 1), (3, 1))
CELLS = [(b, j) for b in range(2) for j in range(CH)]


def after(value, *others):
    return lax.optimization_barrier((value, *others))[0] if others else value


def charge(channel):
    klass = channel % 9
    return klass % 3 - 1, klass // 3 - 1


def live_at(r, b, j):
    to_b = b + charge(CH * r + j)[1]
    return jnp.where((to_b >= 0) & (to_b < 2), 1, 0)


COUNT = [sum(0 <= b + charge(CH * r + j)[1] < 2 for b, j in CELLS) for r in range(ROWS)]


def row_z(r, d):
    return (r // NX + d) % NZ * NX + r % NX


def row_x(r, d):
    return r // NX * NX + (r % NX + d) % NX


def packed_cells(r, a, ket_sizes, bra_sizes):
    places = [(jnp.int32(0), jnp.int32(0), jnp.int32(0)) for _ in range(4)]
    count = jnp.int32(0)
    for b, j in CELLS:
        out_a, out_b = charge(CH * r + j)
        live = live_at(r, b, j)
        at_a, at_b = a + out_a, jnp.clip(b + out_b, 0, 1)
        rows = jnp.where((at_a >= 0) & (at_a < SECS), bra_sizes[at_b, jnp.clip(at_a, 0, SECS - 1)], 0)
        cols = ket_sizes[b, a]
        for i in range(4):
            hit = (live == 1) & (count == i)
            places[i] = tuple(jnp.where(hit, new, old) for new, old in zip((2 * j + b, rows, cols), places[i]))
        count = count + live
    return places, count


def live_count(r):
    return sum(live_at(r, b, j) for b, j in CELLS)


def keep(rows, cols):
    row_at = lax.broadcasted_iota(jnp.int32, (BB, KB), 0)
    col_at = lax.broadcasted_iota(jnp.int32, (BB, KB), 1)
    return (row_at < rows) & (col_at < cols)


def prepare_kernel(place, ket_sizes, bra_sizes, entries, coeffs, env, pair_out, third_out, moving):
    r, a = place[0], place[1]
    lane = lax.broadcasted_iota(jnp.int32, (HEAD, KB), 1)
    slot, field = lane // 8, lane % 8
    places, count = packed_cells(r, a, ket_sizes, bra_sizes)
    for i, (cell, rows, cols) in enumerate(places):
        target = (pair_out.at[0], pair_out.at[1], third_out, moving)[i]
        j, b = cell // 2, cell % 2
        head = jnp.zeros((HEAD, KB), F32)
        for n in range(EPW):
            part = jnp.where(field < 3, 0.0, coeffs[j, n])
            for f in range(3):
                part = jnp.where(field == f, entries[f, j, n].astype(F32), part)
            part = jnp.where(field == 7, (b + 1).astype(F32), part)
            head = jnp.where(slot == n, part, head)
        first = head.astype(BF).astype(F32)
        second = (head - first).astype(BF).astype(F32)
        last = head - first - second
        head = jnp.where(field == 4, second, jnp.where(field == 5, last, first))
        head = jnp.where(i < count, head, 0.0)
        target[:HEAD] = head.astype(BF)
        target[HEAD:] = jnp.where(keep(rows, cols), env[cell], jnp.zeros((BB, KB), BF))


def bra_kernel(place, bra, flipped, strip, strip_low, strip_high):
    r = place[0]
    lines = pl.ds(pl.multiple_of(r % NX * QUARTER, QUARTER), QUARTER)
    for n, (sp, to_b) in enumerate(BRA_CELLS):
        flipped[n] = bra[sp, to_b].T
        value = flipped[n, lines]
        strip[n] = value
        if n < 3:
            strip_low[n] = value
        else:
            strip_high[n - 3] = value


def unpack_kernel(place, ket_sizes, bra_sizes, here0, here1, above, out):
    out[...] = jnp.zeros_like(out)
    places = packed_cells(place[0], place[1], ket_sizes, bra_sizes)[0]
    for i, here in enumerate((here0, here1)):
        cell, rows, cols = places[i]

        @pl.when(rows > 0)
        def _(i=i, here=here, cell=cell, rows=rows, cols=cols):
            value = here[...] + above[i].astype(F32)
            out[cell] = jnp.where(keep(rows, cols), value, 0.0).astype(BF)


def finish_kernel(place, ket_sizes, bra_sizes, here2, here3, above, _, out, done, sem):
    places = packed_cells(place[0], place[1], ket_sizes, bra_sizes)[0]
    for i, here in enumerate((here2, here3)):
        cell, rows, cols = places[2 + i]

        @pl.when(rows > 0)
        def _(i=i, here=here, cell=cell, rows=rows, cols=cols):
            value = here[...] + above[i].astype(F32)
            done[i] = jnp.where(keep(rows, cols), value, 0.0).astype(BF)
            pltpu.make_async_copy(done.at[i], out.at[cell], sem.at[i]).start()

    for i in range(2):
        cell, rows, _ = places[2 + i]

        @pl.when(rows > 0)
        def _(i=i, cell=cell):
            pltpu.make_async_copy(done.at[i], out.at[cell], sem.at[i]).wait()


def terms_kernel(slots, place, ints, values, *refs):
    width = 4 * len(slots)
    two, three, lone = (refs[0], refs[2], refs[4]), (refs[1], refs[3], refs[5]), refs[6:9]
    across2b, ket_in, bra_own, rim, swapped, crossed = refs[9:15]
    outs = refs[15 : 15 + width]
    env_all, ket, bra_all, total, rounded, todo, scale, size, env_sem, ket_sem, bra_sem, out_sem = refs[15 + width :]
    copies = []
    body_rows = pl.ds(HEAD, BB)
    views = []
    for first, third in zip(two, three):
        views += [first.at[0, body_rows], first.at[1, body_rows], third.at[body_rows]]
    views += [lone[0].at[body_rows], lone[1].at[body_rows]]
    copies += [pltpu.make_async_copy(view, env_all.at[n], env_sem.at[n]) for n, view in enumerate(views)]
    half_rows = pl.ds(0, BB // 2)
    copies.append(pltpu.make_async_copy(lone[2].at[pl.ds(HEAD, BB // 2)], env_all.at[11, half_rows], env_sem.at[11]))
    copies.append(pltpu.make_async_copy(across2b, env_all.at[11, pl.ds(BB // 2, BB // 2)], env_sem.at[12]))
    copies += [pltpu.make_async_copy(ket_in.at[s], ket.at[pl.ds(2 * s, 2)], ket_sem.at[s]) for s in range(4)]
    copies.append(pltpu.make_async_copy(bra_own, bra_all.at[pl.ds(6, 6)], bra_sem.at[0]))
    x = place[0] % NX
    y = NX - 1 - x
    quarters = ((rim, 0, x), (swapped, 0, x + 1 - 2 * (x % 2)), (crossed, 0, y), (crossed, 12, y + 1 - 2 * (y % 2)))
    for n, (ref, at, owner) in enumerate(quarters):
        lines = pl.ds(pl.multiple_of(QUARTER * owner, QUARTER), QUARTER)
        for m, (first, count, to) in enumerate(((0, 3, 0), (3, 6, 12), (9, 3, 21))):
            copies.append(pltpu.make_async_copy(
                ref.at[pl.ds(at + first, count)], bra_all.at[pl.ds(to, count), lines], bra_sem.at[1 + 3 * n + m]
            ))
    for copy in copies:
        copy.start()

    r, a = place[0], place[1]
    my_z, my_x = r // NX, r % NX
    for d, slot in enumerate(slots):
        for i in range(4):

            @pl.when(i < live_count(row_x(r, STEPS[slot])))
            def _(at=8 * d + 2 * i):
                total[at] = jnp.zeros((BB, KB), F32)
                total[at + 1] = jnp.zeros((BB, KB), F32)

    size[0] = 0

    @pl.loop(0, 12 * EPW)
    def _(item):
        base = LANES * (item // EPW) + 8 * (item % EPW)
        out_w, s, code = ints[base], ints[base + 2], ints[base + 7]
        q_b = code - 1
        p_b, s_a = q_b + s // 2, s % 2

        @pl.when((code > 0) & (out_w // (CH * NX) == my_z) & (p_b < 2) & (a + s_a < SECS))
        def _():
            out_r, out_j = out_w // CH, out_w % CH

            forward = (out_r % NX - my_x + NX) % NX
            slot = jnp.where(forward == 1, 2, jnp.where(forward == 3, 1, jnp.where(forward == 2, 3, 0)))
            inside = (slot >= slots[0]) & (slot <= slots[-1])

            @pl.when(inside & (live_at(out_r, p_b, out_j) == 1))
            def _():
                sp, at = ints[base + 1], size[0]
                out_a, out_b = charge(out_w)
                low = live_at(out_r, 0, 0)
                inside = low + live_at(out_r, 0, 1) + out_j * live_at(out_r, 1, 0)
                position = jnp.where(p_b == 0, out_j * low, inside)
                todo[4 * at] = item // EPW
                todo[4 * at + 1] = 2 * s + q_b
                todo[4 * at + 2] = 6 * (s_a + out_a + 1) + 3 * (sp % 2) + p_b + out_b + sp // 2
                todo[4 * at + 3] = 8 * (slot - slots[0]) + 2 * position + s_a
                scale[at] = values[base + 3] + values[base + 4] + values[base + 5]
                size[0] = at + 1

    count = size[0]
    for n in range(TOGETHER - 1):
        for field in range(3):
            todo[4 * (count + n) + field] = 0
        todo[4 * (count + n) + 3] = 2 * width
        scale[count + n] = 0.0

    for copy in copies:
        copy.wait()

    @pl.loop(0, (count + TOGETHER - 1) // TOGETHER)
    def _(step):
        places = [step * TOGETHER + n for n in range(TOGETHER)]
        halves = [
            jnp.dot(env_all[todo[4 * n]], ket[todo[4 * n + 1]], preferred_element_type=F32).astype(BF) for n in places
        ]
        terms = [
            jnp.dot(bra_all[todo[4 * n + 2]], half, preferred_element_type=F32) for n, half in zip(places, halves)
        ]
        for n, term in zip(places, terms):
            at = todo[4 * n + 3]
            total[at] = total[at] + scale[n] * term

    def stored(d, i):
        return pltpu.make_async_copy(rounded.at[4 * d + i], outs[4 * d + i], out_sem.at[4 * d + i])

    for d in range(len(slots)):
        for i in range(4):

            @pl.when(i < live_count(row_x(r, STEPS[slots[d]])))
            def _(d=d, i=i):
                for up in range(2):
                    rounded[4 * d + i, up] = total[8 * d + 2 * i + up].astype(BF)
                stored(d, i).start()

    for d in range(len(slots)):
        for i in range(4):

            @pl.when(i < live_count(row_x(r, STEPS[slots[d]])))
            def _(d=d, i=i):
                stored(d, i).wait()


def body(env_in, ket_mps, bra_mps, ket_sizes, bra_sizes, entries, coeffs):
    my_a = lax.axis_index("sec")
    r = lax.axis_index("row")
    place = jnp.stack([r, my_a])
    ket_flat, bra_flat = ket_sizes.T, bra_sizes.T

    smem = pl.BlockSpec(memory_space=pltpu.SMEM)
    vmem = pl.BlockSpec(memory_space=pltpu.VMEM)
    shape = jax.ShapeDtypeStruct
    pair = shape((2, BB, KB), BF)
    params = pltpu.CompilerParams(vmem_limit_bytes=VMEM_BYTES)
    payload = shape((HEAD + BB, KB), BF)
    own01, own2, moving = pl.pallas_call(
        prepare_kernel,
        in_specs=[smem] * 5 + [vmem],
        out_specs=[vmem] * 3,
        out_shape=[shape((2, HEAD + BB, KB), BF), payload, payload],
        compiler_params=params,
    )(place, ket_flat, bra_flat, entries.transpose(2, 0, 1), coeffs, env_in.reshape(4, BB, KB))

    same = lambda n: n
    z_up, z_down = (lambda n: row_z(n, 1)), (lambda n: row_z(n, -1))
    x_up, x_down, x_far = (lambda n: row_x(n, 1)), (lambda n: row_x(n, -1)), (lambda n: row_x(n, 2))

    def sent(value, move, owner, rows):
        return lax.ppermute(value, "row", [(n, move(n)) for n in range(ROWS) if owner(n) in rows])

    everyone = set(range(ROWS))
    full = [n for n in range(ROWS) if COUNT[n] == 4]
    takers, lent = set(), []
    for n in full:
        taker = next(m for m in (row_x(n, 1), row_x(n, -1)) if COUNT[m] == 2 and m not in takers)
        takers.add(taker)
        lent.append((n, taker))
    three = {n for n in range(ROWS) if COUNT[n] > 2} | takers
    behind01 = sent(own01, z_up, same, everyone)
    ahead01 = sent(own01, z_down, same, everyone)

    bra_own, strip, strip_low, strip_high = pl.pallas_call(
        bra_kernel,
        in_specs=[smem, vmem],
        out_specs=[vmem] * 4,
        out_shape=[
            shape((6, BB, BB), BF),
            shape((6, QUARTER, BB), BF),
            shape((3, QUARTER, BB), BF),
            shape((3, QUARTER, BB), BF),
        ],
        compiler_params=params,
    )(place, after(bra_mps, own01)[:, 0])
    up = lambda n: [(i, i + n) for i in range(SECS - n)]
    down = lambda n: [(i + n, i) for i in range(SECS - n)]
    rim_low = lax.ppermute(strip_low, "sec", up(1))
    borrowed = lax.ppermute(after(moving, strip), "row", lent)
    own2 = own2 + borrowed
    behind2 = sent(own2, z_up, same, three)
    ahead2 = sent(own2, z_down, same, three)
    across0 = sent(behind01[0], z_up, z_down, everyone)
    across1 = sent(ahead01[1], z_down, z_up, everyone)
    across2a = sent(behind2[: HEAD + BB // 2], z_up, z_down, three)
    across2b = sent(ahead2[HEAD + BB // 2 :], z_down, z_up, three)
    rim = jnp.concatenate([
        rim_low,
        lax.ppermute(after(strip, borrowed), "sec", down(1)),
        lax.ppermute(after(strip_high, borrowed), "sec", down(2)),
    ])
    swapped = lax.ppermute(rim, "row", [(n, n ^ 1) for n in range(ROWS)])
    crossed = lax.ppermute(jnp.concatenate([rim, swapped]), "row", [(n, n ^ 3) for n in range(ROWS)])

    heads = [own01[0], own01[1], own2, behind01[0], behind01[1], behind2, ahead01[0], ahead01[1], ahead2,
             across0, across1, across2a]
    values = jnp.concatenate([lax.optimization_barrier(head[0, :LANES].astype(F32)) for head in heads])

    hbm = pl.BlockSpec(memory_space=pl.ANY)
    def terms(slots, own):
        width = 4 * len(slots)
        return pl.pallas_call(
            functools.partial(terms_kernel, slots),
            in_specs=[smem] * 3 + [hbm] * 15,
            out_specs=[hbm] * width,
            out_shape=[pair] * width,
            scratch_shapes=[
                pltpu.VMEM((12, BB, KB), BF),
                pltpu.VMEM((8, KB, KB), BF),
                pltpu.VMEM((24, BB, BB), BF),
                pltpu.VMEM((2 * width + 1, BB, KB), F32),
                pltpu.VMEM((width, 2, BB, KB), BF),
                pltpu.SMEM((4 * (12 * EPW + TOGETHER),), jnp.int32),
                pltpu.SMEM((12 * EPW + TOGETHER,), F32),
                pltpu.SMEM((1,), jnp.int32),
                pltpu.SemaphoreType.DMA((13,)),
                pltpu.SemaphoreType.DMA((4,)),
                pltpu.SemaphoreType.DMA((13,)),
                pltpu.SemaphoreType.DMA((width,)),
            ],
            compiler_params=params,
        )(place, values.astype(jnp.int32), values, own, own2, behind01, behind2, ahead01, ahead2,
          across0, across1, across2a, across2b, ket_mps[:, 0], bra_own, rim, swapped, crossed)

    far = terms((3,), own01)
    sides = terms((1, 2), after(own01, *far))
    left, right = sides[:4], sides[4:]

    def added(*parts):
        return functools.reduce(jnp.add, [part.astype(F32) for part in parts])

    def moved(value, move, owner, i):
        return sent(value, move, owner, {n for n in range(ROWS) if COUNT[n] > i})

    far_up = {i: moved(far[i], x_up, x_far, i) for i in (0, 2)}
    far_down = {i: moved(far[i], x_down, x_far, i) for i in (1, 3)}
    mine = terms((0,), after(own01, *sides, far_up[0], far_down[1]))
    from_left = {i: moved(right[i], x_up, x_up, i) for i in (1, 3)}
    from_right = {i: moved(left[i], x_down, x_down, i) for i in (0, 2)}
    for i in (0, 2):
        from_left[i] = moved(added(after(right[i], *mine), far_up[i]).astype(BF), x_up, x_up, i)
    for i in (1, 3):
        from_right[i] = moved(added(after(left[i], *mine), far_down[i]).astype(BF), x_down, x_down, i)

    here = [added(mine[i][0], from_left[i][0], from_right[i][0]) for i in range(4)]
    raised = [added(mine[i][1], from_left[i][1], from_right[i][1]).astype(BF) for i in range(4)]
    above = []
    for i in (0, 2):
        pairs = [(a * ROWS + n, (a + 1) * ROWS + n) for a in range(SECS - 1) for n in range(ROWS) if COUNT[n] > i]
        above.append(lax.ppermute(jnp.stack(raised[i : i + 2]), ("sec", "row"), pairs))

    whole = shape((4, BB, KB), BF)
    out = pl.pallas_call(
        unpack_kernel,
        in_specs=[smem] * 3 + [vmem] * 3,
        out_specs=vmem,
        out_shape=whole,
        compiler_params=params,
    )(place, ket_flat, bra_flat, here[0], here[1], above[0])
    out = pl.pallas_call(
        finish_kernel,
        in_specs=[smem] * 3 + [vmem] * 3 + [hbm],
        out_specs=hbm,
        out_shape=whole,
        scratch_shapes=[pltpu.VMEM((2, BB, KB), BF), pltpu.SemaphoreType.DMA((2,))],
        input_output_aliases={6: 0},
        compiler_params=params,
    )(place, ket_flat, bra_flat, here[2], here[3], above[1], out)
    return out.reshape(CH, 1, 2, BB, KB)


def solution(mesh):
    placed = (
        P("row", "sec", None, None, None),
        P(None, "sec", None, None, None),
        P(None, "sec", None, None, None),
        P(),
        P(),
        P("row", None, None),
        P("row", None),
    )
    return jax.shard_map(
        body,
        mesh=mesh,
        in_specs=placed,
        out_specs=P("row", "sec", None, None, None),
        check_vma=False,
    )
```
